32 devices in a mesh: stream: 8 (over z, y), vert: 4 (over x, core).
Axes of the slice: x: 2, y: 2, z: 4, core: 2. Of those that a mesh axis runs over, the one named last changes fastest.
Arguments:
- particles: float32 [256, 4, 7, 128], P('stream', 'vert'), may hold values from -4 to 4, as said below
- phase_flags: int32 [256, 4, 128], P('stream', 'vert'), may hold values 0 or 1
- neighbours: int32 [256, 4, 4], P('stream', 'vert'), may hold values from 0 to 7, as said below
- history: bfloat16 [256, 4, 3, 126, 128], P('stream', 'vert'), may hold values from -160 to 160
- basis_start: float32 [128, 64], replicated, may hold values from -0.5 to 0.5
Outputs:
- new_state: float32 [256, 4, 7, 128], P('stream', 'vert')
- filtered: float32 [256, 4, 3, 128], P('stream', 'vert')
The draws below stay inside these ranges and needn't reach their ends.
Inputs may be any that keep to these rules, and one draw needn't show every extreme that they name: `particles`: rows 0 to 2 of a particle lie in 0 to 2, rows 3 to 5 in -4 to 4, row 6 in 0.97 to 1.03. `neighbours`: the 4 codes of one block are distinct.
All inputs are finite; a program needn't handle non-finite values. No bound on the sum of `phase_flags` on one device may be relied on, other than what follows from the above.
Results may differ from the reference program's by a relative error of at most 0.0003.
Values sent between devices are 32-bit elements; how exact they have to be, the bound alone decides.
No kernel may reach another device: no remote copies, remote signals or barrier semaphores. Data moves between devices by JAX's collectives and lax.ppermute only.
A program may use at most 64 MiB of HBM per device.

```python
import math
import jax
import jax.numpy as jnp
from jax import lax

PART = 128
NBR = 4
SNAP = 128
RANK = 64
POD_ITERS = 4
GS = 256
GV = 4
HIST = 126


def velocity_field(key):
    velocity = jnp.clip(jax.random.normal(key, (GS, GV, 3, PART), jnp.float32), -3.9, 3.9)
    return velocity


def draw_particles(key, part):
    key_place = jax.random.fold_in(key, 0)
    key_density = jax.random.fold_in(key, 2)
    position = jax.random.uniform(key_place, (GS, GV, 3, PART), jnp.float32, 0.0, 2.0)
    velocity = velocity_field(jax.random.fold_in(key, 11))
    relative = jax.random.uniform(key_density, (GS, GV, 1, PART), jnp.float32, 0.97, 1.03)
    return jnp.concatenate([position, velocity, relative], axis=2)


def draw_neighbours(key, part):
    scores = jax.random.randint(key, (GS, GV, 8), 0, 1 << 20) * 8 + jnp.arange(8, dtype=jnp.int32)
    order = jnp.argsort(scores, axis=-1, stable=True)
    return order[:, :, :NBR].astype(jnp.int32)


def draw_history(key, part):
    key_column, key_value, key_share = jax.random.split(jax.random.fold_in(key, 29), 3)
    column_scale = jnp.exp(jax.random.uniform(key_column, (HIST,), jnp.float32, 0.0, math.log(10.0)))
    share = jax.random.uniform(key_share, (HIST,), jnp.float32, 0.4, 1.0)
    rising = 1.0 + 2.0 * jnp.arange(GS, dtype=jnp.float32) / max(GS - 1, 1)
    velocity = velocity_field(jax.random.fold_in(key, 11))
    noise = jnp.clip(jax.random.normal(key_value, (GS, GV, 3, HIST, PART), jnp.float32), -5.0, 5.0)
    values = 0.8 * share[:, None] * velocity[:, :, :, None, :] + 0.3 * noise
    return (values * column_scale[:, None] * rising[:, None, None, None, None]).astype(jnp.bfloat16)


def with_ends(entries, rng, smallest, high):
    place = [jax.random.randint(jax.random.fold_in(rng, axis), (), 0, length) for axis, length in enumerate(entries.shape)]
    widest = entries.shape.index(max(entries.shape))
    neighbour = place[:widest] + [(place[widest] + 1) % entries.shape[widest]] + place[widest + 1:]
    return entries.at[tuple(place)].set(smallest).at[tuple(neighbour)].set(high)


def centred(stream_key, extent, width, bound, kind=jnp.bfloat16):
    values = width * jax.random.normal(stream_key, extent, jnp.float32)
    return jnp.clip(values, min=-bound, max=bound).astype(kind)


def setup_inputs(seed: int = 0) -> dict:
    splits = jax.random.split(jax.random.key(seed), 6)
    particles = draw_particles(jax.random.fold_in(splits[5], 71), 0)
    phase_flags = with_ends((jax.random.randint(splits[1], (GS, GV, PART), 0, 4) < 1).astype(jnp.int32), jax.random.fold_in(splits[1], 1), 0, 1)
    neighbours = draw_neighbours(jax.random.fold_in(splits[5], 71), 0)
    history = draw_history(jax.random.fold_in(splits[5], 71), 0)
    basis_start = centred(splits[4], (SNAP, RANK), SNAP ** -0.5, 0.5, jnp.float32)
    return dict(particles=particles, phase_flags=phase_flags, neighbours=neighbours, history=history, basis_start=basis_start)


ALPHA_KERNEL = 21.0 / (16.0 * math.pi)
VOLUME = 1.0 / 16.0
STIFFNESS = 100.0 / 7.0
TIME_STEP = 0.02
GRAVITY = 1.0
SEDIMENT_EXTRA = 1.65

def forces(own_block, near_blocks, cell_shifts):
    separation = own_block[:, None, 0:3, :, None] - near_blocks[:, :, 0:3, None, :] - cell_shifts[:, :, :, None, None]
    radius = jnp.sqrt(lax.optimization_barrier(jnp.sum(separation * separation, axis=2)))
    kernel_reach = jnp.maximum(1.0 - 0.5 * radius, 0.0)
    kernel_slope = -5.0 * ALPHA_KERNEL * kernel_reach ** 3 * near_blocks[:, :, 6, None, :]
    closing = own_block[:, None, 3:6, :, None] - near_blocks[:, :, 3:6, None, :]
    density_rate = lax.optimization_barrier(jnp.sum(kernel_slope * lax.optimization_barrier(jnp.sum(closing * separation, axis=2)), axis=(1, 3)))
    pressure_term = kernel_slope * (own_block[:, None, 7, :, None] + near_blocks[:, :, 7, None, :])
    acceleration = -lax.optimization_barrier(jnp.sum(pressure_term[:, :, None] * separation, axis=(1, 4)))
    return (acceleration, density_rate)

def block_layout(neighbours):
    blocks_stream, blocks_vert = (neighbours.shape[0], neighbours.shape[1])
    offset_code = neighbours + (neighbours >= 4).astype(jnp.int32)
    zero_codes = jnp.zeros((blocks_stream, blocks_vert, 1), jnp.int32)
    stream_step = jnp.concatenate([zero_codes, offset_code // 3 - 1], axis=-1)
    vert_step = jnp.concatenate([zero_codes, offset_code % 3 - 1], axis=-1)
    stream_place = jnp.arange(blocks_stream, dtype=jnp.int32)[:, None, None]
    vert_place = jnp.arange(blocks_vert, dtype=jnp.int32)[None, :, None]
    near_index = (stream_place + 1 + stream_step) * (blocks_vert + 2) + (vert_place + 1 + vert_step)
    list_width = near_index.shape[2]
    cell_shifts = jnp.stack([2.0 * stream_step.astype(jnp.float32), jnp.zeros(stream_step.shape, jnp.float32), 2.0 * vert_step.astype(jnp.float32)], axis=-1)
    return (near_index.reshape(-1, list_width).astype(jnp.int32), cell_shifts.reshape(-1, list_width, 3))

def make_payload(particles, rest_density, particle_mass):
    relative = particles[:, :, 6]
    pressure = STIFFNESS * (relative ** 7 - 1.0) / (rest_density * relative * relative)
    return jnp.concatenate([particles[:, :, 0:6], particle_mass[:, :, None], pressure[:, :, None]], axis=2)

def interact(payload, extended, near_index, cell_shifts, group_limit):
    block_count = payload.shape[0] * payload.shape[1]
    group_size = math.gcd(block_count, group_limit)
    flat_blocks = extended.reshape(-1, 8, payload.shape[3])
    list_width = near_index.shape[1]

    def one_group(pieces):
        own_block, index_part, shift_part = pieces
        near_blocks = jnp.take(flat_blocks, index_part, axis=0)
        return forces(own_block, near_blocks, shift_part)
    acceleration, density_rate = lax.map(one_group, (payload.reshape(block_count // group_size, group_size, 8, -1), near_index.reshape(-1, group_size, list_width), cell_shifts.reshape(-1, group_size, list_width, 3)))
    return (acceleration.reshape(payload.shape[0], payload.shape[1], 3, -1), density_rate.reshape(payload.shape[0], payload.shape[1], -1))

def update(particles, rest_density, acceleration, density_rate):
    gravity_vector = jnp.array([0.0, 0.0, -GRAVITY], jnp.float32)[:, None]
    velocity = particles[:, :, 3:6] + TIME_STEP * (acceleration + gravity_vector)
    position = particles[:, :, 0:3] + TIME_STEP * velocity
    relative = particles[:, :, 6] + TIME_STEP * density_rate / rest_density
    return jnp.concatenate([position, velocity, relative[:, :, None]], axis=2)

def orthonormal(matrix):
    for repeat in range(2):
        inner_product = jnp.dot(matrix.T, matrix, precision=lax.Precision.HIGHEST)
        factor = jnp.linalg.cholesky(inner_product)
        matrix = lax.linalg.triangular_solve(factor, matrix, left_side=False, lower=True, transpose_a=True)
    return matrix

def pod_weights(gram_matrix, basis_start):
    basis_now = orthonormal(basis_start)
    for iteration in range(POD_ITERS):
        basis_now = orthonormal(jnp.dot(gram_matrix, basis_now, precision=lax.Precision.HIGHEST))
    return jnp.dot(basis_now, basis_now[-1], precision=lax.Precision.HIGHEST)

def advance_whole(particles, rest_density, particle_mass, near_index, cell_shifts):
    payload = make_payload(particles, rest_density, particle_mass)
    extended = jnp.pad(payload, ((1, 1), (1, 1), (0, 0), (0, 0)))
    acceleration, density_rate = interact(payload, extended, near_index, cell_shifts, 32)
    return update(particles, rest_density, acceleration, density_rate)

def reference(particles, phase_flags, neighbours, history, basis_start):
    rest_density = 1.0 + SEDIMENT_EXTRA * phase_flags.astype(jnp.float32)
    particle_mass = rest_density * VOLUME
    near_index, cell_shifts = block_layout(neighbours)
    first_state = advance_whole(particles, rest_density, particle_mass, near_index, cell_shifts)
    second_state = advance_whole(first_state, rest_density, particle_mass, near_index, cell_shifts)
    new_snapshots = jnp.stack([first_state[:, :, 3:6], second_state[:, :, 3:6]], axis=3).astype(jnp.bfloat16)
    block_count = particles.shape[0] * particles.shape[1]
    group_size = math.gcd(block_count, 64)
    hist_count = history.shape[3]
    part_count = history.shape[4]
    snap_count = basis_start.shape[0]
    hist_groups = history.reshape(block_count // group_size, group_size, 3, hist_count, part_count)
    new_groups = new_snapshots.reshape(block_count // group_size, group_size, 3, 2, part_count)

    def add_gram(total, pieces):
        snapshots = jnp.concatenate([pieces[0], pieces[1]], axis=2).astype(jnp.float32)
        return (total + jnp.einsum('bcsp,bctp->st', snapshots, snapshots, precision=lax.Precision.HIGHEST), None)
    gram_matrix, unused = lax.scan(add_gram, jnp.zeros((snap_count, snap_count), jnp.float32), (hist_groups, new_groups))
    weights = pod_weights(gram_matrix, basis_start)

    def filter_group(pieces):
        snapshots = jnp.concatenate([pieces[0], pieces[1]], axis=2).astype(jnp.float32)
        return jnp.einsum('bcsp,s->bcp', snapshots, weights, precision=lax.Precision.HIGHEST)
    filtered = lax.map(filter_group, (hist_groups, new_groups)).reshape(particles.shape[0], particles.shape[1], 3, part_count)
    return (second_state, filtered)
```

```python
import functools
import math

import jax
import jax.numpy as jnp
from jax import lax
from jax.experimental import pallas as pl
from jax.experimental.pallas import tpu as pltpu
from jax.sharding import PartitionSpec as P

POD_ITERS = 4
SEDIMENT_EXTRA = 1.65


ALPHA_KERNEL = 21.0 / (16.0 * math.pi)
VOLUME = 1.0 / 16.0
STIFFNESS = 100.0 / 7.0
TIME_STEP = 0.02
GRAVITY = 1.0
F32, BF16 = jnp.float32, jnp.bfloat16

def pieces(x):
    a = x.astype(BF16).astype(F32)
    r = x - a
    b = r.astype(BF16).astype(F32)
    return a, b, r - b

def rows(*parts):
    return jnp.concatenate(parts, axis=0)

def features(state):
    x, y, z = (state[i:i + 1] - 1.0 for i in range(3))
    u, v, w = (state[i:i + 1] for i in range(3, 6))
    r, rho = state[6:7], state[7:8]
    live = rho > 0.0
    mass = rho * VOLUME
    safe_rho = jnp.where(live, rho, 1.0)
    r2 = r * r
    pressure = jnp.where(live, STIFFNESS * (r2 * r2 * r2 * r - 1.0) / (safe_rho * r2), 0.0)
    zero, one = jnp.zeros_like(x), jnp.ones_like(x)
    norm = 0.25 * (x * x + y * y + z * z)
    mp = mass * pressure
    near = rows(-0.5 * x, -0.5 * y, -0.5 * z, one, norm, zero, zero, zero)
    near_x = rows(-0.5 * one, zero, zero, zero, 0.5 * x, zero, zero, zero)
    near_z = rows(zero, zero, -0.5 * one, zero, 0.5 * z, zero, zero, zero)
    mu, mv, mw = mass * u, mass * v, mass * w
    flux = mu * x + mv * y + mw * z
    sums_a = rows(mass, mass * x, mass * y, mass * z, mu, mv, mw, flux)
    sums_b = rows(mp, mp * x, mp * y, mp * z, zero, zero, zero, zero)
    sums_ax = rows(zero, mass, zero, zero, zero, zero, zero, mu)
    sums_az = rows(zero, zero, zero, mass, zero, zero, zero, mw)
    sums_bx = rows(zero, mp, zero, zero, zero, zero, zero, zero)
    sums_bz = rows(zero, zero, zero, mp, zero, zero, zero, zero)
    own = rows(x, y, z, norm, one, zero, zero, zero)
    return own, rows(near, sums_a, sums_b), rows(near_x, sums_ax, sums_bx), rows(near_z, sums_az, sums_bz), pressure

def step_kernel(codes_ref, edge_ref, mid_ref, low_ref, high_ref, out_ref, b0, b1, b2, nst, fst):
    count = out_ref.shape[0]
    ext = count + 2
    for col, ref in ((0, low_ref), (1, mid_ref), (2, high_ref)):
        def prep(i, _):
            st = ref[i]
            on = edge_ref[col]
            rowon = jnp.where(i == 0, edge_ref[3], jnp.where(i == ext - 1, edge_ref[4], 1))
            keep = (on * rowon).astype(F32)
            sel = lax.broadcasted_iota(jnp.int32, (8, 1), 0) == 7
            st = jnp.where(sel, st * keep, st)
            _, a, b, c, _ = features(st)
            b0[col * ext + i] = a
            b1[col * ext + i] = b
            b2[col * ext + i] = c
            return 0
        lax.fori_loop(0, ext, prep, 0, unroll=2)
    row = lax.broadcasted_iota(jnp.int32, (24, 1), 0)
    normrow = (row == 4).astype(F32)

    def block(b, _):
        st = mid_ref[b + 1]
        own, g_self, _, _, pressure = features(st)
        o1, o2, o3 = pieces(own)
        lhs = rows(o1, o1, o2, o2, o1, o3).astype(BF16)
        for n in range(5):
            if n == 0:
                g = b0[ext + b + 1]
            else:
                c = codes_ref[b, n - 1]
                o = c + jnp.where(c >= 4, 1, 0)
                ds1 = (o * 11) >> 5
                dv1 = o - 3 * ds1
                idx = dv1 * ext + b + ds1
                tx = 2.0 * (ds1 - 1).astype(F32)
                tz = 2.0 * (dv1 - 1).astype(F32)
                g = b0[idx] + tx * b1[idx] + tz * b2[idx] + normrow * (0.25 * (tx * tx + tz * tz))
            p1, p2, p3 = pieces(g[0:8])
            f1, f2, f3 = pieces(g[8:24])
            sl = slice(n * 128, (n + 1) * 128)
            nst[:, sl] = rows(p1, p2, p1, p2, p3, p1).astype(BF16)
            fst[:, sl] = rows(f1, f2, f3).astype(BF16)
        s = lax.dot_general(lhs, nst[...], (((0,), (0,)), ((), ())), preferred_element_type=F32)
        s = jnp.maximum(s, 1e-20)
        k = jnp.maximum(1.0 - s * lax.rsqrt(s), 0.0)
        wgt = k * k * k
        wh = wgt.astype(BF16)
        wl = (wgt - wh.astype(F32)).astype(BF16)
        f = fst[...]
        acc = lax.dot_general(wh, f, (((1,), (1,)), ((), ())), preferred_element_type=F32)
        acc = acc + lax.dot_general(wl, f, (((1,), (1,)), ((), ())), preferred_element_type=F32)
        acc = acc.T
        t = acc[0:16] + acc[16:32] + acc[32:48]
        x, vel = st[0:3] - 1.0, st[3:6]
        coef = -5.0 * ALPHA_KERNEL
        sw, swx, swv, swf = t[0:1], t[1:4], t[4:7], t[7:8]
        swp, swpx = t[8:9], t[9:12]
        dens = coef * (jnp.sum(vel * (x * sw - swx) - x * swv, axis=0, keepdims=True) + swf)
        acc3 = -coef * (pressure * (x * sw - swx) + x * swp - swpx)
        grav = jnp.where(lax.broadcasted_iota(jnp.int32, (3, 1), 0) == 2, -GRAVITY, 0.0)
        vel2 = vel + TIME_STEP * (acc3 + grav)
        pos2 = st[0:3] + TIME_STEP * vel2
        rho = st[7:8]
        r2 = st[6:7] + TIME_STEP * dens / rho
        out_ref[b] = rows(pos2, vel2, r2, rho)
        return 0
    lax.fori_loop(0, count, block, 0, unroll=1)

def sph_step(codes, edges, low, mid, high):
    ext, _, part = mid.shape
    count = ext - 2
    v = pl.BlockSpec(memory_space=pltpu.VMEM)
    sm = pl.BlockSpec(memory_space=pltpu.SMEM)
    return pl.pallas_call(step_kernel, out_shape=jax.ShapeDtypeStruct((count, 8, part), F32),
        in_specs=[sm, sm, v, v, v], out_specs=v,
        scratch_shapes=[pltpu.VMEM((3 * ext, 24, part), F32)] * 3 + [pltpu.VMEM((48, 5 * part), BF16)] * 2,
        compiler_params=pltpu.CompilerParams(vmem_limit_bytes=48 << 20),
    )(codes, edges, mid, low, high)


HI=lax.Precision.HIGHEST
def nt(a,b): return lax.dot_general(a,b,(((1,),(1,)),((),())),precision=HI,preferred_element_type=jnp.float32)
def diag_col(s):
    n=s.shape[0]
    eq=lax.broadcasted_iota(jnp.int32,s.shape,0)==lax.broadcasted_iota(jnp.int32,s.shape,1)
    return jnp.sum(jnp.where(eq,s,0.0),axis=1,keepdims=True)
def elim1(s,m):
    n=s.shape[0]
    sb=[s[8*k:8*k+8] for k in range(n//8)]; mb=[m[8*k:8*k+8] for k in range(n//8)]
    sub=lax.broadcasted_iota(jnp.int32,(8,1),0)
    for j in range(n):
        k,r=divmod(j,8)
        rs=sb[k][r:r+1]; rm=mb[k][r:r+1]
        inv=1.0/rs[:,j:j+1]
        us=rs*inv; um=rm*inv
        for i in range(k,n//8):
            c=sb[i][:,j:j+1]
            if i==k:
                if r==7: continue
                c=jnp.where(sub>r,c,0.0)
            sb[i]=sb[i]-c*us; mb[i]=mb[i]-c*um
    return jnp.concatenate(sb,0),jnp.concatenate(mb,0)
def ortho(m,elim):
    s=nt(m,m)
    d0=diag_col(s)
    s,m=elim(s,m)
    d=diag_col(s)
    return m*lax.rsqrt(d),jnp.min(d/d0)
def weights_kernel(elim,iters,g_ref,b_ref,w_ref,r_ref):
    g=g_ref[...]
    q=b_ref[...]
    q,r=ortho(q,elim)
    def it(i,c):
        q,r=c
        m=jnp.dot(q,g,precision=HI,preferred_element_type=jnp.float32)
        q,r2=ortho(m,elim)
        return q,jnp.minimum(r,r2)
    q,r=lax.fori_loop(0,iters,it,(q,r))
    n=q.shape[1]
    e=(lax.broadcasted_iota(jnp.int32,(1,n),1)==n-1).astype(jnp.float32)
    w=jnp.zeros((1,n),jnp.float32)
    for k in range(3):
        y=jnp.sum(q*(e-w),axis=1,keepdims=True)
        w=w+jnp.sum(q*y,axis=0,keepdims=True)
    w_ref[...]=jnp.broadcast_to(w,w_ref.shape)
    r_ref[...]=jnp.full(r_ref.shape,r)
def weights(elim,g,bt,iters=4):
    return pl.pallas_call(functools.partial(weights_kernel,elim,iters),out_shape=(jax.ShapeDtypeStruct((8,128),jnp.float32),jax.ShapeDtypeStruct((8,128),jnp.float32)),
      in_specs=[pl.BlockSpec(memory_space=pltpu.VMEM)]*2,out_specs=(pl.BlockSpec(memory_space=pltpu.VMEM),)*2)(g,bt)


def snapshot(hist_ref, first_ref, second_ref, b, c):
    new = rows(first_ref[b, 3 + c:4 + c], second_ref[b, 3 + c:4 + c])
    return rows(hist_ref[b, 0, c].astype(F32), new).astype(BF16)


def gram_kernel(hist_ref, first_ref, second_ref, g_ref):
    @pl.when(pl.program_id(0) == 0)
    def _():
        g_ref[...] = jnp.zeros_like(g_ref)
    total = g_ref[...]
    for b in range(hist_ref.shape[0]):
        for c in range(3):
            x = snapshot(hist_ref, first_ref, second_ref, b, c)
            total = total + lax.dot_general(x, x, (((1,), (1,)), ((), ())), preferred_element_type=F32)
    g_ref[...] = total


def filter_kernel(hist_ref, first_ref, second_ref, w_ref, out_ref):
    w1, w2, w3 = pieces(w_ref[0:1])
    zero = jnp.zeros_like(w1)
    w = rows(w1, w2, w3, zero, zero, zero, zero, zero).astype(BF16)
    for b in range(hist_ref.shape[0]):
        for c in range(3):
            x = snapshot(hist_ref, first_ref, second_ref, b, c)
            f = jnp.dot(w, x, preferred_element_type=F32)
            out_ref[b, 0, c:c + 1] = f[0:1] + f[1:2] + f[2:3]


def hist_specs(history, first, group):
    return [
        pl.BlockSpec((group,) + history.shape[1:], lambda i: (i, 0, 0, 0, 0)),
        pl.BlockSpec((group,) + first.shape[1:], lambda i: (i, 0, 0)),
        pl.BlockSpec((group,) + first.shape[1:], lambda i: (i, 0, 0)),
    ]


def local_gram(history, first, second):
    snaps = history.shape[3] + 2
    group = math.gcd(history.shape[0], 4)
    return pl.pallas_call(
        gram_kernel, grid=(history.shape[0] // group,),
        out_shape=jax.ShapeDtypeStruct((snaps, snaps), F32),
        in_specs=hist_specs(history, first, group),
        out_specs=pl.BlockSpec((snaps, snaps), lambda i: (0, 0)),
    )(history, first, second)


def local_filter(history, first, second, weights):
    group = math.gcd(history.shape[0], 4)
    count, _, comps, _, part = history.shape
    return pl.pallas_call(
        filter_kernel, grid=(count // group,),
        out_shape=jax.ShapeDtypeStruct((count, 1, comps, part), F32),
        in_specs=hist_specs(history, first, group) + [pl.BlockSpec(weights.shape, lambda i: (0, 0))],
        out_specs=pl.BlockSpec((group, 1, comps, part), lambda i: (i, 0, 0, 0)),
    )(history, first, second, weights)


def shift(x, axis, by):
    count = lax.axis_size(axis)
    return lax.ppermute(x, axis, [(i, (i + by) % count) for i in range(count)])


def reduce_all(x):
    for axis in ("vert", "stream"):
        count = lax.axis_size(axis)
        if count & (count - 1):
            x = lax.psum(x, axis)
            continue
        k = 1
        while k < count:
            x = x + lax.ppermute(x, axis, [(i, i ^ k) for i in range(count)])
            k *= 2
    return x


def advance(codes, edges, state):
    low_row = shift(state[-1:], "stream", 1)
    high_row = shift(state[:1], "stream", -1)
    mid = jnp.concatenate([low_row, state, high_row], axis=0)
    low = shift(mid, "vert", 1)
    high = shift(mid, "vert", -1)
    return sph_step(codes, edges, low, mid, high)


def body(particles, phase_flags, neighbours, history, basis_start):
    rest_density = 1.0 + SEDIMENT_EXTRA * phase_flags.astype(F32)
    state = jnp.concatenate([particles[:, 0], rest_density], axis=1)
    codes = neighbours[:, 0]
    s, v = lax.axis_index("stream"), lax.axis_index("vert")
    ns, nv = lax.axis_size("stream"), lax.axis_size("vert")
    one = jnp.ones((), jnp.int32)
    edges = jnp.stack([v > 0, one, v < nv - 1, s > 0, s < ns - 1, one, one, one]).astype(jnp.int32)
    first = advance(codes, edges, state)
    second = advance(codes, edges, first)
    gram = reduce_all(local_gram(history, first, second))
    w = weights(elim1, gram, basis_start.T, POD_ITERS)[0]
    return (second[:, None, 0:7], local_filter(history, first, second, w))


def solution(mesh):
    in_specs = (
        P("stream", "vert", None, None),
        P("stream", "vert", None),
        P("stream", "vert", None),
        P("stream", "vert", None, None, None),
        P(),
    )
    out_specs = (P("stream", "vert", None, None), P("stream", "vert", None, None))
    return jax.shard_map(body, mesh=mesh, in_specs=in_specs, out_specs=out_specs, check_vma=False)
```

```python
import functools
import math

import jax
import jax.numpy as jnp
from jax import lax
from jax.experimental import pallas as pl
from jax.experimental.pallas import tpu as pltpu
from jax.sharding import PartitionSpec as P

POD_ITERS = 4
SEDIMENT_EXTRA = 1.65


ALPHA_KERNEL = 21.0 / (16.0 * math.pi)
VOLUME = 1.0 / 16.0
STIFFNESS = 100.0 / 7.0
TIME_STEP = 0.02
GRAVITY = 1.0
F32, BF16 = jnp.float32, jnp.bfloat16

def pieces(x):
    a = x.astype(BF16).astype(F32)
    r = x - a
    b = r.astype(BF16).astype(F32)
    return a, b, r - b

def rows(*parts):
    return jnp.concatenate(parts, axis=0)

def row_is(*which):
    index = lax.broadcasted_iota(jnp.int32, (8, 128), 0)
    hit = index == which[0]
    for w in which[1:]:
        hit = hit | (index == w)
    return hit

def spread(row):
    return jnp.broadcast_to(row, (8, row.shape[1]))

def features(state):
    centred = jnp.where(row_is(0, 1, 2), state - 1.0, state)
    r, rho = spread(state[6:7]), spread(state[7:8])
    live = rho > 0.0
    mass = rho * VOLUME
    r2 = r * r
    pressure = jnp.where(live, STIFFNESS * (r2 * r2 * r2 * r - 1.0) / (jnp.where(live, rho, 1.0) * r2), 0.0)
    mp = mass * pressure
    place = jnp.where(row_is(0, 1, 2), centred, 0.0)
    norm = 0.25 * jnp.sum(place * place, axis=0, keepdims=True)
    speed = jnp.where(row_is(0, 1, 2), pltpu.roll(centred, 5, 0), 0.0)
    flux = jnp.sum(place * speed, axis=0, keepdims=True)
    own = jnp.where(row_is(3), norm, jnp.where(row_is(4), 1.0, place))
    near = jnp.where(row_is(3), 1.0, jnp.where(row_is(4), norm, -0.5 * place))
    moved = jnp.where(row_is(0), 1.0, jnp.where(row_is(7), flux, pltpu.roll(centred, 1, 0)))
    sums_a = mass * moved
    sums_b = jnp.where(row_is(0, 1, 2, 3), mp * moved, 0.0)
    near_x = jnp.where(row_is(0), -0.5, jnp.where(row_is(4), 0.5 * centred[0:1], 0.0))
    near_z = jnp.where(row_is(2), -0.5, jnp.where(row_is(4), 0.5 * centred[2:3], 0.0))
    sums_ax = mass * jnp.where(row_is(1), 1.0, jnp.where(row_is(7), centred[3:4], 0.0))
    sums_az = mass * jnp.where(row_is(3), 1.0, jnp.where(row_is(7), centred[5:6], 0.0))
    sums_bx = jnp.where(row_is(1), mp, 0.0)
    sums_bz = jnp.where(row_is(3), mp, 0.0)
    return own, rows(near, sums_a, sums_b), rows(near_x, sums_ax, sums_bx), rows(near_z, sums_az, sums_bz), pressure[0:1]

def step_kernel(codes_ref, edge_ref, mid_ref, low_ref, high_ref, out_ref, b0, b1, b2):
    count = out_ref.shape[0]
    ext = count + 2
    for col, ref in ((0, low_ref), (1, mid_ref), (2, high_ref)):
        def prep(i, _):
            st = ref[i]
            on = edge_ref[col]
            rowon = jnp.where(i == 0, edge_ref[3], jnp.where(i == ext - 1, edge_ref[4], 1))
            keep = (on * rowon).astype(F32)
            sel = lax.broadcasted_iota(jnp.int32, (8, 1), 0) == 7
            st = jnp.where(sel, st * keep, st)
            _, a, b, c, _ = features(st)
            b0[col * ext + i] = a
            b1[col * ext + i] = b
            b2[col * ext + i] = c
            return 0
        lax.fori_loop(0, ext, prep, 0, unroll=2 if ext % 2 == 0 else 1)
    row = lax.broadcasted_iota(jnp.int32, (24, 1), 0)
    normrow = (row == 4).astype(F32)

    def block(b, _):
        st = mid_ref[b + 1]
        own, g_self, _, _, pressure = features(st)
        o1, o2, o3 = pieces(own)
        lhs = rows(o1, o1, o2, o2, o1, o3).astype(BF16)
        ns, fs = [], []
        for n in range(5):
            if n == 0:
                g = b0[ext + b + 1]
            else:
                c = codes_ref[b, n - 1]
                o = c + jnp.where(c >= 4, 1, 0)
                ds1 = (o * 11) >> 5
                dv1 = o - 3 * ds1
                idx = dv1 * ext + b + ds1
                tx = 2.0 * (ds1 - 1).astype(F32)
                tz = 2.0 * (dv1 - 1).astype(F32)
                g = b0[idx] + tx * b1[idx] + tz * b2[idx] + normrow * (0.25 * (tx * tx + tz * tz))
            p1, p2, p3 = pieces(g[0:8])
            f1, f2, f3 = pieces(g[8:24])
            ns.append(rows(p1, p2, p1, p2, p3, p1).astype(BF16))
            fs.append(rows(f1, f2, f3).astype(BF16))
        nall = jnp.concatenate(ns, axis=1)
        f = jnp.concatenate(fs+fs, axis=1)
        s = lax.dot_general(nall, lhs, (((0,), (0,)), ((), ())), preferred_element_type=F32)
        s = jnp.maximum(s, 1e-20)
        k = jnp.maximum(1.0 - s * lax.rsqrt(s), 0.0)
        wgt = k * k * k
        wh = wgt.astype(BF16)
        wl = (wgt - wh.astype(F32)).astype(BF16)
        acc = jnp.dot(f, jnp.concatenate([wh,wl],0), preferred_element_type=F32)
        t = acc[0:16] + acc[16:32] + acc[32:48]
        x, vel = st[0:3] - 1.0, st[3:6]
        coef = -5.0 * ALPHA_KERNEL
        sw, swx, swv, swf = t[0:1], t[1:4], t[4:7], t[7:8]
        swp, swpx = t[8:9], t[9:12]
        dens = coef * (jnp.sum(vel * (x * sw - swx) - x * swv, axis=0, keepdims=True) + swf)
        acc3 = -coef * (pressure * (x * sw - swx) + x * swp - swpx)
        grav = jnp.where(lax.broadcasted_iota(jnp.int32, (3, 1), 0) == 2, -GRAVITY, 0.0)
        vel2 = vel + TIME_STEP * (acc3 + grav)
        pos2 = st[0:3] + TIME_STEP * vel2
        rho = st[7:8]
        r2 = st[6:7] + TIME_STEP * dens / rho
        out_ref[b] = rows(pos2, vel2, r2, rho)
        return 0
    lax.fori_loop(0, count, block, 0, unroll=math.gcd(count, 8))

def sph_step(codes, edges, low, mid, high):
    ext, _, part = mid.shape
    count = ext - 2
    v = pl.BlockSpec(memory_space=pltpu.VMEM)
    sm = pl.BlockSpec(memory_space=pltpu.SMEM)
    return pl.pallas_call(step_kernel, out_shape=jax.ShapeDtypeStruct((count, 8, part), F32),
        in_specs=[sm, sm, v, v, v], out_specs=v,
        scratch_shapes=[pltpu.VMEM((3 * ext, 24, part), F32)] * 3,
        compiler_params=pltpu.CompilerParams(vmem_limit_bytes=48 << 20),
    )(codes, edges, mid, low, high)


HIGHEST = lax.Precision.HIGHEST
REPEAT_BELOW = 1e-5


def gram_of(m):
    return lax.dot_general(m, m, (((1,), (1,)), ((), ())), precision=HIGHEST, preferred_element_type=F32)


def orthonormal(m):
    n, wide = m.shape
    nb = n // 8
    s = gram_of(m)
    s = jnp.concatenate([s, jnp.zeros((n, wide - n), F32)], axis=1)
    sb = [s[8 * k:8 * k + 8] for k in range(nb)]
    mb = [m[8 * k:8 * k + 8] for k in range(nb)]
    sub = lax.broadcasted_iota(jnp.int32, (8, wide), 0)
    full = lambda x: jnp.broadcast_to(x, (8, wide))
    worst = None
    for k in range(nb):
        p = 8 * k
        norm0 = jnp.sum(m[8 * k:8 * k + 8] * m[8 * k:8 * k + 8], axis=1, keepdims=True)
        rs = [full(sb[k][i:i + 1]) for i in range(8)]
        rm = [full(mb[k][i:i + 1]) for i in range(8)]
        e = [[full(rs[i][:, p + j:p + j + 1]) for j in range(i + 1)] for i in range(8)]
        cols = [[full(sb[t][:, p + j:p + j + 1]) for j in range(8)] for t in range(k + 1, nb)]
        inv, low = [], [[None] * 8 for _ in range(8)]
        for j in range(8):
            inv.append(1.0 / e[j][j])
            for i in range(j + 1, 8):
                for t in range(j + 1, i + 1):
                    e[i][t] = e[i][t] - (e[i][j] * e[t][j]) * inv[j]
            for i in range(j + 1, 8):
                low[i][j] = e[i][j] * inv[j]
            for i in range(j + 1, 8):
                rs[i] = rs[i] - low[i][j] * rs[j]
                rm[i] = rm[i] - low[i][j] * rm[j]
        d = e[0][0]
        out = rm[0]
        for i in range(1, 8):
            d = jnp.where(sub == i, e[i][i], d)
            out = jnp.where(sub == i, rm[i], out)
        mb[k] = out * lax.rsqrt(d)
        ratio = d / norm0
        worst = ratio if worst is None else jnp.minimum(worst, ratio)
        if k == nb - 1:
            break
        us = [rs[j] * inv[j] for j in range(8)]
        um = [rm[j] * inv[j] for j in range(8)]
        for t in range(k + 1, nb):
            c = cols[t - k - 1]
            for j in range(8):
                for i in range(j + 1, 8):
                    c[i] = c[i] - low[i][j] * c[j]
                sb[t] = sb[t] - c[j] * us[j]
                mb[t] = mb[t] - c[j] * um[j]
    return jnp.concatenate(mb, 0), jnp.min(worst)


def repeated(m, q_ref):
    q, worst = orthonormal(m)
    q_ref[...] = q

    @pl.when(jnp.logical_not(worst >= REPEAT_BELOW))
    def _():
        q_ref[...] = orthonormal(q_ref[...])[0]


def weights_kernel(iters, g_ref, b_ref, w_ref, q_ref):
    repeated(b_ref[...], q_ref)

    def iterate(i, _):
        repeated(jnp.dot(q_ref[...], g_ref[...], precision=HIGHEST, preferred_element_type=F32), q_ref)
        return 0

    lax.fori_loop(0, iters, iterate, 0)
    q = q_ref[...]
    n = q.shape[1]
    last = (lax.broadcasted_iota(jnp.int32, (1, n), 1) == n - 1).astype(F32)
    w = jnp.zeros((1, n), F32)
    for _ in range(3):
        y = jnp.sum(q * (last - w), axis=1, keepdims=True)
        w = w + jnp.sum(q * y, axis=0, keepdims=True)
    w_ref[...] = jnp.broadcast_to(w, w_ref.shape)


def weights(gram, basis_t):
    v = pl.BlockSpec(memory_space=pltpu.VMEM)
    return pl.pallas_call(
        functools.partial(weights_kernel, POD_ITERS),
        out_shape=jax.ShapeDtypeStruct((8, gram.shape[0]), F32),
        in_specs=[v, v], out_specs=v,
        scratch_shapes=[pltpu.VMEM(basis_t.shape, F32)],
    )(gram, basis_t)


def snapshot(hist_ref, first_ref, second_ref, b, c):
    new = rows(first_ref[b, 3 + c:4 + c], second_ref[b, 3 + c:4 + c])
    return rows(hist_ref[b, 0, c].astype(F32), new).astype(BF16)


def gram_kernel(hist_ref, first_ref, second_ref, g_ref):
    @pl.when(pl.program_id(0) == 0)
    def _():
        g_ref[...] = jnp.zeros_like(g_ref)
    total = g_ref[...]
    for b in range(hist_ref.shape[0]):
        for c in range(3):
            x = snapshot(hist_ref, first_ref, second_ref, b, c)
            total = total + lax.dot_general(x, x, (((1,), (1,)), ((), ())), preferred_element_type=F32)
    g_ref[...] = total


def filter_kernel(hist_ref, first_ref, second_ref, w_ref, out_ref):
    w1, w2, w3 = pieces(w_ref[0:1])
    zero = jnp.zeros_like(w1)
    w = rows(w1, w2, w3, zero, zero, zero, zero, zero).astype(BF16)
    for b in range(hist_ref.shape[0]):
        for c in range(3):
            x = snapshot(hist_ref, first_ref, second_ref, b, c)
            f = jnp.dot(w, x, preferred_element_type=F32)
            out_ref[b, 0, c:c + 1] = f[0:1] + f[1:2] + f[2:3]


def hist_specs(history, first, group):
    return [
        pl.BlockSpec((group,) + history.shape[1:], lambda i: (i, 0, 0, 0, 0)),
        pl.BlockSpec((group,) + first.shape[1:], lambda i: (i, 0, 0)),
        pl.BlockSpec((group,) + first.shape[1:], lambda i: (i, 0, 0)),
    ]


def local_gram(history, first, second):
    snaps = history.shape[3] + 2
    group = math.gcd(history.shape[0], 4)
    return pl.pallas_call(
        gram_kernel, grid=(history.shape[0] // group,),
        out_shape=jax.ShapeDtypeStruct((snaps, snaps), F32),
        in_specs=hist_specs(history, first, group),
        out_specs=pl.BlockSpec((snaps, snaps), lambda i: (0, 0)),
    )(history, first, second)


def local_filter(history, first, second, weights):
    group = math.gcd(history.shape[0], 4)
    count, _, comps, _, part = history.shape
    return pl.pallas_call(
        filter_kernel, grid=(count // group,),
        out_shape=jax.ShapeDtypeStruct((count, 1, comps, part), F32),
        in_specs=hist_specs(history, first, group) + [pl.BlockSpec(weights.shape, lambda i: (0, 0))],
        out_specs=pl.BlockSpec((group, 1, comps, part), lambda i: (i, 0, 0, 0)),
    )(history, first, second, weights)


def shift(x, axis, by):
    count = lax.axis_size(axis)
    return lax.ppermute(x, axis, [(i, (i + by) % count) for i in range(count)])


def reduce_all(x):
    for axis in ("vert", "stream"):
        count = lax.axis_size(axis)
        if count & (count - 1):
            x = lax.psum(x, axis)
            continue
        k = 1
        while k < count:
            x = x + lax.ppermute(x, axis, [(i, i ^ k) for i in range(count)])
            k *= 2
    return x


def advance(codes, edges, state):
    low_row = shift(state[-1:], "stream", 1)
    high_row = shift(state[:1], "stream", -1)
    mid = jnp.concatenate([low_row, state, high_row], axis=0)
    low = shift(mid, "vert", 1)
    high = shift(mid, "vert", -1)
    return sph_step(codes, edges, low, mid, high)


def body(particles, phase_flags, neighbours, history, basis_start):
    rest_density = 1.0 + SEDIMENT_EXTRA * phase_flags.astype(F32)
    state = jnp.concatenate([particles[:, 0], rest_density], axis=1)
    codes = neighbours[:, 0]
    s, v = lax.axis_index("stream"), lax.axis_index("vert")
    ns, nv = lax.axis_size("stream"), lax.axis_size("vert")
    one = jnp.ones((), jnp.int32)
    edges = jnp.stack([v > 0, one, v < nv - 1, s > 0, s < ns - 1, one, one, one]).astype(jnp.int32)
    first = advance(codes, edges, state)
    second = advance(codes, edges, first)
    gram = reduce_all(local_gram(history, first, second))
    w = weights(gram, basis_start.T)
    return (second[:, None, 0:7], local_filter(history, first, second, w))


def solution(mesh):
    in_specs = (
        P("stream", "vert", None, None),
        P("stream", "vert", None),
        P("stream", "vert", None),
        P("stream", "vert", None, None, None),
        P(),
    )
    out_specs = (P("stream", "vert", None, None), P("stream", "vert", None, None))
    return jax.shard_map(body, mesh=mesh, in_specs=in_specs, out_specs=out_specs, check_vma=False)
```

```python
import functools
import math

import jax
import jax.numpy as jnp
from jax import lax
from jax.experimental import pallas as pl
from jax.experimental.pallas import tpu as pltpu
from jax.sharding import PartitionSpec as P

POD_ITERS = 4
SEDIMENT_EXTRA = 1.65


ALPHA_KERNEL = 21.0 / (16.0 * math.pi)
VOLUME = 1.0 / 16.0
STIFFNESS = 100.0 / 7.0
TIME_STEP = 0.02
GRAVITY = 1.0
F32, BF16 = jnp.float32, jnp.bfloat16

def pieces(x):
    a = x.astype(BF16).astype(F32)
    r = x - a
    b = r.astype(BF16).astype(F32)
    return a, b, r - b

def rows(*parts):
    return jnp.concatenate(parts, axis=0)

def row_is(*which):
    index = lax.broadcasted_iota(jnp.int32, (8, 128), 0)
    hit = index == which[0]
    for w in which[1:]:
        hit = hit | (index == w)
    return hit

def spread(row):
    return jnp.broadcast_to(row, (8, row.shape[1]))

def features(state):
    centred = jnp.where(row_is(0, 1, 2), state - 1.0, state)
    r, rho = spread(state[6:7]), spread(state[7:8])
    live = rho > 0.0
    mass = rho * VOLUME
    r2 = r * r
    pressure = jnp.where(live, STIFFNESS * (r2 * r2 * r2 * r - 1.0) / (jnp.where(live, rho, 1.0) * r2), 0.0)
    mp = mass * pressure
    place = jnp.where(row_is(0, 1, 2), centred, 0.0)
    norm = 0.25 * jnp.sum(place * place, axis=0, keepdims=True)
    speed = jnp.where(row_is(0, 1, 2), pltpu.roll(centred, 5, 0), 0.0)
    flux = jnp.sum(place * speed, axis=0, keepdims=True)
    own = jnp.where(row_is(3), norm, jnp.where(row_is(4), 1.0, place))
    near = jnp.where(row_is(3), 1.0, jnp.where(row_is(4), norm, -0.5 * place))
    moved = jnp.where(row_is(0), 1.0, jnp.where(row_is(7), flux, pltpu.roll(centred, 1, 0)))
    sums_a = mass * moved
    sums_b = jnp.where(row_is(0, 1, 2, 3), mp * moved, 0.0)
    near_x = jnp.where(row_is(0), -0.5, jnp.where(row_is(4), 0.5 * centred[0:1], 0.0))
    near_z = jnp.where(row_is(2), -0.5, jnp.where(row_is(4), 0.5 * centred[2:3], 0.0))
    sums_ax = mass * jnp.where(row_is(1), 1.0, jnp.where(row_is(7), centred[3:4], 0.0))
    sums_az = mass * jnp.where(row_is(3), 1.0, jnp.where(row_is(7), centred[5:6], 0.0))
    sums_bx = jnp.where(row_is(1), mp, 0.0)
    sums_bz = jnp.where(row_is(3), mp, 0.0)
    return own, rows(near, sums_a, sums_b), rows(near_x, sums_ax, sums_bx), rows(near_z, sums_az, sums_bz), pressure[0:1]

def prep_kernel(particles_ref, flags_ref, codes_ref, state_ref, lo_ref, hi_ref, flat):
    count = flags_ref.shape[0]
    fields = particles_ref.shape[0] // count
    for i in range(fields):
        flat[pl.ds(i, count, stride=8), :] = particles_ref[pl.ds(i, count, stride=fields), :]
    flat[pl.ds(fields, count, stride=8), :] = 1.0 + SEDIMENT_EXTRA * flags_ref[...].astype(F32)
    for b in range(count):
        state_ref[b] = flat[8 * b:8 * b + 8]
    for ref, first, edge in ((lo_ref, 0, 0), (hi_ref, count - 2, count - 1)):
        for i in range(2):
            ref[i] = flat[8 * (first + i):8 * (first + i) + 8]
        ref[2] = jnp.zeros_like(ref[2])
        ref[2, 0:codes_ref.shape[0], 0:1] = codes_ref[:, edge:edge + 1].astype(F32)


def prepare(particles, flags, codes):
    count, fields, part = particles.shape
    v = pl.BlockSpec(memory_space=pltpu.VMEM)
    rim = jax.ShapeDtypeStruct((3, 8, part), F32)
    return pl.pallas_call(
        prep_kernel,
        out_shape=(jax.ShapeDtypeStruct((count, 8, part), F32), rim, rim),
        in_specs=[v, v, v], out_specs=(v, v, v),
        scratch_shapes=[pltpu.VMEM((count * 8, part), F32)],
    )(particles.reshape(count * fields, part), flags, codes)


def step_blocks(codes_ref, edge_ref, low_ref, mid_ref, high_ref, out_ref, b0, b1, b2):
    ext = mid_ref.shape[0]
    count = ext - 2
    sel = lax.broadcasted_iota(jnp.int32, (8, 1), 0) == 7
    rim = edge_ref[5]
    for col, ref in ((0, low_ref), (1, mid_ref), (2, high_ref)):
        def prep(i, _):
            st = ref[i]
            rowon = jnp.where(i < rim, edge_ref[3], jnp.where(i >= ext - rim, edge_ref[4], 1))
            keep = (edge_ref[col] * rowon).astype(F32)
            _, a, b, c, _ = features(jnp.where(sel, st * keep, st))
            b0[col * ext + i] = a
            b1[col * ext + i] = b
            b2[col * ext + i] = c
            return 0
        lax.fori_loop(0, ext, prep, 0, unroll=2 if ext % 2 == 0 else 1)
    normrow = (lax.broadcasted_iota(jnp.int32, (24, 1), 0) == 4).astype(F32)
    skip = edge_ref[6]

    def block(b, _):
        st = mid_ref[b + 1]
        own, g_self, _, _, pressure = features(st)
        o1, o2, o3 = pieces(own)
        rhs = rows(o1, o1, o2, o2, o1, o3).astype(BF16)
        ns, fs = [], []
        for n in range(codes_ref.shape[0] + 1):
            if n == 0:
                g = g_self
            else:
                c = codes_ref[n - 1, b + skip]
                o = c + jnp.where(c >= 4, 1, 0)
                ds1 = (o * 11) >> 5
                dv1 = o - 3 * ds1
                idx = dv1 * ext + b + ds1
                tx = 2.0 * (ds1 - 1).astype(F32)
                tz = 2.0 * (dv1 - 1).astype(F32)
                g = b0[idx] + tx * b1[idx] + tz * b2[idx] + normrow * (0.25 * (tx * tx + tz * tz))
            p1, p2, p3 = pieces(g[0:8])
            f1, f2, f3 = pieces(g[8:24])
            ns.append(rows(p1, p2, p1, p2, p3, p1).astype(BF16))
            fs.append(rows(f1, f2, f3).astype(BF16))
        nall = jnp.concatenate(ns, axis=1)
        f = jnp.concatenate(fs + fs, axis=1)
        s = lax.dot_general(nall, rhs, (((0,), (0,)), ((), ())), preferred_element_type=F32)
        s = jnp.maximum(s, 1e-20)
        k = jnp.maximum(1.0 - s * lax.rsqrt(s), 0.0)
        wgt = k * k * k
        wh = wgt.astype(BF16)
        wl = (wgt - wh.astype(F32)).astype(BF16)
        acc = jnp.dot(f, jnp.concatenate([wh, wl], 0), preferred_element_type=F32)
        t = acc[0:16] + acc[16:32] + acc[32:48]
        x, vel = st[0:3] - 1.0, st[3:6]
        coef = -5.0 * ALPHA_KERNEL
        sw, swx, swv, swf = t[0:1], t[1:4], t[4:7], t[7:8]
        swp, swpx = t[8:9], t[9:12]
        dens = coef * (jnp.sum(vel * (x * sw - swx) - x * swv, axis=0, keepdims=True) + swf)
        acc3 = -coef * (pressure * (x * sw - swx) + x * swp - swpx)
        grav = jnp.where(lax.broadcasted_iota(jnp.int32, (3, 1), 0) == 2, -GRAVITY, 0.0)
        vel2 = vel + TIME_STEP * (acc3 + grav)
        pos2 = st[0:3] + TIME_STEP * vel2
        rho = st[7:8]
        r2 = st[6:7] + TIME_STEP * dens / rho
        out_ref[b] = rows(pos2, vel2, r2, rho)
        return 0
    unroll = max(u for u in range(1, 18) if count % u == 0)
    lax.fori_loop(0, count, block, 0, unroll=unroll)


def step_scratch(ext, part):
    return [pltpu.VMEM((3 * ext, 24, part), F32)] * 3


def first_step(codes, edges, low, mid, high, basis):
    ext, _, part = mid.shape
    v = pl.BlockSpec(memory_space=pltpu.VMEM)
    sm = pl.BlockSpec(memory_space=pltpu.SMEM)
    def kernel(codes_ref, edge_ref, low_ref, mid_ref, high_ref, basis_any, out_ref, *scratch):
        step_blocks(codes_ref, edge_ref, low_ref, mid_ref, high_ref, out_ref, *scratch)

    return pl.pallas_call(
        kernel, out_shape=jax.ShapeDtypeStruct((ext - 2, 8, part), F32),
        in_specs=[sm, sm, v, v, v, pl.BlockSpec(memory_space=pl.ANY)], out_specs=v,
        scratch_shapes=step_scratch(ext, part),
        compiler_params=pltpu.CompilerParams(vmem_limit_bytes=48 << 20),
    )(codes, edges, low, mid, high, basis)


def cross_row(hist_ref, new, others, terms):
    comps, hist = hist_ref.shape[0], hist_ref.shape[1]
    groups = new[0].shape[0] // 8

    def fold(x):
        total = x[0:8]
        for g in range(1, groups):
            total = total + x[8 * g:8 * g + 8]
        return total

    def one(s, _):
        total = hist_ref[0, s].astype(F32) * new[0]
        for c in range(1, comps):
            total = total + hist_ref[c, s].astype(F32) * new[c]
        terms[pl.ds(pl.multiple_of(8 * s, 8), 8), :] = fold(total)
        return 0
    lax.fori_loop(0, hist, one, 0, unroll=max(u for u in range(1, 10) if hist % u == 0))
    snaps = terms.shape[0] // 8
    for k in range(snaps - hist):
        if k < len(others):
            total = others[k][0] * new[0]
            for c in range(1, comps):
                total = total + others[k][c] * new[c]
            terms[8 * (hist + k):8 * (hist + k) + 8] = fold(total)
        else:
            terms[8 * (hist + k):8 * (hist + k) + 8] = jnp.zeros_like(terms[0:8])
    by_snap = terms[pl.ds(0, snaps, stride=8), :]
    for i in range(1, 8):
        by_snap = by_snap + terms[pl.ds(i, snaps, stride=8), :]
    ones = jnp.ones((8, by_snap.shape[1]), F32)
    return lax.dot_general(ones, by_snap, (((1,), (1,)), ((), ())), precision=HIGHEST, preferred_element_type=F32)[0:1]


def load_new(ref, skip, count, flat):
    def move(b, _):
        flat[pl.ds(pl.multiple_of(8 * b, 8), 8), :] = ref[b + skip]
        return 0
    lax.fori_loop(0, count, move, 0, unroll=math.gcd(count, 8))
    return [flat[pl.ds(3 + c, count, stride=8), :].astype(BF16).astype(F32) for c in range(3)]


def second_step(codes, edges, low, mid, high, hist, gram):
    ext, _, part = mid.shape
    count = ext - 2
    snaps = gram.shape[0]
    v = pl.BlockSpec(memory_space=pltpu.VMEM)
    sm = pl.BlockSpec(memory_space=pltpu.SMEM)

    def kernel(codes_ref, edge_ref, low_ref, mid_ref, high_ref, hist_any, gram_ref, new_ref, state_ref, gram_out,
               b0, b1, b2, hist_ref, flat, terms, sem):
        copy = pltpu.make_async_copy(hist_any, hist_ref, sem)
        copy.start()
        step_blocks(codes_ref, edge_ref, low_ref, mid_ref, high_ref, state_ref, b0, b1, b2)
        copy.wait()
        first = load_new(mid_ref, 1, count, flat)
        second = load_new(state_ref, 0, count, flat)
        for i in range(7):
            new_ref[pl.ds(i, count, stride=7), :] = flat[pl.ds(i, count, stride=8), :]
        row = cross_row(hist_ref, second, (first, second), terms)
        last = lax.broadcasted_iota(jnp.int32, (snaps, 1), 0) == snaps - 1
        gram_out[...] = jnp.where(last, row, gram_ref[...])

    return pl.pallas_call(
        kernel,
        out_shape=(jax.ShapeDtypeStruct((count * 7, part), F32), jax.ShapeDtypeStruct((count, 8, part), F32),
                   jax.ShapeDtypeStruct((snaps, snaps), F32)),
        in_specs=[sm, sm, v, v, v, pl.BlockSpec(memory_space=pl.ANY), v], out_specs=(v, v, v),
        scratch_shapes=step_scratch(ext, part) + [
            pltpu.VMEM(hist.shape, BF16), pltpu.VMEM((count * 8, part), F32), pltpu.VMEM((snaps * 8, part), F32),
            pltpu.SemaphoreType.DMA],
        compiler_params=pltpu.CompilerParams(vmem_limit_bytes=48 << 20),
    )(codes, edges, low, mid, high, hist, gram)


def early_gram(hist, first):
    comps, snaps_old, count, part = hist.shape
    snaps = snaps_old + 2
    v = pl.BlockSpec(memory_space=pltpu.VMEM)

    def kernel(hist_any, first_ref, out_ref, hist_ref, wide, flat, terms, sems):
        copies = [pltpu.make_async_copy(hist_any.at[c], hist_ref.at[c], sems.at[c]) for c in range(comps)]
        for copy in copies:
            copy.start()
        total = jnp.zeros((snaps_old, snaps_old), F32)
        for c in range(comps):
            copies[c].wait()

            def expand(s, _):
                wide[pl.ds(pl.multiple_of(count * s, 8), count), :] = hist_ref[c, s].astype(F32)
                return 0
            lax.fori_loop(0, snaps_old, expand, 0, unroll=max(u for u in range(1, 10) if snaps_old % u == 0))
            for b in range(0, count, 8):
                x = jnp.concatenate([wide[pl.ds(b + j, snaps_old, stride=count), :].astype(BF16) for j in range(8)], axis=1)
                total = total + lax.dot_general(x, x, (((1,), (1,)), ((), ())), preferred_element_type=F32)
        out_ref[...] = jnp.zeros_like(out_ref)
        out_ref[0:snaps_old, 0:snaps_old] = total
        new = load_new(first_ref, 1, count, flat)
        out_ref[snaps_old:snaps_old + 1] = cross_row(hist_ref, new, (new,), terms)

    return pl.pallas_call(
        kernel, out_shape=jax.ShapeDtypeStruct((snaps, snaps), F32),
        in_specs=[pl.BlockSpec(memory_space=pl.ANY), v], out_specs=v,
        scratch_shapes=[pltpu.VMEM(hist.shape, BF16), pltpu.VMEM((snaps_old * count, part), F32), pltpu.VMEM((count * 8, part), F32),
                        pltpu.VMEM((snaps * 8, part), F32), pltpu.SemaphoreType.DMA((comps,))],
        compiler_params=pltpu.CompilerParams(vmem_limit_bytes=48 << 20),
        cost_estimate=pl.CostEstimate(flops=2 * comps * snaps * snaps * count * part, bytes_accessed=2 * comps * snaps * count * part, transcendentals=0),
    )(hist, first)


HIGHEST = lax.Precision.HIGHEST
REPEAT_BELOW = 1e-5


def gram_of(m):
    return lax.dot_general(m, m, (((1,), (1,)), ((), ())), precision=HIGHEST, preferred_element_type=F32)


def orthonormal(m):
    n, wide = m.shape
    nb = n // 8
    s = gram_of(m)
    s = jnp.concatenate([s, jnp.zeros((n, wide - n), F32)], axis=1)
    sb = [s[8 * k:8 * k + 8] for k in range(nb)]
    mb = [m[8 * k:8 * k + 8] for k in range(nb)]
    sub = lax.broadcasted_iota(jnp.int32, (8, wide), 0)
    full = lambda x: jnp.broadcast_to(x, (8, wide))
    worst = None
    for k in range(nb):
        p = 8 * k
        norm0 = jnp.sum(m[8 * k:8 * k + 8] * m[8 * k:8 * k + 8], axis=1, keepdims=True)
        rs = [full(sb[k][i:i + 1]) for i in range(8)]
        rm = [full(mb[k][i:i + 1]) for i in range(8)]
        e = [[full(rs[i][:, p + j:p + j + 1]) for j in range(i + 1)] for i in range(8)]
        cols = [[full(sb[t][:, p + j:p + j + 1]) for j in range(8)] for t in range(k + 1, nb)]
        inv, low = [], [[None] * 8 for _ in range(8)]
        for j in range(8):
            inv.append(1.0 / e[j][j])
            for i in range(j + 1, 8):
                for t in range(j + 1, i + 1):
                    e[i][t] = e[i][t] - (e[i][j] * e[t][j]) * inv[j]
            for i in range(j + 1, 8):
                low[i][j] = e[i][j] * inv[j]
            for i in range(j + 1, 8):
                rs[i] = rs[i] - low[i][j] * rs[j]
                rm[i] = rm[i] - low[i][j] * rm[j]
        d = e[0][0]
        out = rm[0]
        for i in range(1, 8):
            d = jnp.where(sub == i, e[i][i], d)
            out = jnp.where(sub == i, rm[i], out)
        mb[k] = out * lax.rsqrt(d)
        ratio = d / norm0
        worst = ratio if worst is None else jnp.minimum(worst, ratio)
        if k == nb - 1:
            break
        us = [rs[j] * inv[j] for j in range(8)]
        um = [rm[j] * inv[j] for j in range(8)]
        for t in range(k + 1, nb):
            c = cols[t - k - 1]
            for j in range(8):
                for i in range(j + 1, 8):
                    c[i] = c[i] - low[i][j] * c[j]
                sb[t] = sb[t] - c[j] * us[j]
                mb[t] = mb[t] - c[j] * um[j]
    return jnp.concatenate(mb, 0), jnp.min(worst)


def repeated(m, q_ref):
    q, worst = orthonormal(m)
    q_ref[...] = q

    @pl.when(jnp.logical_not(worst >= REPEAT_BELOW))
    def _():
        q_ref[...] = orthonormal(q_ref[...])[0]


def start_basis(basis_t):
    v = pl.BlockSpec(memory_space=pltpu.VMEM)

    def kernel(b_ref, q_ref):
        repeated(b_ref[...], q_ref)

    return pl.pallas_call(
        kernel, out_shape=jax.ShapeDtypeStruct(basis_t.shape, F32), in_specs=[v], out_specs=v,
        cost_estimate=pl.CostEstimate(flops=1 << 30, bytes_accessed=1 << 20, transcendentals=0),
    )(basis_t)


def weigh(iters, g_ref, b_ref, q_ref):
    snaps = g_ref.shape[0]
    rows_in = lax.broadcasted_iota(jnp.int32, (snaps, snaps), 0)
    cols_in = lax.broadcasted_iota(jnp.int32, (snaps, snaps), 1)
    g = g_ref[...]
    low = (rows_in >= snaps - 2) & (cols_in < rows_in)
    g = jnp.where(low | (rows_in == cols_in) | ((rows_in < snaps - 2) & (cols_in < snaps - 2)), g, 0.0)
    g_ref[...] = g + jnp.where(low, g, 0.0).T
    q_ref[...] = b_ref[...]

    def iterate(i, _):
        repeated(jnp.dot(q_ref[...], g_ref[...], precision=HIGHEST, preferred_element_type=F32), q_ref)
        return 0

    lax.fori_loop(0, iters, iterate, 0)
    q = q_ref[...]
    last = (lax.broadcasted_iota(jnp.int32, (1, snaps), 1) == snaps - 1).astype(F32)
    w = jnp.zeros((1, snaps), F32)
    for _ in range(3):
        y = jnp.sum(q * (last - w), axis=1, keepdims=True)
        w = w + jnp.sum(q * y, axis=0, keepdims=True)
    return w


def filtered_field(gram, basis_t, hist, first, second):
    comps, snaps_old, count, part = hist.shape
    v = pl.BlockSpec(memory_space=pltpu.VMEM)

    def kernel(gram_ref, b_ref, hist_any, first_ref, second_ref, out_ref, g_ref, q_ref, hist_ref, flat, table, sem):
        copy = pltpu.make_async_copy(hist_any, hist_ref, sem)
        copy.start()
        g_ref[...] = gram_ref[...]
        w = weigh(POD_ITERS, g_ref, b_ref, q_ref)
        table[...] = jnp.broadcast_to(w, table.shape).T
        copy.wait()
        start = []
        for k, (ref, skip) in enumerate(((first_ref, 1), (second_ref, 0))):
            wk = table[snaps_old + k:snaps_old + k + 1]
            new = [wk * x for x in load_new(ref, skip, count, flat)]
            start = [x + y for x, y in zip(start, new)] if start else new

        def one(s, total):
            wk = table[pl.ds(s, 1), :]
            return [total[c] + wk * hist_ref[c, s].astype(F32) for c in range(comps)]
        total = lax.fori_loop(0, snaps_old, one, start, unroll=max(u for u in range(1, 10) if snaps_old % u == 0))
        for c in range(comps):
            out_ref[pl.ds(c, count, stride=comps), :] = total[c]

    return pl.pallas_call(
        kernel, out_shape=jax.ShapeDtypeStruct((count * comps, part), F32),
        in_specs=[v, v, pl.BlockSpec(memory_space=pl.ANY), v, v], out_specs=v,
        scratch_shapes=[pltpu.VMEM(gram.shape, F32), pltpu.VMEM(basis_t.shape, F32), pltpu.VMEM(hist.shape, BF16),
                        pltpu.VMEM((count * 8, part), F32), pltpu.VMEM(gram.shape, F32), pltpu.SemaphoreType.DMA],
        compiler_params=pltpu.CompilerParams(vmem_limit_bytes=48 << 20),
    )(gram, basis_t, hist, first, second)


def shift(x, axis, by):
    count = lax.axis_size(axis)
    return lax.ppermute(x, axis, [(i, (i + by) % count) for i in range(count)])


def exchange(x, axis, bits):
    count = lax.axis_size(axis)
    masks = [0]
    for bit in bits:
        masks = masks + [m ^ bit for m in masks]
    total = x
    for m in masks[1:]:
        total = total + lax.ppermute(x, axis, [(i, i ^ m) for i in range(count)])
    return total


def reduce_all(x):
    for axis, together in (("vert", 1), ("stream", 2)):
        count = lax.axis_size(axis)
        if count & (count - 1):
            x = lax.psum(x, axis)
            continue
        bits = [1 << k for k in range(count.bit_length() - 1)]
        for k in range(0, len(bits), together):
            x = exchange(x, axis, bits[k:k + together])
    return x


def body(particles, phase_flags, neighbours, history, basis_start):
    count = particles.shape[0]
    codes = neighbours[:, 0].T
    width = codes.shape[0]
    hist = history[:, 0].transpose(1, 2, 0, 3)
    s, v = lax.axis_index("stream"), lax.axis_index("vert")
    ns, nv = lax.axis_size("stream"), lax.axis_size("vert")
    one = jnp.ones((), jnp.int32)
    common = [v > 0, one, v < nv - 1, s > 0, s < ns - 1]
    edges1 = jnp.stack(common + [2 * one, 0 * one, one]).astype(jnp.int32)
    edges2 = jnp.stack(common + [one, one, one]).astype(jnp.int32)
    state, lo, hi = prepare(particles[:, 0], phase_flags[:, 0], codes)
    from_low = shift(hi, "stream", 1)
    from_high = shift(lo, "stream", -1)
    mid = jnp.concatenate([from_low[0:2], state, from_high[0:2]], axis=0)
    wide_codes = jnp.concatenate(
        [from_low[2, 0:width, 0:1].astype(jnp.int32), codes, from_high[2, 0:width, 0:1].astype(jnp.int32)], axis=1)
    basis = start_basis(basis_start.T)
    first = first_step(wide_codes, edges1, shift(mid, "vert", 1), mid, shift(mid, "vert", -1), basis)
    low, high = shift(first, "vert", 1), shift(first, "vert", -1)
    gram = early_gram(hist, first)
    new_state, second, gram = second_step(wide_codes, edges2, low, first, high, hist, gram)
    gram = reduce_all(gram)
    out = filtered_field(gram, basis, hist, first, second)
    return (new_state.reshape(count, 1, 7, -1), out.reshape(count, 1, 3, -1))


def solution(mesh):
    in_specs = (
        P("stream", "vert", None, None),
        P("stream", "vert", None),
        P("stream", "vert", None),
        P("stream", "vert", None, None, None),
        P(),
    )
    out_specs = (P("stream", "vert", None, None), P("stream", "vert", None, None))
    return jax.shard_map(body, mesh=mesh, in_specs=in_specs, out_specs=out_specs, check_vma=False)
```

```python
import functools
import math

import jax
import jax.numpy as jnp
from jax import lax
from jax.experimental import pallas as pl
from jax.experimental.pallas import tpu as pltpu
from jax.sharding import PartitionSpec as P

POD_ITERS = 4
VMEM_LIMIT = 20 << 20
SEDIMENT_EXTRA = 1.65


ALPHA_KERNEL = 21.0 / (16.0 * math.pi)
VOLUME = 1.0 / 16.0
STIFFNESS = 100.0 / 7.0
TIME_STEP = 0.02
GRAVITY = 1.0
F32, BF16 = jnp.float32, jnp.bfloat16

def pieces(x):
    a = x.astype(BF16).astype(F32)
    r = x - a
    b = r.astype(BF16).astype(F32)
    return a, b, r - b

def rows(*parts):
    return jnp.concatenate(parts, axis=0)

def row_is(*which):
    index = lax.broadcasted_iota(jnp.int32, (8, 128), 0)
    hit = index == which[0]
    for w in which[1:]:
        hit = hit | (index == w)
    return hit

def spread(row):
    return jnp.broadcast_to(row, (8, row.shape[1]))

def features(state):
    centred = jnp.where(row_is(0, 1, 2), state - 1.0, state)
    r, rho = spread(state[6:7]), spread(state[7:8])
    live = rho > 0.0
    mass = rho * VOLUME
    r2 = r * r
    pressure = jnp.where(live, STIFFNESS * (r2 * r2 * r2 * r - 1.0) / (jnp.where(live, rho, 1.0) * r2), 0.0)
    mp = mass * pressure
    place = jnp.where(row_is(0, 1, 2), centred, 0.0)
    norm = 0.25 * jnp.sum(place * place, axis=0, keepdims=True)
    speed = jnp.where(row_is(0, 1, 2), pltpu.roll(centred, 5, 0), 0.0)
    flux = jnp.sum(place * speed, axis=0, keepdims=True)
    own = jnp.where(row_is(3), norm, jnp.where(row_is(4), 1.0, place))
    near = jnp.where(row_is(3), 1.0, jnp.where(row_is(4), norm, -0.5 * place))
    moved = jnp.where(row_is(0), 1.0, jnp.where(row_is(7), flux, pltpu.roll(centred, 1, 0)))
    sums_a = mass * moved
    sums_b = jnp.where(row_is(0, 1, 2, 3), mp * moved, 0.0)
    near_x = jnp.where(row_is(0), -0.5, jnp.where(row_is(4), 0.5 * centred[0:1], 0.0))
    near_z = jnp.where(row_is(2), -0.5, jnp.where(row_is(4), 0.5 * centred[2:3], 0.0))
    sums_ax = mass * jnp.where(row_is(1), 1.0, jnp.where(row_is(7), centred[3:4], 0.0))
    sums_az = mass * jnp.where(row_is(3), 1.0, jnp.where(row_is(7), centred[5:6], 0.0))
    sums_bx = jnp.where(row_is(1), mp, 0.0)
    sums_bz = jnp.where(row_is(3), mp, 0.0)
    return own, rows(near, sums_a, sums_b), rows(near_x, sums_ax, sums_bx), rows(near_z, sums_az, sums_bz), pressure[0:1]

def prep_kernel(particles_ref, flags_ref, codes_ref, state_ref, lo_ref, hi_ref, flat):
    count = flags_ref.shape[0]
    fields = particles_ref.shape[0] // count
    for i in range(fields):
        flat[pl.ds(i, count, stride=8), :] = particles_ref[pl.ds(i, count, stride=fields), :]
    flat[pl.ds(fields, count, stride=8), :] = 1.0 + SEDIMENT_EXTRA * flags_ref[...].astype(F32)
    for b in range(count):
        state_ref[b] = flat[8 * b:8 * b + 8]
    for ref, first, edge in ((lo_ref, 0, 0), (hi_ref, count - 2, count - 1)):
        for i in range(2):
            ref[i] = flat[8 * (first + i):8 * (first + i) + 8]
        ref[2] = jnp.zeros_like(ref[2])
        ref[2, 0:codes_ref.shape[0], 0:1] = codes_ref[:, edge:edge + 1].astype(F32)


def prepare(particles, flags, codes):
    count, fields, part = particles.shape
    v = pl.BlockSpec(memory_space=pltpu.VMEM)
    rim = jax.ShapeDtypeStruct((3, 8, part), F32)
    return pl.pallas_call(
        prep_kernel,
        out_shape=(jax.ShapeDtypeStruct((count, 8, part), F32), rim, rim),
        in_specs=[v, v, v], out_specs=(v, v, v),
        scratch_shapes=[pltpu.VMEM((count * 8, part), F32)],
    )(particles.reshape(count * fields, part), flags, codes)


def step_blocks(codes_ref, edge_ref, low_ref, mid_ref, high_ref, out_ref, b0, b1, b2):
    ext = mid_ref.shape[0]
    count = ext - 2
    sel = lax.broadcasted_iota(jnp.int32, (8, 1), 0) == 7
    rim = edge_ref[5]
    for col, ref in ((0, low_ref), (1, mid_ref), (2, high_ref)):
        def prep(i, _):
            st = ref[i]
            rowon = jnp.where(i < rim, edge_ref[3], jnp.where(i >= ext - rim, edge_ref[4], 1))
            keep = (edge_ref[col] * rowon).astype(F32)
            _, a, b, c, _ = features(jnp.where(sel, st * keep, st))
            b0[col * ext + i] = a
            b1[col * ext + i] = b
            b2[col * ext + i] = c
            return 0
        lax.fori_loop(0, ext, prep, 0, unroll=2 if ext % 2 == 0 else 1)
    normrow = (lax.broadcasted_iota(jnp.int32, (24, 1), 0) == 4).astype(F32)
    skip = edge_ref[6]

    def block(b, _):
        st = mid_ref[b + 1]
        own, g_self, _, _, pressure = features(st)
        o1, o2, o3 = pieces(own)
        rhs = rows(o1, o1, o2, o2, o1, o3).astype(BF16)
        ns, fs = [], []
        for n in range(codes_ref.shape[0] + 1):
            if n == 0:
                g = g_self
            else:
                c = codes_ref[n - 1, b + skip]
                o = c + jnp.where(c >= 4, 1, 0)
                ds1 = (o * 11) >> 5
                dv1 = o - 3 * ds1
                idx = dv1 * ext + b + ds1
                tx = 2.0 * (ds1 - 1).astype(F32)
                tz = 2.0 * (dv1 - 1).astype(F32)
                g = b0[idx] + tx * b1[idx] + tz * b2[idx] + normrow * (0.25 * (tx * tx + tz * tz))
            p1, p2, p3 = pieces(g[0:8])
            f1, f2, f3 = pieces(g[8:24])
            ns.append(rows(p1, p2, p1, p2, p3, p1).astype(BF16))
            fs.append(rows(f1, f2, f3).astype(BF16))
        nall = jnp.concatenate(ns, axis=1)
        f = jnp.concatenate(fs + fs, axis=1)
        s = lax.dot_general(nall, rhs, (((0,), (0,)), ((), ())), preferred_element_type=F32)
        s = jnp.maximum(s, 1e-20)
        k = jnp.maximum(1.0 - s * lax.rsqrt(s), 0.0)
        wgt = k * k * k
        wh = wgt.astype(BF16)
        wl = (wgt - wh.astype(F32)).astype(BF16)
        acc = jnp.dot(f, jnp.concatenate([wh, wl], 0), preferred_element_type=F32)
        t = acc[0:16] + acc[16:32] + acc[32:48]
        x, vel = st[0:3] - 1.0, st[3:6]
        coef = -5.0 * ALPHA_KERNEL
        sw, swx, swv, swf = t[0:1], t[1:4], t[4:7], t[7:8]
        swp, swpx = t[8:9], t[9:12]
        dens = coef * (jnp.sum(vel * (x * sw - swx) - x * swv, axis=0, keepdims=True) + swf)
        acc3 = -coef * (pressure * (x * sw - swx) + x * swp - swpx)
        grav = jnp.where(lax.broadcasted_iota(jnp.int32, (3, 1), 0) == 2, -GRAVITY, 0.0)
        vel2 = vel + TIME_STEP * (acc3 + grav)
        pos2 = st[0:3] + TIME_STEP * vel2
        rho = st[7:8]
        r2 = st[6:7] + TIME_STEP * dens / rho
        out_ref[b] = rows(pos2, vel2, r2, rho)
        return 0
    unroll = max(u for u in range(1, 18) if count % u == 0)
    lax.fori_loop(0, count, block, 0, unroll=unroll)


def step_scratch(ext, part):
    return [pltpu.VMEM((3 * ext, 24, part), F32)] * 3


def first_step(codes, edges, low, mid, high):
    ext, _, part = mid.shape
    v = pl.BlockSpec(memory_space=pltpu.VMEM)
    sm = pl.BlockSpec(memory_space=pltpu.SMEM)
    return pl.pallas_call(
        step_blocks, out_shape=jax.ShapeDtypeStruct((ext - 2, 8, part), F32),
        in_specs=[sm, sm, v, v, v], out_specs=v,
        scratch_shapes=step_scratch(ext, part),
        compiler_params=pltpu.CompilerParams(vmem_limit_bytes=VMEM_LIMIT),
    )(codes, edges, low, mid, high)


def cross_row(hist_ref, new, others, terms):
    comps, hist = hist_ref.shape[0], hist_ref.shape[1]
    groups = new[0].shape[0] // 8

    def fold(x):
        total = x[0:8]
        for g in range(1, groups):
            total = total + x[8 * g:8 * g + 8]
        return total

    def one(s, _):
        total = hist_ref[0, s].astype(F32) * new[0]
        for c in range(1, comps):
            total = total + hist_ref[c, s].astype(F32) * new[c]
        terms[pl.ds(pl.multiple_of(8 * s, 8), 8), :] = fold(total)
        return 0
    lax.fori_loop(0, hist, one, 0, unroll=max(u for u in range(1, 10) if hist % u == 0))
    snaps = terms.shape[0] // 8
    for k in range(snaps - hist):
        if k < len(others):
            total = others[k][0] * new[0]
            for c in range(1, comps):
                total = total + others[k][c] * new[c]
            terms[8 * (hist + k):8 * (hist + k) + 8] = fold(total)
        else:
            terms[8 * (hist + k):8 * (hist + k) + 8] = jnp.zeros_like(terms[0:8])
    by_snap = terms[pl.ds(0, snaps, stride=8), :]
    for i in range(1, 8):
        by_snap = by_snap + terms[pl.ds(i, snaps, stride=8), :]
    ones = jnp.ones((8, by_snap.shape[1]), F32)
    return lax.dot_general(ones, by_snap, (((1,), (1,)), ((), ())), precision=HIGHEST, preferred_element_type=F32)[0:1]


def load_new(ref, skip, count, flat):
    def move(b, _):
        flat[pl.ds(pl.multiple_of(8 * b, 8), 8), :] = ref[b + skip]
        return 0
    lax.fori_loop(0, count, move, 0, unroll=math.gcd(count, 8))
    return [flat[pl.ds(3 + c, count, stride=8), :].astype(BF16).astype(F32) for c in range(3)]


def second_step(codes, edges, low, mid, high, hist, gram):
    ext, _, part = mid.shape
    count = ext - 2
    snaps = gram.shape[0]
    v = pl.BlockSpec(memory_space=pltpu.VMEM)
    sm = pl.BlockSpec(memory_space=pltpu.SMEM)

    def kernel(codes_ref, edge_ref, low_ref, mid_ref, high_ref, hist_ref, gram_ref, new_ref, state_ref, gram_out,
               b0, b1, b2, flat, terms):
        step_blocks(codes_ref, edge_ref, low_ref, mid_ref, high_ref, state_ref, b0, b1, b2)
        first = load_new(mid_ref, 1, count, flat)
        second = load_new(state_ref, 0, count, flat)
        for i in range(7):
            new_ref[pl.ds(i, count, stride=7), :] = flat[pl.ds(i, count, stride=8), :]
        row = cross_row(hist_ref, second, (first, second), terms)
        last = lax.broadcasted_iota(jnp.int32, (snaps, 1), 0) == snaps - 1
        gram_out[...] = jnp.where(last, row, gram_ref[...])

    return pl.pallas_call(
        kernel,
        out_shape=(jax.ShapeDtypeStruct((count * 7, part), F32), jax.ShapeDtypeStruct((count, 8, part), F32),
                   jax.ShapeDtypeStruct((snaps, snaps), F32)),
        in_specs=[sm, sm, v, v, v, v, v], out_specs=(v, v, v),
        scratch_shapes=step_scratch(ext, part) + [
            pltpu.VMEM((count * 8, part), F32), pltpu.VMEM((snaps * 8, part), F32)],
        compiler_params=pltpu.CompilerParams(vmem_limit_bytes=VMEM_LIMIT),
    )(codes, edges, low, mid, high, hist, gram)


def early_gram(hist, first):
    comps, snaps_old, count, part = hist.shape
    snaps = snaps_old + 2
    pitch = count + 8
    v = pl.BlockSpec(memory_space=pltpu.VMEM)

    def kernel(hist_ref, first_ref, out_ref, wide, flat, terms):
        total = jnp.zeros((snaps_old, snaps_old), F32)
        for c in range(comps):
            def expand(s, _):
                wide[pl.ds(pl.multiple_of(pitch * s, 8), count), :] = hist_ref[c, s].astype(F32)
                return 0
            lax.fori_loop(0, snaps_old, expand, 0, unroll=max(u for u in range(1, 10) if snaps_old % u == 0))
            for b in range(0, count, 8):
                x = jnp.concatenate([wide[pl.ds(b + j, snaps_old, stride=pitch), :].astype(BF16) for j in range(8)], axis=1)
                total = total + lax.dot_general(x, x, (((1,), (1,)), ((), ())), preferred_element_type=F32)
        out_ref[...] = jnp.zeros_like(out_ref)
        out_ref[0:snaps_old, 0:snaps_old] = total
        new = load_new(first_ref, 1, count, flat)
        out_ref[snaps_old:snaps_old + 1] = cross_row(hist_ref, new, (new,), terms)

    return pl.pallas_call(
        kernel, out_shape=jax.ShapeDtypeStruct((snaps, snaps), F32),
        in_specs=[v, v], out_specs=v,
        scratch_shapes=[pltpu.VMEM((snaps_old * pitch, part), F32), pltpu.VMEM((count * 8, part), F32),
                        pltpu.VMEM((snaps * 8, part), F32)],
        compiler_params=pltpu.CompilerParams(vmem_limit_bytes=VMEM_LIMIT),
        cost_estimate=pl.CostEstimate(flops=2 * comps * snaps * snaps * count * part, bytes_accessed=2 * comps * snaps * count * part, transcendentals=0),
    )(hist, first)


HIGHEST = lax.Precision.HIGHEST
REPEAT_BELOW = 1e-5


def gram_of(m):
    return lax.dot_general(m, m, (((1,), (1,)), ((), ())), precision=HIGHEST, preferred_element_type=F32)


def orthonormal(m):
    n, wide = m.shape
    nb = n // 8
    s = gram_of(m)
    s = jnp.concatenate([s, jnp.zeros((n, wide - n), F32)], axis=1)
    sb = [s[8 * k:8 * k + 8] for k in range(nb)]
    mb = [m[8 * k:8 * k + 8] for k in range(nb)]
    sub = lax.broadcasted_iota(jnp.int32, (8, wide), 0)
    full = lambda x: jnp.broadcast_to(x, (8, wide))
    worst = None
    for k in range(nb):
        p = 8 * k
        norm0 = jnp.sum(m[8 * k:8 * k + 8] * m[8 * k:8 * k + 8], axis=1, keepdims=True)
        rs = [full(sb[k][i:i + 1]) for i in range(8)]
        rm = [full(mb[k][i:i + 1]) for i in range(8)]
        e = [[full(rs[i][:, p + j:p + j + 1]) for j in range(i + 1)] for i in range(8)]
        cols = [[full(sb[t][:, p + j:p + j + 1]) for j in range(8)] for t in range(k + 1, nb)]
        inv, low = [], [[None] * 8 for _ in range(8)]
        for j in range(8):
            inv.append(1.0 / e[j][j])
            for i in range(j + 1, 8):
                for t in range(j + 1, i + 1):
                    e[i][t] = e[i][t] - (e[i][j] * e[t][j]) * inv[j]
            for i in range(j + 1, 8):
                low[i][j] = e[i][j] * inv[j]
            for i in range(j + 1, 8):
                rs[i] = rs[i] - low[i][j] * rs[j]
                rm[i] = rm[i] - low[i][j] * rm[j]
        d = e[0][0]
        out = rm[0]
        for i in range(1, 8):
            d = jnp.where(sub == i, e[i][i], d)
            out = jnp.where(sub == i, rm[i], out)
        mb[k] = out * lax.rsqrt(d)
        ratio = d / norm0
        worst = ratio if worst is None else jnp.minimum(worst, ratio)
        if k == nb - 1:
            break
        us = [rs[j] * inv[j] for j in range(8)]
        um = [rm[j] * inv[j] for j in range(8)]
        for t in range(k + 1, nb):
            c = cols[t - k - 1]
            for j in range(8):
                for i in range(j + 1, 8):
                    c[i] = c[i] - low[i][j] * c[j]
                sb[t] = sb[t] - c[j] * us[j]
                mb[t] = mb[t] - c[j] * um[j]
    return jnp.concatenate(mb, 0), jnp.min(worst)


def repeated(m, q_ref):
    q, worst = orthonormal(m)
    q_ref[...] = q

    @pl.when(jnp.logical_not(worst >= REPEAT_BELOW))
    def _():
        q_ref[...] = orthonormal(q_ref[...])[0]


def start_basis(basis_t):
    v = pl.BlockSpec(memory_space=pltpu.VMEM)

    def kernel(b_ref, q_ref):
        repeated(b_ref[...], q_ref)

    return pl.pallas_call(
        kernel, out_shape=jax.ShapeDtypeStruct(basis_t.shape, F32), in_specs=[v], out_specs=v,
        cost_estimate=pl.CostEstimate(flops=1 << 30, bytes_accessed=1 << 20, transcendentals=0),
    )(basis_t)


def weigh(iters, g_ref, b_ref, q_ref):
    snaps = g_ref.shape[0]
    rows_in = lax.broadcasted_iota(jnp.int32, (snaps, snaps), 0)
    cols_in = lax.broadcasted_iota(jnp.int32, (snaps, snaps), 1)
    g = g_ref[...]
    low = (rows_in >= snaps - 2) & (cols_in < rows_in)
    g = jnp.where(low | (rows_in == cols_in) | ((rows_in < snaps - 2) & (cols_in < snaps - 2)), g, 0.0)
    g_ref[...] = g + jnp.where(low, g, 0.0).T
    q_ref[...] = b_ref[...]

    def iterate(i, _):
        repeated(jnp.dot(q_ref[...], g_ref[...], precision=HIGHEST, preferred_element_type=F32), q_ref)
        return 0

    lax.fori_loop(0, iters, iterate, 0)
    q = q_ref[...]
    last = (lax.broadcasted_iota(jnp.int32, (1, snaps), 1) == snaps - 1).astype(F32)
    w = jnp.zeros((1, snaps), F32)
    for _ in range(3):
        y = jnp.sum(q * (last - w), axis=1, keepdims=True)
        w = w + jnp.sum(q * y, axis=0, keepdims=True)
    return w


def filtered_field(gram, basis_t, hist, first, second):
    comps, snaps_old, count, part = hist.shape
    v = pl.BlockSpec(memory_space=pltpu.VMEM)

    def kernel(gram_ref, b_ref, hist_ref, first_ref, second_ref, out_ref, g_ref, q_ref, flat, table):
        g_ref[...] = gram_ref[...]
        w = weigh(POD_ITERS, g_ref, b_ref, q_ref)
        table[...] = jnp.broadcast_to(w, table.shape).T
        start = []
        for k, (ref, skip) in enumerate(((first_ref, 1), (second_ref, 0))):
            wk = table[snaps_old + k:snaps_old + k + 1]
            new = [wk * x for x in load_new(ref, skip, count, flat)]
            start = [x + y for x, y in zip(start, new)] if start else new

        def one(s, total):
            wk = table[pl.ds(s, 1), :]
            return [total[c] + wk * hist_ref[c, s].astype(F32) for c in range(comps)]
        total = lax.fori_loop(0, snaps_old, one, start, unroll=max(u for u in range(1, 10) if snaps_old % u == 0))
        for c in range(comps):
            out_ref[pl.ds(c, count, stride=comps), :] = total[c]

    return pl.pallas_call(
        kernel, out_shape=jax.ShapeDtypeStruct((count * comps, part), F32),
        in_specs=[v, v, v, v, v], out_specs=v,
        scratch_shapes=[pltpu.VMEM(gram.shape, F32), pltpu.VMEM(basis_t.shape, F32),
                        pltpu.VMEM((count * 8, part), F32), pltpu.VMEM(gram.shape, F32)],
        compiler_params=pltpu.CompilerParams(vmem_limit_bytes=VMEM_LIMIT),
    )(gram, basis_t, hist, first, second)


def shift(x, axis, by):
    count = lax.axis_size(axis)
    return lax.ppermute(x, axis, [(i, (i + by) % count) for i in range(count)])


def exchange(x, axis, bits):
    count = lax.axis_size(axis)
    masks = [0]
    for bit in bits:
        masks = masks + [m ^ bit for m in masks]
    total = x
    for m in masks[1:]:
        total = total + lax.ppermute(x, axis, [(i, i ^ m) for i in range(count)])
    return total


def reduce_all(x):
    for axis, together in (("vert", 1), ("stream", 2)):
        count = lax.axis_size(axis)
        if count & (count - 1):
            x = lax.psum(x, axis)
            continue
        bits = [1 << k for k in range(count.bit_length() - 1)]
        for k in range(0, len(bits), together):
            x = exchange(x, axis, bits[k:k + together])
    return x


def body(particles, phase_flags, neighbours, history, basis_start):
    count = particles.shape[0]
    codes = neighbours[:, 0].T
    width = codes.shape[0]
    hist = history[:, 0].transpose(1, 2, 0, 3)
    s, v = lax.axis_index("stream"), lax.axis_index("vert")
    ns, nv = lax.axis_size("stream"), lax.axis_size("vert")
    one = jnp.ones((), jnp.int32)
    common = [v > 0, one, v < nv - 1, s > 0, s < ns - 1]
    edges1 = jnp.stack(common + [2 * one, 0 * one, one]).astype(jnp.int32)
    edges2 = jnp.stack(common + [one, one, one]).astype(jnp.int32)
    state, lo, hi = prepare(particles[:, 0], phase_flags[:, 0], codes)
    from_low = shift(hi, "stream", 1)
    from_high = shift(lo, "stream", -1)
    mid = jnp.concatenate([from_low[0:2], state, from_high[0:2]], axis=0)
    wide_codes = jnp.concatenate(
        [from_low[2, 0:width, 0:1].astype(jnp.int32), codes, from_high[2, 0:width, 0:1].astype(jnp.int32)], axis=1)
    low_mid, high_mid = shift(mid, "vert", 1), shift(mid, "vert", -1)
    basis = start_basis(basis_start.T)
    wide_codes, basis = lax.optimization_barrier((wide_codes, basis))
    first = first_step(wide_codes, edges1, low_mid, mid, high_mid)
    low, high = shift(first, "vert", 1), shift(first, "vert", -1)
    gram = early_gram(hist, first)
    new_state, second, gram = second_step(wide_codes, edges2, low, first, high, hist, gram)
    gram = reduce_all(gram)
    out = filtered_field(gram, basis, hist, first, second)
    return (new_state.reshape(count, 1, 7, -1), out.reshape(count, 1, 3, -1))


def solution(mesh):
    in_specs = (
        P("stream", "vert", None, None),
        P("stream", "vert", None),
        P("stream", "vert", None),
        P("stream", "vert", None, None, None),
        P(),
    )
    out_specs = (P("stream", "vert", None, None), P("stream", "vert", None, None))
    return jax.shard_map(body, mesh=mesh, in_specs=in_specs, out_specs=out_specs, check_vma=False)
```

```python
import functools
import math

import jax
import jax.numpy as jnp
from jax import lax
from jax.experimental import pallas as pl
from jax.experimental.pallas import tpu as pltpu
from jax.sharding import PartitionSpec as P

POD_ITERS = 4
VMEM_LIMIT = 20 << 20
SEDIMENT_EXTRA = 1.65


ALPHA_KERNEL = 21.0 / (16.0 * math.pi)
VOLUME = 1.0 / 16.0
STIFFNESS = 100.0 / 7.0
TIME_STEP = 0.02
GRAVITY = 1.0
F32, BF16 = jnp.float32, jnp.bfloat16

def pieces(x):
    a = x.astype(BF16).astype(F32)
    r = x - a
    b = r.astype(BF16).astype(F32)
    return a, b, r - b

def rows(*parts):
    return jnp.concatenate(parts, axis=0)

def row_is(*which):
    index = lax.broadcasted_iota(jnp.int32, (8, 128), 0)
    hit = index == which[0]
    for w in which[1:]:
        hit = hit | (index == w)
    return hit

def spread(row):
    return jnp.broadcast_to(row, (8, row.shape[1]))

def features(state):
    centred = jnp.where(row_is(0, 1, 2), state - 1.0, state)
    r, rho = spread(state[6:7]), spread(state[7:8])
    live = rho > 0.0
    mass = rho * VOLUME
    r2 = r * r
    pressure = jnp.where(live, STIFFNESS * (r2 * r2 * r2 * r - 1.0) / (jnp.where(live, rho, 1.0) * r2), 0.0)
    mp = mass * pressure
    place = jnp.where(row_is(0, 1, 2), centred, 0.0)
    norm = 0.25 * jnp.sum(place * place, axis=0, keepdims=True)
    speed = jnp.where(row_is(0, 1, 2), pltpu.roll(centred, 5, 0), 0.0)
    flux = jnp.sum(place * speed, axis=0, keepdims=True)
    own = jnp.where(row_is(3), norm, jnp.where(row_is(4), 1.0, place))
    near = jnp.where(row_is(3), 1.0, jnp.where(row_is(4), norm, -0.5 * place))
    moved = jnp.where(row_is(0), 1.0, jnp.where(row_is(7), flux, pltpu.roll(centred, 1, 0)))
    sums_a = mass * moved
    sums_b = jnp.where(row_is(0, 1, 2, 3), mp * moved, 0.0)
    near_x = jnp.where(row_is(0), -0.5, jnp.where(row_is(4), 0.5 * centred[0:1], 0.0))
    near_z = jnp.where(row_is(2), -0.5, jnp.where(row_is(4), 0.5 * centred[2:3], 0.0))
    sums_ax = mass * jnp.where(row_is(1), 1.0, jnp.where(row_is(7), centred[3:4], 0.0))
    sums_az = mass * jnp.where(row_is(3), 1.0, jnp.where(row_is(7), centred[5:6], 0.0))
    sums_bx = jnp.where(row_is(1), mp, 0.0)
    sums_bz = jnp.where(row_is(3), mp, 0.0)
    return own, rows(near, sums_a, sums_b), rows(near_x, sums_ax, sums_bx), rows(near_z, sums_az, sums_bz), pressure[0:1]

def prep_kernel(particles_ref, flags_ref, codes_ref, state_ref, lo_ref, hi_ref, flat):
    count = flags_ref.shape[0]
    fields = particles_ref.shape[0] // count
    for i in range(fields):
        flat[pl.ds(i, count, stride=8), :] = particles_ref[pl.ds(i, count, stride=fields), :]
    flat[pl.ds(fields, count, stride=8), :] = 1.0 + SEDIMENT_EXTRA * flags_ref[...].astype(F32)
    for b in range(count):
        state_ref[b] = flat[8 * b:8 * b + 8]
    for ref, first, edge in ((lo_ref, 0, 0), (hi_ref, count - 2, count - 1)):
        for i in range(2):
            ref[i] = flat[8 * (first + i):8 * (first + i) + 8]
        ref[2] = jnp.zeros_like(ref[2])
        ref[2, 0:codes_ref.shape[0], 0:1] = codes_ref[:, edge:edge + 1].astype(F32)


def prepare(particles, flags, codes):
    count, fields, part = particles.shape
    v = pl.BlockSpec(memory_space=pltpu.VMEM)
    rim = jax.ShapeDtypeStruct((3, 8, part), F32)
    return pl.pallas_call(
        prep_kernel,
        out_shape=(jax.ShapeDtypeStruct((count, 8, part), F32), rim, rim),
        in_specs=[v, v, v], out_specs=(v, v, v),
        scratch_shapes=[pltpu.VMEM((count * 8, part), F32)],
    )(particles.reshape(count * fields, part), flags, codes)


def step_blocks(codes_ref, edge_ref, low_ref, mid_ref, high_ref, out_ref, b0, b1, b2):
    ext = mid_ref.shape[0]
    count = ext - 2
    sel = lax.broadcasted_iota(jnp.int32, (8, 1), 0) == 7
    rim = edge_ref[5]

    def prep(i):
        rowon = jnp.where(i < rim, edge_ref[3], jnp.where(i >= ext - rim, edge_ref[4], 1))
        for col, ref in ((0, low_ref), (1, mid_ref), (2, high_ref)):
            st = ref[i]
            keep = (edge_ref[col] * rowon).astype(F32)
            _, a, b, c, _ = features(jnp.where(sel, st * keep, st))
            b0[col * ext + i] = a
            b1[col * ext + i] = b
            b2[col * ext + i] = c

    for i in range(3):
        prep(i)
    normrow = (lax.broadcasted_iota(jnp.int32, (24, 1), 0) == 4).astype(F32)
    skip = edge_ref[6]

    def operands(b):
        st = mid_ref[b + 1]
        own, g_self, _, _, pressure = features(st)
        o1, o2, o3 = pieces(own)
        rhs = rows(o1, o1, o2, o2, o1, o3).astype(BF16)
        gs = [g_self]
        for n in range(codes_ref.shape[0]):
            c = codes_ref[n, b + skip]
            o = c + jnp.where(c >= 4, 1, 0)
            ds1 = (o * 11) >> 5
            dv1 = o - 3 * ds1
            idx = dv1 * ext + b + ds1
            tx = 2.0 * (ds1 - 1).astype(F32)
            tz = 2.0 * (dv1 - 1).astype(F32)
            gs.append(b0[idx] + tx * b1[idx] + tz * b2[idx] + normrow * (0.25 * (tx * tx + tz * tz)))
        prep(jnp.minimum(b + 3, ext - 1))
        ns, fs = [], []
        for g in gs:
            p1, p2, p3 = pieces(g[0:8])
            f1 = g[8:24].astype(BF16)
            f2 = (g[8:24] - f1.astype(F32)).astype(BF16)
            ns.append(rows(p1, p2, p1, p2, p3, p1).astype(BF16))
            fs.append(rows(f1, f2))
        return st, pressure, rhs, jnp.concatenate(ns, axis=1), jnp.concatenate(fs + fs, axis=1)

    def finish(b, st, pressure, acc):
        t = acc[0:16] + acc[16:32]
        x, vel = st[0:3] - 1.0, st[3:6]
        coef = -5.0 * ALPHA_KERNEL
        sw, swx, swv, swf = t[0:1], t[1:4], t[4:7], t[7:8]
        swp, swpx = t[8:9], t[9:12]
        dens = coef * (jnp.sum(vel * (x * sw - swx) - x * swv, axis=0, keepdims=True) + swf)
        acc3 = -coef * (pressure * (x * sw - swx) + x * swp - swpx)
        grav = jnp.where(lax.broadcasted_iota(jnp.int32, (3, 1), 0) == 2, -GRAVITY, 0.0)
        vel2 = vel + TIME_STEP * (acc3 + grav)
        pos2 = st[0:3] + TIME_STEP * vel2
        rho = st[7:8]
        r2 = st[6:7] + TIME_STEP * dens / rho
        out_ref[b] = rows(pos2, vel2, r2, rho)

    def blocks(i, _):
        group = [operands(width * i + k) for k in range(width)]
        zero = jnp.zeros_like(group[0][2])
        rhs = rows(*[jnp.concatenate([g[2] if m == k else zero for m in range(width)], axis=1) for k, g in enumerate(group)])
        nall = rows(*[g[3] for g in group])
        s = lax.dot_general(nall, rhs, (((0,), (0,)), ((), ())), preferred_element_type=F32)
        s = jnp.maximum(s, 1e-20)
        k = jnp.maximum(1.0 - s * lax.rsqrt(s), 0.0)
        wgt = k * k * k
        wh = wgt.astype(BF16)
        wl = (wgt - wh.astype(F32)).astype(BF16)
        acc = jnp.dot(rows(*[g[4] for g in group]), rows(wh, wl), preferred_element_type=F32)
        high, part = acc.shape[0] // width, zero.shape[1]
        for k, g in enumerate(group):
            finish(width * i + k, g[0], g[1], acc[high * k:high * (k + 1), part * k:part * (k + 1)])
        return 0
    width = 2 if count % 2 == 0 else 1
    trips = count // width
    lax.fori_loop(0, trips, blocks, 0, unroll=max(u for u in range(1, 18) if trips % u == 0))


def step_scratch(ext, part):
    return [pltpu.VMEM((3 * ext, 24, part), F32)] * 3


def first_step(codes, edges, low, mid, high):
    ext, _, part = mid.shape
    v = pl.BlockSpec(memory_space=pltpu.VMEM)
    sm = pl.BlockSpec(memory_space=pltpu.SMEM)
    return pl.pallas_call(
        step_blocks, out_shape=jax.ShapeDtypeStruct((ext - 2, 8, part), F32),
        in_specs=[sm, sm, v, v, v], out_specs=v,
        scratch_shapes=step_scratch(ext, part),
        compiler_params=pltpu.CompilerParams(vmem_limit_bytes=VMEM_LIMIT),
    )(codes, edges, low, mid, high)


def cross_row(hist_ref, new, others, terms):
    comps, hist = hist_ref.shape[0], hist_ref.shape[1]
    groups = new[0].shape[0] // 8

    def fold(x):
        total = x[0:8]
        for g in range(1, groups):
            total = total + x[8 * g:8 * g + 8]
        return total

    def one(s, _):
        total = hist_ref[0, s].astype(F32) * new[0]
        for c in range(1, comps):
            total = total + hist_ref[c, s].astype(F32) * new[c]
        terms[pl.ds(pl.multiple_of(8 * s, 8), 8), :] = fold(total)
        return 0
    lax.fori_loop(0, hist, one, 0, unroll=max(u for u in range(1, 10) if hist % u == 0))
    snaps = terms.shape[0] // 8
    for k in range(snaps - hist):
        if k < len(others):
            total = others[k][0] * new[0]
            for c in range(1, comps):
                total = total + others[k][c] * new[c]
            terms[8 * (hist + k):8 * (hist + k) + 8] = fold(total)
        else:
            terms[8 * (hist + k):8 * (hist + k) + 8] = jnp.zeros_like(terms[0:8])
    by_snap = terms[pl.ds(0, snaps, stride=8), :]
    for i in range(1, 8):
        by_snap = by_snap + terms[pl.ds(i, snaps, stride=8), :]
    ones = jnp.ones((8, by_snap.shape[1]), F32)
    return lax.dot_general(ones, by_snap, (((1,), (1,)), ((), ())), precision=HIGHEST, preferred_element_type=F32)[0:1]


def load_new(ref, skip, count, flat):
    def move(b, _):
        flat[pl.ds(pl.multiple_of(8 * b, 8), 8), :] = ref[b + skip]
        return 0
    lax.fori_loop(0, count, move, 0, unroll=math.gcd(count, 8))
    return [flat[pl.ds(3 + c, count, stride=8), :].astype(BF16).astype(F32) for c in range(3)]


def second_step(codes, edges, low, mid, high, hist, gram):
    ext, _, part = mid.shape
    count = ext - 2
    snaps = gram.shape[0]
    v = pl.BlockSpec(memory_space=pltpu.VMEM)
    sm = pl.BlockSpec(memory_space=pltpu.SMEM)

    def kernel(codes_ref, edge_ref, low_ref, mid_ref, high_ref, hist_ref, gram_ref, new_ref, state_ref, gram_out,
               b0, b1, b2, flat, terms):
        step_blocks(codes_ref, edge_ref, low_ref, mid_ref, high_ref, state_ref, b0, b1, b2)
        first = load_new(mid_ref, 1, count, flat)
        second = load_new(state_ref, 0, count, flat)
        for i in range(7):
            new_ref[pl.ds(i, count, stride=7), :] = flat[pl.ds(i, count, stride=8), :]
        row = cross_row(hist_ref, second, (first, second), terms)
        last = lax.broadcasted_iota(jnp.int32, (snaps, 1), 0) == snaps - 1
        gram_out[...] = jnp.where(last, row, gram_ref[...])

    return pl.pallas_call(
        kernel,
        out_shape=(jax.ShapeDtypeStruct((count * 7, part), F32), jax.ShapeDtypeStruct((count, 8, part), F32),
                   jax.ShapeDtypeStruct((snaps, snaps), F32)),
        in_specs=[sm, sm, v, v, v, v, v], out_specs=(v, v, v),
        scratch_shapes=step_scratch(ext, part) + [
            pltpu.VMEM((count * 8, part), F32), pltpu.VMEM((snaps * 8, part), F32)],
        compiler_params=pltpu.CompilerParams(vmem_limit_bytes=VMEM_LIMIT),
    )(codes, edges, low, mid, high, hist, gram)


def early_gram(hist, first):
    comps, snaps_old, count, part = hist.shape
    snaps = snaps_old + 2
    pitch = count + 8
    v = pl.BlockSpec(memory_space=pltpu.VMEM)

    def kernel(hist_ref, first_ref, out_ref, wide, flat, terms):
        total = jnp.zeros((snaps_old, snaps_old), F32)
        for c in range(comps):
            def expand(s, _):
                wide[pl.ds(pl.multiple_of(pitch * s, 8), count), :] = hist_ref[c, s].astype(F32)
                return 0
            lax.fori_loop(0, snaps_old, expand, 0, unroll=max(u for u in range(1, 10) if snaps_old % u == 0))
            for b in range(0, count, 8):
                x = jnp.concatenate([wide[pl.ds(b + j, snaps_old, stride=pitch), :].astype(BF16) for j in range(8)], axis=1)
                total = total + lax.dot_general(x, x, (((1,), (1,)), ((), ())), preferred_element_type=F32)
        out_ref[...] = jnp.zeros_like(out_ref)
        out_ref[0:snaps_old, 0:snaps_old] = total
        new = load_new(first_ref, 1, count, flat)
        out_ref[snaps_old:snaps_old + 1] = cross_row(hist_ref, new, (new,), terms)

    return pl.pallas_call(
        kernel, out_shape=jax.ShapeDtypeStruct((snaps, snaps), F32),
        in_specs=[v, v], out_specs=v,
        scratch_shapes=[pltpu.VMEM((snaps_old * pitch, part), F32), pltpu.VMEM((count * 8, part), F32),
                        pltpu.VMEM((snaps * 8, part), F32)],
        compiler_params=pltpu.CompilerParams(vmem_limit_bytes=VMEM_LIMIT),
        cost_estimate=pl.CostEstimate(flops=2 * comps * snaps * snaps * count * part, bytes_accessed=2 * comps * snaps * count * part, transcendentals=0),
    )(hist, first)


HIGHEST = lax.Precision.HIGHEST
REPEAT_BELOW = 1e-5
JOIN_ABOVE = 1e-4


def gram_of(m):
    return lax.dot_general(m, m, (((1,), (1,)), ((), ())), precision=HIGHEST, preferred_element_type=F32)


def orthonormal(m):
    n, wide = m.shape
    nb = n // 8
    s = gram_of(m)
    s = jnp.concatenate([s, jnp.zeros((n, wide - n), F32)], axis=1)
    sb = [s[8 * k:8 * k + 8] for k in range(nb)]
    mb = [m[8 * k:8 * k + 8] for k in range(nb)]
    sub = lax.broadcasted_iota(jnp.int32, (8, wide), 0)
    full = lambda x: jnp.broadcast_to(x, (8, wide))
    worst = None
    for k in range(nb):
        p = 8 * k
        norm0 = jnp.sum(m[8 * k:8 * k + 8] * m[8 * k:8 * k + 8], axis=1, keepdims=True)
        rs = [full(sb[k][i:i + 1]) for i in range(8)]
        rm = [full(mb[k][i:i + 1]) for i in range(8)]
        e = [[full(rs[i][:, p + j:p + j + 1]) for j in range(i + 1)] for i in range(8)]
        cols = [[full(sb[t][:, p + j:p + j + 1]) for j in range(8)] for t in range(k + 1, nb)]
        inv, low = [], [[None] * 8 for _ in range(8)]
        for j in range(8):
            inv.append(1.0 / e[j][j])
            for i in range(j + 1, 8):
                for t in range(j + 1, i + 1):
                    e[i][t] = e[i][t] - (e[i][j] * e[t][j]) * inv[j]
            for i in range(j + 1, 8):
                low[i][j] = e[i][j] * inv[j]
            for i in range(j + 1, 8):
                rs[i] = rs[i] - low[i][j] * rs[j]
                rm[i] = rm[i] - low[i][j] * rm[j]
        d = e[0][0]
        out = rm[0]
        for i in range(1, 8):
            d = jnp.where(sub == i, e[i][i], d)
            out = jnp.where(sub == i, rm[i], out)
        mb[k] = out * lax.rsqrt(d)
        ratio = d / norm0
        worst = ratio if worst is None else jnp.minimum(worst, ratio)
        if k == nb - 1:
            break
        us = [rs[j] * inv[j] for j in range(8)]
        um = [rm[j] * inv[j] for j in range(8)]
        for t in range(k + 1, nb):
            c = cols[t - k - 1]
            for j in range(8):
                for i in range(j + 1, 8):
                    c[i] = c[i] - low[i][j] * c[j]
                sb[t] = sb[t] - c[j] * us[j]
                mb[t] = mb[t] - c[j] * um[j]
    return jnp.concatenate(mb, 0), jnp.min(worst)


def repeated(m, q_ref):
    q, worst = orthonormal(m)
    q_ref[...] = q

    @pl.when(jnp.logical_not(worst >= REPEAT_BELOW))
    def _():
        q_ref[...] = orthonormal(q_ref[...])[0]


def start_basis(basis_t):
    v = pl.BlockSpec(memory_space=pltpu.VMEM)

    def kernel(b_ref, q_ref):
        repeated(b_ref[...], q_ref)

    return pl.pallas_call(
        kernel, out_shape=jax.ShapeDtypeStruct(basis_t.shape, F32), in_specs=[v], out_specs=v,
        cost_estimate=pl.CostEstimate(flops=1 << 30, bytes_accessed=1 << 20, transcendentals=0),
    )(basis_t)


def weigh(iters, g_ref, b_ref, q_ref):
    snaps = g_ref.shape[0]
    rows_in = lax.broadcasted_iota(jnp.int32, (snaps, snaps), 0)
    cols_in = lax.broadcasted_iota(jnp.int32, (snaps, snaps), 1)
    g = g_ref[...]
    low = (rows_in >= snaps - 2) & (cols_in < rows_in)
    g = jnp.where(low | (rows_in == cols_in) | ((rows_in < snaps - 2) & (cols_in < snaps - 2)), g, 0.0)
    trace = jnp.sum(jnp.where(rows_in == cols_in, g, 0.0), axis=(0, 1), keepdims=True)
    g_ref[...] = (g + jnp.where(low, g, 0.0).T) * (1.0 / trace)
    q_ref[...] = b_ref[...]

    def product(q):
        return jnp.dot(q, g_ref[...], precision=HIGHEST, preferred_element_type=F32)

    def iterate(i, _):
        repeated(product(q_ref[...]), q_ref)
        return 0

    lax.fori_loop(0, iters - 2, iterate, 0)
    q, worst = orthonormal(product(product(q_ref[...])))
    good = worst >= JOIN_ABOVE

    @pl.when(jnp.logical_not(good))
    def _():
        lax.fori_loop(iters - 2, iters, iterate, 0)

    @pl.when(good)
    def _():
        q_ref[...] = q

    q = q_ref[...]
    last = (lax.broadcasted_iota(jnp.int32, (1, snaps), 1) == snaps - 1).astype(F32)
    w = jnp.zeros((1, snaps), F32)
    for _ in range(3):
        y = jnp.sum(q * (last - w), axis=1, keepdims=True)
        w = w + jnp.sum(q * y, axis=0, keepdims=True)
    return w


def filtered_field(gram, basis_t, hist, first, second):
    comps, snaps_old, count, part = hist.shape
    v = pl.BlockSpec(memory_space=pltpu.VMEM)

    def kernel(gram_ref, b_ref, hist_ref, first_ref, second_ref, out_ref, g_ref, q_ref, flat, table):
        g_ref[...] = gram_ref[...]
        w = weigh(POD_ITERS, g_ref, b_ref, q_ref)
        table[...] = jnp.broadcast_to(w, table.shape).T
        start = []
        for k, (ref, skip) in enumerate(((first_ref, 1), (second_ref, 0))):
            wk = table[snaps_old + k:snaps_old + k + 1]
            new = [wk * x for x in load_new(ref, skip, count, flat)]
            start = [x + y for x, y in zip(start, new)] if start else new

        def one(s, total):
            wk = table[pl.ds(s, 1), :]
            return [total[c] + wk * hist_ref[c, s].astype(F32) for c in range(comps)]
        total = lax.fori_loop(0, snaps_old, one, start, unroll=max(u for u in range(1, 10) if snaps_old % u == 0))
        for c in range(comps):
            out_ref[pl.ds(c, count, stride=comps), :] = total[c]

    return pl.pallas_call(
        kernel, out_shape=jax.ShapeDtypeStruct((count * comps, part), F32),
        in_specs=[v, v, v, v, v], out_specs=v,
        scratch_shapes=[pltpu.VMEM(gram.shape, F32), pltpu.VMEM(basis_t.shape, F32),
                        pltpu.VMEM((count * 8, part), F32), pltpu.VMEM(gram.shape, F32)],
        compiler_params=pltpu.CompilerParams(vmem_limit_bytes=VMEM_LIMIT),
    )(gram, basis_t, hist, first, second)


def shift(x, axis, by):
    count = lax.axis_size(axis)
    return lax.ppermute(x, axis, [(i, (i + by) % count) for i in range(count)])


def exchange(x, axis, bits):
    count = lax.axis_size(axis)
    masks = [0]
    for bit in bits:
        masks = masks + [m ^ bit for m in masks]
    total = x
    for m in masks[1:]:
        total = total + lax.ppermute(x, axis, [(i, i ^ m) for i in range(count)])
    return total


def reduce_all(x):
    for axis, together in (("vert", 1), ("stream", 2)):
        count = lax.axis_size(axis)
        if count & (count - 1):
            x = lax.psum(x, axis)
            continue
        bits = [1 << k for k in range(count.bit_length() - 1)]
        for k in range(0, len(bits), together):
            x = exchange(x, axis, bits[k:k + together])
    return x


def body(particles, phase_flags, neighbours, history, basis_start):
    count = particles.shape[0]
    codes = neighbours[:, 0].T
    width = codes.shape[0]
    hist = history[:, 0].transpose(1, 2, 0, 3)
    s, v = lax.axis_index("stream"), lax.axis_index("vert")
    ns, nv = lax.axis_size("stream"), lax.axis_size("vert")
    one = jnp.ones((), jnp.int32)
    common = [v > 0, one, v < nv - 1, s > 0, s < ns - 1]
    edges1 = jnp.stack(common + [2 * one, 0 * one, one]).astype(jnp.int32)
    edges2 = jnp.stack(common + [one, one, one]).astype(jnp.int32)
    state, lo, hi = prepare(particles[:, 0], phase_flags[:, 0], codes)
    from_low = shift(hi, "stream", 1)
    from_high = shift(lo, "stream", -1)
    mid = jnp.concatenate([from_low[0:2], state, from_high[0:2]], axis=0)
    wide_codes = jnp.concatenate(
        [from_low[2, 0:width, 0:1].astype(jnp.int32), codes, from_high[2, 0:width, 0:1].astype(jnp.int32)], axis=1)
    low_mid, high_mid = shift(mid, "vert", 1), shift(mid, "vert", -1)
    basis = start_basis(basis_start.T)
    wide_codes, basis = lax.optimization_barrier((wide_codes, basis))
    first = first_step(wide_codes, edges1, low_mid, mid, high_mid)
    low, high = shift(first, "vert", 1), shift(first, "vert", -1)
    gram = early_gram(hist, first)
    new_state, second, gram = second_step(wide_codes, edges2, low, first, high, hist, gram)
    gram = reduce_all(gram)
    out = filtered_field(gram, basis, hist, first, second)
    return (new_state.reshape(count, 1, 7, -1), out.reshape(count, 1, 3, -1))


def solution(mesh):
    in_specs = (
        P("stream", "vert", None, None),
        P("stream", "vert", None),
        P("stream", "vert", None),
        P("stream", "vert", None, None, None),
        P(),
    )
    out_specs = (P("stream", "vert", None, None), P("stream", "vert", None, None))
    return jax.shard_map(body, mesh=mesh, in_specs=in_specs, out_specs=out_specs, check_vma=False)
```

```python
import functools
import math

import jax
import jax.numpy as jnp
from jax import lax
from jax.experimental import pallas as pl
from jax.experimental.pallas import tpu as pltpu
from jax.sharding import PartitionSpec as P

POD_ITERS = 4
VMEM_LIMIT = 20 << 20
SEDIMENT_EXTRA = 1.65


ALPHA_KERNEL = 21.0 / (16.0 * math.pi)
VOLUME = 1.0 / 16.0
STIFFNESS = 100.0 / 7.0
TIME_STEP = 0.02
GRAVITY = 1.0
F32, BF16 = jnp.float32, jnp.bfloat16

def pieces(x):
    a = x.astype(BF16).astype(F32)
    r = x - a
    b = r.astype(BF16).astype(F32)
    return a, b, r - b

def rows(*parts):
    return jnp.concatenate(parts, axis=0)

def row_is(*which):
    index = lax.broadcasted_iota(jnp.int32, (8, 128), 0)
    hit = index == which[0]
    for w in which[1:]:
        hit = hit | (index == w)
    return hit

def spread(row):
    return jnp.broadcast_to(row, (8, row.shape[1]))

def features(state):
    centred = jnp.where(row_is(0, 1, 2), state - 1.0, state)
    r, rho = spread(state[6:7]), spread(state[7:8])
    live = rho > 0.0
    mass = rho * VOLUME
    r2 = r * r
    pressure = jnp.where(live, STIFFNESS * (r2 * r2 * r2 * r - 1.0) / (jnp.where(live, rho, 1.0) * r2), 0.0)
    mp = mass * pressure
    place = jnp.where(row_is(0, 1, 2), centred, 0.0)
    norm = 0.25 * jnp.sum(place * place, axis=0, keepdims=True)
    speed = jnp.where(row_is(0, 1, 2), pltpu.roll(centred, 5, 0), 0.0)
    flux = jnp.sum(place * speed, axis=0, keepdims=True)
    own = jnp.where(row_is(3), norm, jnp.where(row_is(4), 1.0, place))
    near = jnp.where(row_is(3), 1.0, jnp.where(row_is(4), norm, -0.5 * place))
    moved = jnp.where(row_is(0), 1.0, jnp.where(row_is(7), flux, pltpu.roll(centred, 1, 0)))
    sums_a = mass * moved
    sums_b = jnp.where(row_is(0, 1, 2, 3), mp * moved, 0.0)
    near_x = jnp.where(row_is(0), -0.5, jnp.where(row_is(4), 0.5 * centred[0:1], 0.0))
    near_z = jnp.where(row_is(2), -0.5, jnp.where(row_is(4), 0.5 * centred[2:3], 0.0))
    sums_ax = mass * jnp.where(row_is(1), 1.0, jnp.where(row_is(7), centred[3:4], 0.0))
    sums_az = mass * jnp.where(row_is(3), 1.0, jnp.where(row_is(7), centred[5:6], 0.0))
    sums_bx = jnp.where(row_is(1), mp, 0.0)
    sums_bz = jnp.where(row_is(3), mp, 0.0)
    return own, rows(near, sums_a, sums_b), rows(near_x, sums_ax, sums_bx), rows(near_z, sums_az, sums_bz), pressure[0:1]

def prep_kernel(particles_ref, flags_ref, codes_ref, state_ref, lo_ref, hi_ref, flat):
    count = flags_ref.shape[0]
    fields = particles_ref.shape[0] // count
    for i in range(fields):
        flat[pl.ds(i, count, stride=8), :] = particles_ref[pl.ds(i, count, stride=fields), :]
    flat[pl.ds(fields, count, stride=8), :] = 1.0 + SEDIMENT_EXTRA * flags_ref[...].astype(F32)
    for b in range(count):
        state_ref[b] = flat[8 * b:8 * b + 8]
    for ref, first, edge in ((lo_ref, 0, 0), (hi_ref, count - 2, count - 1)):
        for i in range(2):
            ref[i] = flat[8 * (first + i):8 * (first + i) + 8]
        ref[2] = jnp.zeros_like(ref[2])
        ref[2, 0:codes_ref.shape[0], 0:1] = codes_ref[:, edge:edge + 1].astype(F32)


def prepare(particles, flags, codes):
    count, fields, part = particles.shape
    v = pl.BlockSpec(memory_space=pltpu.VMEM)
    rim = jax.ShapeDtypeStruct((3, 8, part), F32)
    return pl.pallas_call(
        prep_kernel,
        out_shape=(jax.ShapeDtypeStruct((count, 8, part), F32), rim, rim),
        in_specs=[v, v, v], out_specs=(v, v, v),
        scratch_shapes=[pltpu.VMEM((count * 8, part), F32)],
    )(particles.reshape(count * fields, part), flags, codes)


def own_side(own):
    o1, o2, o3 = pieces(own)
    return rows(o1, o1, o2, o2, o1, o3).astype(BF16)


def near_side(g):
    p1, p2, p3 = pieces(g[0:8])
    f1 = g[8:24].astype(BF16)
    f2 = (g[8:24] - f1.astype(F32)).astype(BF16)
    return rows(p1, p2, p1, p2, p3, p1).astype(BF16), rows(f1, f2)


def weighted_sums(group):
    width = len(group)
    zero = jnp.zeros_like(group[0][0])
    rhs = rows(*[jnp.concatenate([g[0] if m == k else zero for m in range(width)], axis=1) for k, g in enumerate(group)])
    s = lax.dot_general(rows(*[g[1] for g in group]), rhs, (((0,), (0,)), ((), ())), preferred_element_type=F32)
    s = jnp.maximum(s, 1e-20)
    k = jnp.maximum(1.0 - s * lax.rsqrt(s), 0.0)
    wgt = k * k * k
    wh = wgt.astype(BF16)
    wl = (wgt - wh.astype(F32)).astype(BF16)
    f = rows(*[jnp.concatenate([g[2], g[2]], axis=1) for g in group])
    acc = jnp.dot(f, rows(wh, wl), preferred_element_type=F32)
    part = zero.shape[1]
    cut = [acc[32 * k:32 * (k + 1), part * k:part * (k + 1)] for k in range(width)]
    return [t[0:16] + t[16:32] for t in cut]


def in_groups(count, run):
    width = 2 if count % 2 == 0 else 1
    trips = count // width

    def trip(i, _):
        run([width * i + k for k in range(width)])
        return 0
    lax.fori_loop(0, trips, trip, 0, unroll=max(u for u in range(1, 18) if trips % u == 0))


def inner_part(state_ref, skip, self_ref, side_ref):
    def run(blocks):
        group = []
        for b in blocks:
            own, g_self, _, _, pressure = features(state_ref[b + skip])
            side = own_side(own)
            side_ref[b] = side
            self_ref[b, 16:24] = spread(pressure)
            group.append((side,) + near_side(g_self))
        for b, t in zip(blocks, weighted_sums(group)):
            self_ref[b, 0:16] = t
    in_groups(self_ref.shape[0], run)


def inner_shapes(count, part):
    return (jax.ShapeDtypeStruct((count, 24, part), F32), jax.ShapeDtypeStruct((count, 48, part), BF16))


def step_blocks(codes_ref, edge_ref, low_ref, mid_ref, high_ref, self_ref, side_ref, out_ref, b0, b1, b2):
    ext = mid_ref.shape[0]
    count = ext - 2
    sel = lax.broadcasted_iota(jnp.int32, (8, 1), 0) == 7
    rim = edge_ref[5]

    def prep(i):
        rowon = jnp.where(i < rim, edge_ref[3], jnp.where(i >= ext - rim, edge_ref[4], 1))
        for col, ref in ((0, low_ref), (1, mid_ref), (2, high_ref)):
            st = ref[i]
            keep = (edge_ref[col] * rowon).astype(F32)
            _, a, b, c, _ = features(jnp.where(sel, st * keep, st))
            b0[col * ext + i] = a
            b1[col * ext + i] = b
            b2[col * ext + i] = c

    for i in range(3):
        prep(i)
    normrow = (lax.broadcasted_iota(jnp.int32, (24, 1), 0) == 4).astype(F32)
    skip = edge_ref[6]

    def operands(b):
        st = mid_ref[b + 1]
        gs = []
        for n in range(codes_ref.shape[0]):
            c = codes_ref[n, b + skip]
            o = c + jnp.where(c >= 4, 1, 0)
            ds1 = (o * 11) >> 5
            dv1 = o - 3 * ds1
            idx = dv1 * ext + b + ds1
            tx = 2.0 * (ds1 - 1).astype(F32)
            tz = 2.0 * (dv1 - 1).astype(F32)
            gs.append(b0[idx] + tx * b1[idx] + tz * b2[idx] + normrow * (0.25 * (tx * tx + tz * tz)))
        prep(jnp.minimum(b + 3, ext - 1))
        near = [near_side(g) for g in gs]
        return st, (side_ref[b],) + tuple(jnp.concatenate(x, axis=1) for x in zip(*near))

    def finish(b, st, pressure, t):
        x, vel = st[0:3] - 1.0, st[3:6]
        coef = -5.0 * ALPHA_KERNEL
        sw, swx, swv, swf = t[0:1], t[1:4], t[4:7], t[7:8]
        swp, swpx = t[8:9], t[9:12]
        dens = coef * (jnp.sum(vel * (x * sw - swx) - x * swv, axis=0, keepdims=True) + swf)
        acc3 = -coef * (pressure * (x * sw - swx) + x * swp - swpx)
        grav = jnp.where(lax.broadcasted_iota(jnp.int32, (3, 1), 0) == 2, -GRAVITY, 0.0)
        vel2 = vel + TIME_STEP * (acc3 + grav)
        pos2 = st[0:3] + TIME_STEP * vel2
        rho = st[7:8]
        r2 = st[6:7] + TIME_STEP * dens / rho
        out_ref[b] = rows(pos2, vel2, r2, rho)

    def run(blocks):
        group = [operands(b) for b in blocks]
        for b, (st, _), t in zip(blocks, group, weighted_sums([g[1] for g in group])):
            finish(b, st, self_ref[b, 16:17], t + self_ref[b, 0:16])
    in_groups(count, run)


def step_scratch(ext, part):
    return [pltpu.VMEM((3 * ext, 24, part), F32)] * 3


def first_step(codes, edges, low, mid, high, inner):
    ext, _, part = mid.shape
    v = pl.BlockSpec(memory_space=pltpu.VMEM)
    sm = pl.BlockSpec(memory_space=pltpu.SMEM)
    return pl.pallas_call(
        step_blocks, out_shape=jax.ShapeDtypeStruct((ext - 2, 8, part), F32),
        in_specs=[sm, sm, v, v, v, v, v], out_specs=v,
        scratch_shapes=step_scratch(ext, part),
        compiler_params=pltpu.CompilerParams(vmem_limit_bytes=VMEM_LIMIT),
    )(codes, edges, low, mid, high, *inner)


def cross_row(hist_ref, new, others, terms):
    comps, hist = hist_ref.shape[0], hist_ref.shape[1]
    groups = new[0].shape[0] // 8

    def fold(x):
        total = x[0:8]
        for g in range(1, groups):
            total = total + x[8 * g:8 * g + 8]
        return total

    def one(s, _):
        total = hist_ref[0, s].astype(F32) * new[0]
        for c in range(1, comps):
            total = total + hist_ref[c, s].astype(F32) * new[c]
        terms[pl.ds(pl.multiple_of(8 * s, 8), 8), :] = fold(total)
        return 0
    lax.fori_loop(0, hist, one, 0, unroll=max(u for u in range(1, 10) if hist % u == 0))
    snaps = terms.shape[0] // 8
    for k in range(snaps - hist):
        if k < len(others):
            total = others[k][0] * new[0]
            for c in range(1, comps):
                total = total + others[k][c] * new[c]
            terms[8 * (hist + k):8 * (hist + k) + 8] = fold(total)
        else:
            terms[8 * (hist + k):8 * (hist + k) + 8] = jnp.zeros_like(terms[0:8])
    by_snap = terms[pl.ds(0, snaps, stride=8), :]
    for i in range(1, 8):
        by_snap = by_snap + terms[pl.ds(i, snaps, stride=8), :]
    ones = jnp.ones((8, by_snap.shape[1]), F32)
    return lax.dot_general(ones, by_snap, (((1,), (1,)), ((), ())), precision=HIGHEST, preferred_element_type=F32)[0:1]


def load_new(ref, skip, count, flat):
    def move(b, _):
        flat[pl.ds(pl.multiple_of(8 * b, 8), 8), :] = ref[b + skip]
        return 0
    lax.fori_loop(0, count, move, 0, unroll=math.gcd(count, 8))
    return [flat[pl.ds(3 + c, count, stride=8), :].astype(BF16).astype(F32) for c in range(3)]


def second_step(codes, edges, low, mid, high, inner, hist, gram):
    ext, _, part = mid.shape
    count = ext - 2
    snaps = gram.shape[0]
    v = pl.BlockSpec(memory_space=pltpu.VMEM)
    sm = pl.BlockSpec(memory_space=pltpu.SMEM)

    def kernel(codes_ref, edge_ref, low_ref, mid_ref, high_ref, self_ref, side_ref, hist_ref, gram_ref, new_ref, state_ref, gram_out,
               b0, b1, b2, flat, terms):
        step_blocks(codes_ref, edge_ref, low_ref, mid_ref, high_ref, self_ref, side_ref, state_ref, b0, b1, b2)
        first = load_new(mid_ref, 1, count, flat)
        second = load_new(state_ref, 0, count, flat)
        for i in range(7):
            new_ref[pl.ds(i, count, stride=7), :] = flat[pl.ds(i, count, stride=8), :]
        row = cross_row(hist_ref, second, (first, second), terms)
        last = lax.broadcasted_iota(jnp.int32, (snaps, 1), 0) == snaps - 1
        gram_out[...] = jnp.where(last, row, gram_ref[...])

    return pl.pallas_call(
        kernel,
        out_shape=(jax.ShapeDtypeStruct((count * 7, part), F32), jax.ShapeDtypeStruct((count, 8, part), F32),
                   jax.ShapeDtypeStruct((snaps, snaps), F32)),
        in_specs=[sm, sm] + [v] * 7, out_specs=(v, v, v),
        scratch_shapes=step_scratch(ext, part) + [
            pltpu.VMEM((count * 8, part), F32), pltpu.VMEM((snaps * 8, part), F32)],
        compiler_params=pltpu.CompilerParams(vmem_limit_bytes=VMEM_LIMIT),
    )(codes, edges, low, mid, high, *inner, hist, gram)


def inner_sums(mid):
    count, _, part = mid.shape
    v = pl.BlockSpec(memory_space=pltpu.VMEM)

    def kernel(mid_ref, self_ref, side_ref):
        inner_part(mid_ref, 1, self_ref, side_ref)

    return pl.pallas_call(
        kernel, out_shape=inner_shapes(count - 2, part), in_specs=[v], out_specs=(v, v),
        compiler_params=pltpu.CompilerParams(vmem_limit_bytes=VMEM_LIMIT),
        cost_estimate=pl.CostEstimate(flops=1 << 30, bytes_accessed=1 << 20, transcendentals=0),
    )(mid)


def early_gram(hist, first):
    comps, snaps_old, count, part = hist.shape
    snaps = snaps_old + 2
    pitch = count + 8
    v = pl.BlockSpec(memory_space=pltpu.VMEM)

    def kernel(hist_ref, first_ref, out_ref, wide, flat, terms):
        total = jnp.zeros((snaps_old, snaps_old), F32)
        for c in range(comps):
            def expand(s, _):
                wide[pl.ds(pl.multiple_of(pitch * s, 8), count), :] = hist_ref[c, s].astype(F32)
                return 0
            lax.fori_loop(0, snaps_old, expand, 0, unroll=max(u for u in range(1, 10) if snaps_old % u == 0))
            for b in range(0, count, 8):
                x = jnp.concatenate([wide[pl.ds(b + j, snaps_old, stride=pitch), :].astype(BF16) for j in range(8)], axis=1)
                total = total + lax.dot_general(x, x, (((1,), (1,)), ((), ())), preferred_element_type=F32)
        out_ref[...] = jnp.zeros_like(out_ref)
        out_ref[0:snaps_old, 0:snaps_old] = total
        new = load_new(first_ref, 1, count, flat)
        out_ref[snaps_old:snaps_old + 1] = cross_row(hist_ref, new, (new,), terms)

    return pl.pallas_call(
        kernel, out_shape=jax.ShapeDtypeStruct((snaps, snaps), F32),
        in_specs=[v, v], out_specs=v,
        scratch_shapes=[pltpu.VMEM((snaps_old * pitch, part), F32), pltpu.VMEM((count * 8, part), F32),
                        pltpu.VMEM((snaps * 8, part), F32)],
        compiler_params=pltpu.CompilerParams(vmem_limit_bytes=VMEM_LIMIT),
        cost_estimate=pl.CostEstimate(flops=2 * comps * snaps * snaps * count * part, bytes_accessed=2 * comps * snaps * count * part, transcendentals=0),
    )(hist, first)


HIGHEST = lax.Precision.HIGHEST
REPEAT_BELOW = 1e-5
JOIN_ABOVE = 1e-4


def gram_of(m):
    return lax.dot_general(m, m, (((1,), (1,)), ((), ())), precision=HIGHEST, preferred_element_type=F32)


def orthonormal(m):
    n, wide = m.shape
    nb = n // 8
    s = gram_of(m)
    s = jnp.concatenate([s, jnp.zeros((n, wide - n), F32)], axis=1)
    sb = [s[8 * k:8 * k + 8] for k in range(nb)]
    mb = [m[8 * k:8 * k + 8] for k in range(nb)]
    sub = lax.broadcasted_iota(jnp.int32, (8, wide), 0)
    full = lambda x: jnp.broadcast_to(x, (8, wide))
    worst = None
    for k in range(nb):
        p = 8 * k
        norm0 = jnp.sum(m[8 * k:8 * k + 8] * m[8 * k:8 * k + 8], axis=1, keepdims=True)
        rs = [full(sb[k][i:i + 1]) for i in range(8)]
        rm = [full(mb[k][i:i + 1]) for i in range(8)]
        e = [[full(rs[i][:, p + j:p + j + 1]) for j in range(i + 1)] for i in range(8)]
        cols = [[full(sb[t][:, p + j:p + j + 1]) for j in range(8)] for t in range(k + 1, nb)]
        inv, low = [], [[None] * 8 for _ in range(8)]
        for j in range(8):
            inv.append(1.0 / e[j][j])
            for i in range(j + 1, 8):
                for t in range(j + 1, i + 1):
                    e[i][t] = e[i][t] - (e[i][j] * e[t][j]) * inv[j]
            for i in range(j + 1, 8):
                low[i][j] = e[i][j] * inv[j]
            for i in range(j + 1, 8):
                rs[i] = rs[i] - low[i][j] * rs[j]
                rm[i] = rm[i] - low[i][j] * rm[j]
        d = e[0][0]
        out = rm[0]
        for i in range(1, 8):
            d = jnp.where(sub == i, e[i][i], d)
            out = jnp.where(sub == i, rm[i], out)
        mb[k] = out * lax.rsqrt(d)
        ratio = d / norm0
        worst = ratio if worst is None else jnp.minimum(worst, ratio)
        if k == nb - 1:
            break
        us = [rs[j] * inv[j] for j in range(8)]
        um = [rm[j] * inv[j] for j in range(8)]
        for t in range(k + 1, nb):
            c = cols[t - k - 1]
            for j in range(8):
                for i in range(j + 1, 8):
                    c[i] = c[i] - low[i][j] * c[j]
                sb[t] = sb[t] - c[j] * us[j]
                mb[t] = mb[t] - c[j] * um[j]
    return jnp.concatenate(mb, 0), jnp.min(worst)


def repeated(m, q_ref):
    q, worst = orthonormal(m)
    q_ref[...] = q

    @pl.when(jnp.logical_not(worst >= REPEAT_BELOW))
    def _():
        q_ref[...] = orthonormal(q_ref[...])[0]


def start_basis(basis_t):
    v = pl.BlockSpec(memory_space=pltpu.VMEM)

    def kernel(b_ref, q_ref):
        repeated(b_ref[...], q_ref)

    return pl.pallas_call(
        kernel, out_shape=jax.ShapeDtypeStruct(basis_t.shape, F32), in_specs=[v], out_specs=v,
        cost_estimate=pl.CostEstimate(flops=1 << 30, bytes_accessed=1 << 20, transcendentals=0),
    )(basis_t)


def weigh(iters, g_ref, b_ref, q_ref):
    snaps = g_ref.shape[0]
    rows_in = lax.broadcasted_iota(jnp.int32, (snaps, snaps), 0)
    cols_in = lax.broadcasted_iota(jnp.int32, (snaps, snaps), 1)
    g = g_ref[...]
    low = (rows_in >= snaps - 2) & (cols_in < rows_in)
    g = jnp.where(low | (rows_in == cols_in) | ((rows_in < snaps - 2) & (cols_in < snaps - 2)), g, 0.0)
    trace = jnp.sum(jnp.where(rows_in == cols_in, g, 0.0), axis=(0, 1), keepdims=True)
    g_ref[...] = (g + jnp.where(low, g, 0.0).T) * (1.0 / trace)
    q_ref[...] = b_ref[...]

    def product(q):
        return jnp.dot(q, g_ref[...], precision=HIGHEST, preferred_element_type=F32)

    def iterate(i, _):
        repeated(product(q_ref[...]), q_ref)
        return 0

    lax.fori_loop(0, iters - 2, iterate, 0)
    q, worst = orthonormal(product(product(q_ref[...])))
    good = worst >= JOIN_ABOVE

    @pl.when(jnp.logical_not(good))
    def _():
        lax.fori_loop(iters - 2, iters, iterate, 0)

    @pl.when(good)
    def _():
        q_ref[...] = q

    q = q_ref[...]
    last = (lax.broadcasted_iota(jnp.int32, (1, snaps), 1) == snaps - 1).astype(F32)
    w = jnp.zeros((1, snaps), F32)
    for _ in range(3):
        y = jnp.sum(q * (last - w), axis=1, keepdims=True)
        w = w + jnp.sum(q * y, axis=0, keepdims=True)
    return w


def filtered_field(gram, basis_t, hist, first, second):
    comps, snaps_old, count, part = hist.shape
    v = pl.BlockSpec(memory_space=pltpu.VMEM)

    def kernel(gram_ref, b_ref, hist_ref, first_ref, second_ref, out_ref, g_ref, q_ref, flat, table):
        g_ref[...] = gram_ref[...]
        w = weigh(POD_ITERS, g_ref, b_ref, q_ref)
        table[...] = jnp.broadcast_to(w, table.shape).T
        start = []
        for k, (ref, skip) in enumerate(((first_ref, 1), (second_ref, 0))):
            wk = table[snaps_old + k:snaps_old + k + 1]
            new = [wk * x for x in load_new(ref, skip, count, flat)]
            start = [x + y for x, y in zip(start, new)] if start else new

        def one(s, total):
            wk = table[pl.ds(s, 1), :]
            return [total[c] + wk * hist_ref[c, s].astype(F32) for c in range(comps)]
        total = lax.fori_loop(0, snaps_old, one, start, unroll=max(u for u in range(1, 10) if snaps_old % u == 0))
        for c in range(comps):
            out_ref[pl.ds(c, count, stride=comps), :] = total[c]

    return pl.pallas_call(
        kernel, out_shape=jax.ShapeDtypeStruct((count * comps, part), F32),
        in_specs=[v, v, v, v, v], out_specs=v,
        scratch_shapes=[pltpu.VMEM(gram.shape, F32), pltpu.VMEM(basis_t.shape, F32),
                        pltpu.VMEM((count * 8, part), F32), pltpu.VMEM(gram.shape, F32)],
        compiler_params=pltpu.CompilerParams(vmem_limit_bytes=VMEM_LIMIT),
    )(gram, basis_t, hist, first, second)


def shift(x, axis, by):
    count = lax.axis_size(axis)
    return lax.ppermute(x, axis, [(i, (i + by) % count) for i in range(count)])


def reduce_all(x):
    axes = ("stream", "vert")
    sizes = [lax.axis_size(a) for a in axes]
    if any(n & (n - 1) for n in sizes):
        return lax.psum(x, axes)
    bits = [(0, 1 << k) for k in range(sizes[1].bit_length() - 1)] + [(1 << k, 0) for k in range(sizes[0].bit_length() - 1)]
    start = len(bits) % 2
    for group in [bits[0:start]] * start + [bits[k:k + 2] for k in range(start, len(bits), 2)]:
        masks = [(0, 0)]
        for s, v in group:
            masks = masks + [(a ^ s, b ^ v) for a, b in masks]
        total = x
        for s, v in masks[1:]:
            total = total + lax.ppermute(x, axes, [
                (i * sizes[1] + j, (i ^ s) * sizes[1] + (j ^ v)) for i in range(sizes[0]) for j in range(sizes[1])])
        x = total
    return x


def body(particles, phase_flags, neighbours, history, basis_start):
    count = particles.shape[0]
    codes = neighbours[:, 0].T
    width = codes.shape[0]
    hist = history[:, 0].transpose(1, 2, 0, 3)
    s, v = lax.axis_index("stream"), lax.axis_index("vert")
    ns, nv = lax.axis_size("stream"), lax.axis_size("vert")
    one = jnp.ones((), jnp.int32)
    common = [v > 0, one, v < nv - 1, s > 0, s < ns - 1]
    edges1 = jnp.stack(common + [2 * one, 0 * one, one]).astype(jnp.int32)
    edges2 = jnp.stack(common + [one, one, one]).astype(jnp.int32)
    state, lo, hi = prepare(particles[:, 0], phase_flags[:, 0], codes)
    from_low = shift(hi, "stream", 1)
    from_high = shift(lo, "stream", -1)
    mid = jnp.concatenate([from_low[0:2], state, from_high[0:2]], axis=0)
    wide_codes = jnp.concatenate(
        [from_low[2, 0:width, 0:1].astype(jnp.int32), codes, from_high[2, 0:width, 0:1].astype(jnp.int32)], axis=1)
    low_mid, high_mid = shift(mid, "vert", 1), shift(mid, "vert", -1)
    basis = start_basis(basis_start.T)
    wide_codes, basis = lax.optimization_barrier((wide_codes, basis))
    first = first_step(wide_codes, edges1, low_mid, mid, high_mid, inner_sums(mid))
    low, high = shift(first, "vert", 1), shift(first, "vert", -1)
    inner = inner_sums(first)
    gram = early_gram(hist, first)
    new_state, second, gram = second_step(wide_codes, edges2, low, first, high, inner, hist, gram)
    gram = reduce_all(gram)
    out = filtered_field(gram, basis, hist, first, second)
    return (new_state.reshape(count, 1, 7, -1), out.reshape(count, 1, 3, -1))


def solution(mesh):
    in_specs = (
        P("stream", "vert", None, None),
        P("stream", "vert", None),
        P("stream", "vert", None),
        P("stream", "vert", None, None, None),
        P(),
    )
    out_specs = (P("stream", "vert", None, None), P("stream", "vert", None, None))
    return jax.shard_map(body, mesh=mesh, in_specs=in_specs, out_specs=out_specs, check_vma=False)
```

```python
import functools
import math

import jax
import jax.numpy as jnp
from jax import lax
from jax.experimental import pallas as pl
from jax.experimental.pallas import tpu as pltpu
from jax.sharding import PartitionSpec as P

POD_ITERS = 4
VMEM_LIMIT = 20 << 20
SEDIMENT_EXTRA = 1.65


ALPHA_KERNEL = 21.0 / (16.0 * math.pi)
VOLUME = 1.0 / 16.0
STIFFNESS = 100.0 / 7.0
TIME_STEP = 0.02
GRAVITY = 1.0
F32, BF16 = jnp.float32, jnp.bfloat16

def pieces(x):
    a = x.astype(BF16).astype(F32)
    r = x - a
    b = r.astype(BF16).astype(F32)
    return a, b, r - b

def rows(*parts):
    return jnp.concatenate(parts, axis=0)

def row_is(*which):
    index = lax.broadcasted_iota(jnp.int32, (8, 128), 0)
    hit = index == which[0]
    for w in which[1:]:
        hit = hit | (index == w)
    return hit

def spread(row):
    return jnp.broadcast_to(row, (8, row.shape[1]))

def features(state):
    centred = jnp.where(row_is(0, 1, 2), state - 1.0, state)
    r, rho = spread(state[6:7]), spread(state[7:8])
    live = rho > 0.0
    mass = rho * VOLUME
    r2 = r * r
    pressure = jnp.where(live, STIFFNESS * (r2 * r2 * r2 * r - 1.0) / (jnp.where(live, rho, 1.0) * r2), 0.0)
    mp = mass * pressure
    place = jnp.where(row_is(0, 1, 2), centred, 0.0)
    norm = 0.25 * jnp.sum(place * place, axis=0, keepdims=True)
    speed = jnp.where(row_is(0, 1, 2), pltpu.roll(centred, 5, 0), 0.0)
    flux = jnp.sum(place * speed, axis=0, keepdims=True)
    own = jnp.where(row_is(3), norm, jnp.where(row_is(4), 1.0, place))
    near = jnp.where(row_is(3), 1.0, jnp.where(row_is(4), norm, -0.5 * place))
    moved = jnp.where(row_is(0), 1.0, jnp.where(row_is(7), flux, pltpu.roll(centred, 1, 0)))
    sums_a = mass * moved
    sums_b = jnp.where(row_is(0, 1, 2, 3), mp * moved, 0.0)
    near_x = jnp.where(row_is(0), -0.5, jnp.where(row_is(4), 0.5 * centred[0:1], 0.0))
    near_z = jnp.where(row_is(2), -0.5, jnp.where(row_is(4), 0.5 * centred[2:3], 0.0))
    sums_ax = mass * jnp.where(row_is(1), 1.0, jnp.where(row_is(7), centred[3:4], 0.0))
    sums_az = mass * jnp.where(row_is(3), 1.0, jnp.where(row_is(7), centred[5:6], 0.0))
    sums_bx = jnp.where(row_is(1), mp, 0.0)
    sums_bz = jnp.where(row_is(3), mp, 0.0)
    return own, rows(near, sums_a, sums_b), rows(near_x, sums_ax, sums_bx), rows(near_z, sums_az, sums_bz), pressure[0:1]

def prep_kernel(particles_ref, flags_ref, codes_ref, state_ref, lo_ref, hi_ref, flat):
    count = flags_ref.shape[0]
    fields = particles_ref.shape[0] // count
    for i in range(fields):
        flat[pl.ds(i, count, stride=8), :] = particles_ref[pl.ds(i, count, stride=fields), :]
    flat[pl.ds(fields, count, stride=8), :] = 1.0 + SEDIMENT_EXTRA * flags_ref[...].astype(F32)
    for b in range(count):
        state_ref[b] = flat[8 * b:8 * b + 8]
    for ref, first, edge in ((lo_ref, 0, 0), (hi_ref, count - 2, count - 1)):
        for i in range(2):
            ref[i] = flat[8 * (first + i):8 * (first + i) + 8]
        ref[2] = jnp.zeros_like(ref[2])
        ref[2, 0:codes_ref.shape[0], 0:1] = codes_ref[:, edge:edge + 1].astype(F32)


def prepare(particles, flags, codes):
    count, fields, part = particles.shape
    v = pl.BlockSpec(memory_space=pltpu.VMEM)
    rim = jax.ShapeDtypeStruct((3, 8, part), F32)
    return pl.pallas_call(
        prep_kernel,
        out_shape=(jax.ShapeDtypeStruct((count, 8, part), F32), rim, rim),
        in_specs=[v, v, v], out_specs=(v, v, v),
        scratch_shapes=[pltpu.VMEM((count * 8, part), F32)],
    )(particles.reshape(count * fields, part), flags, codes)


def own_side(own):
    o1, o2, o3 = pieces(own)
    return rows(o1, o1, o2, o2, o1, o3).astype(BF16)


def near_side(g):
    p1, p2, p3 = pieces(g[0:8])
    f1 = g[8:24].astype(BF16)
    f2 = (g[8:24] - f1.astype(F32)).astype(BF16)
    return rows(p1, p2, p1, p2, p3, p1).astype(BF16), rows(f1, f2)


def weighted_sums(group):
    width = len(group)
    zero = jnp.zeros_like(group[0][0])
    rhs = rows(*[jnp.concatenate([g[0] if m == k else zero for m in range(width)], axis=1) for k, g in enumerate(group)])
    s = lax.dot_general(rows(*[g[1] for g in group]), rhs, (((0,), (0,)), ((), ())), preferred_element_type=F32)
    s = jnp.maximum(s, 1e-20)
    k = jnp.maximum(1.0 - s * lax.rsqrt(s), 0.0)
    wgt = k * k * k
    wh = wgt.astype(BF16)
    wl = (wgt - wh.astype(F32)).astype(BF16)
    f = rows(*[jnp.concatenate([g[2], g[2]], axis=1) for g in group])
    acc = jnp.dot(f, rows(wh, wl), preferred_element_type=F32)
    part = zero.shape[1]
    cut = [acc[32 * k:32 * (k + 1), part * k:part * (k + 1)] for k in range(width)]
    return [t[0:16] + t[16:32] for t in cut]


def in_groups(count, run):
    width = 2 if count % 2 == 0 else 1
    trips = count // width

    def trip(i, _):
        run([width * i + k for k in range(width)])
        return 0
    lax.fori_loop(0, trips, trip, 0, unroll=max(u for u in range(1, 18) if trips % u == 0))


def inner_part(state_ref, skip, self_ref, side_ref):
    def run(blocks):
        group = []
        for b in blocks:
            own, g_self, _, _, pressure = features(state_ref[b + skip])
            side = own_side(own)
            side_ref[b] = side
            self_ref[b, 16:24] = spread(pressure)
            group.append((side,) + near_side(g_self))
        for b, t in zip(blocks, weighted_sums(group)):
            self_ref[b, 0:16] = t
    in_groups(self_ref.shape[0], run)


def inner_shapes(count, part):
    return (jax.ShapeDtypeStruct((count, 24, part), F32), jax.ShapeDtypeStruct((count, 48, part), BF16))


def step_blocks(codes_ref, edge_ref, low_ref, mid_ref, high_ref, self_ref, side_ref, out_ref, b0, b1, b2):
    ext = mid_ref.shape[0]
    count = ext - 2
    sel = lax.broadcasted_iota(jnp.int32, (8, 1), 0) == 7
    rim = edge_ref[5]

    def prep(i):
        rowon = jnp.where(i < rim, edge_ref[3], jnp.where(i >= ext - rim, edge_ref[4], 1))
        for col, ref in ((0, low_ref), (1, mid_ref), (2, high_ref)):
            st = ref[i]
            keep = (edge_ref[col] * rowon).astype(F32)
            _, a, b, c, _ = features(jnp.where(sel, st * keep, st))
            b0[col * ext + i] = a
            b1[col * ext + i] = b
            b2[col * ext + i] = c

    for i in range(3):
        prep(i)
    normrow = (lax.broadcasted_iota(jnp.int32, (24, 1), 0) == 4).astype(F32)
    skip = edge_ref[6]

    def operands(b):
        st = mid_ref[b + 1]
        gs = []
        for n in range(codes_ref.shape[0]):
            c = codes_ref[n, b + skip]
            o = c + jnp.where(c >= 4, 1, 0)
            ds1 = (o * 11) >> 5
            dv1 = o - 3 * ds1
            idx = dv1 * ext + b + ds1
            tx = 2.0 * (ds1 - 1).astype(F32)
            tz = 2.0 * (dv1 - 1).astype(F32)
            gs.append(b0[idx] + tx * b1[idx] + tz * b2[idx] + normrow * (0.25 * (tx * tx + tz * tz)))
        prep(jnp.minimum(b + 3, ext - 1))
        near = [near_side(g) for g in gs]
        return st, (side_ref[b],) + tuple(jnp.concatenate(x, axis=1) for x in zip(*near))

    def finish(b, st, pressure, t):
        x, vel = st[0:3] - 1.0, st[3:6]
        coef = -5.0 * ALPHA_KERNEL
        sw, swx, swv, swf = t[0:1], t[1:4], t[4:7], t[7:8]
        swp, swpx = t[8:9], t[9:12]
        dens = coef * (jnp.sum(vel * (x * sw - swx) - x * swv, axis=0, keepdims=True) + swf)
        acc3 = -coef * (pressure * (x * sw - swx) + x * swp - swpx)
        grav = jnp.where(lax.broadcasted_iota(jnp.int32, (3, 1), 0) == 2, -GRAVITY, 0.0)
        vel2 = vel + TIME_STEP * (acc3 + grav)
        pos2 = st[0:3] + TIME_STEP * vel2
        rho = st[7:8]
        r2 = st[6:7] + TIME_STEP * dens / rho
        out_ref[b] = rows(pos2, vel2, r2, rho)

    def run(blocks):
        group = [operands(b) for b in blocks]
        for b, (st, _), t in zip(blocks, group, weighted_sums([g[1] for g in group])):
            finish(b, st, self_ref[b, 16:17], t + self_ref[b, 0:16])
    in_groups(count, run)


def step_scratch(ext, part):
    return [pltpu.VMEM((3 * ext, 24, part), F32)] * 3


def first_step(codes, edges, low, mid, high, inner):
    ext, _, part = mid.shape
    v = pl.BlockSpec(memory_space=pltpu.VMEM)
    sm = pl.BlockSpec(memory_space=pltpu.SMEM)
    return pl.pallas_call(
        step_blocks, out_shape=jax.ShapeDtypeStruct((ext - 2, 8, part), F32),
        in_specs=[sm, sm, v, v, v, v, v], out_specs=v,
        scratch_shapes=step_scratch(ext, part),
        compiler_params=pltpu.CompilerParams(vmem_limit_bytes=VMEM_LIMIT),
    )(codes, edges, low, mid, high, *inner)


def cross_row(hist_ref, new, others, terms):
    comps, hist = hist_ref.shape[0], hist_ref.shape[1]
    groups = new[0].shape[0] // 8

    def fold(x):
        total = x[0:8]
        for g in range(1, groups):
            total = total + x[8 * g:8 * g + 8]
        return total

    def one(s, _):
        total = hist_ref[0, s].astype(F32) * new[0]
        for c in range(1, comps):
            total = total + hist_ref[c, s].astype(F32) * new[c]
        terms[pl.ds(pl.multiple_of(8 * s, 8), 8), :] = fold(total)
        return 0
    lax.fori_loop(0, hist, one, 0, unroll=max(u for u in range(1, 10) if hist % u == 0))
    snaps = terms.shape[0] // 8
    for k in range(snaps - hist):
        if k < len(others):
            total = others[k][0] * new[0]
            for c in range(1, comps):
                total = total + others[k][c] * new[c]
            terms[8 * (hist + k):8 * (hist + k) + 8] = fold(total)
        else:
            terms[8 * (hist + k):8 * (hist + k) + 8] = jnp.zeros_like(terms[0:8])
    by_snap = terms[pl.ds(0, snaps, stride=8), :]
    for i in range(1, 8):
        by_snap = by_snap + terms[pl.ds(i, snaps, stride=8), :]
    ones = jnp.ones((8, by_snap.shape[1]), F32)
    return lax.dot_general(ones, by_snap, (((1,), (1,)), ((), ())), precision=HIGHEST, preferred_element_type=F32)[0:1]


def load_new(ref, skip, count, flat):
    def move(b, _):
        flat[pl.ds(pl.multiple_of(8 * b, 8), 8), :] = ref[b + skip]
        return 0
    lax.fori_loop(0, count, move, 0, unroll=math.gcd(count, 8))
    return [flat[pl.ds(3 + c, count, stride=8), :].astype(BF16).astype(F32) for c in range(3)]


def corner(n):
    rows_in = lax.broadcasted_iota(jnp.int32, (n, n), 0)
    cols_in = lax.broadcasted_iota(jnp.int32, (n, n), 1)
    return rows_in, cols_in


def pack(g, out_ref):
    n = g.shape[0] // 2
    rows_in, cols_in = corner(n)
    right = g[n:, n:]
    out_ref[0:n, 0:n] = jnp.where(rows_in >= cols_in, g[0:n, 0:n], right.T)
    out_ref[0:n, n:] = g[n:, 0:n]
    diagonal = jnp.sum(jnp.where(rows_in == cols_in, right, 0.0), axis=0, keepdims=True)
    out_ref[n:] = jnp.broadcast_to(jnp.concatenate([diagonal, diagonal], axis=1), (8, 2 * n))


def unpack(p_ref):
    n = p_ref.shape[1] // 2
    rows_in, cols_in = corner(n)
    both = p_ref[0:n, 0:n]
    turned = both.T
    left = jnp.where(rows_in >= cols_in, both, turned)
    right = jnp.where(rows_in < cols_in, both, turned)
    right = jnp.where(rows_in == cols_in, p_ref[n:n + 1, 0:n], right)
    below = p_ref[0:n, n:]
    return rows(jnp.concatenate([left, below.T], axis=1), jnp.concatenate([below, right], axis=1))


def second_step(codes, edges, low, mid, high, inner, hist, gram):
    ext, _, part = mid.shape
    count = ext - 2
    snaps = gram.shape[0]
    v = pl.BlockSpec(memory_space=pltpu.VMEM)
    sm = pl.BlockSpec(memory_space=pltpu.SMEM)

    def kernel(codes_ref, edge_ref, low_ref, mid_ref, high_ref, self_ref, side_ref, hist_ref, gram_ref, new_ref, state_ref, gram_out,
               b0, b1, b2, flat, terms):
        step_blocks(codes_ref, edge_ref, low_ref, mid_ref, high_ref, self_ref, side_ref, state_ref, b0, b1, b2)
        first = load_new(mid_ref, 1, count, flat)
        second = load_new(state_ref, 0, count, flat)
        for i in range(7):
            new_ref[pl.ds(i, count, stride=7), :] = flat[pl.ds(i, count, stride=8), :]
        row = cross_row(hist_ref, second, (first, second), terms)
        last = lax.broadcasted_iota(jnp.int32, (snaps, 1), 0) == snaps - 1
        pack(jnp.where(last, row, gram_ref[...]), gram_out)

    return pl.pallas_call(
        kernel,
        out_shape=(jax.ShapeDtypeStruct((count * 7, part), F32), jax.ShapeDtypeStruct((count, 8, part), F32),
                   jax.ShapeDtypeStruct((snaps // 2 + 8, snaps), F32)),
        in_specs=[sm, sm] + [v] * 7, out_specs=(v, v, v),
        scratch_shapes=step_scratch(ext, part) + [
            pltpu.VMEM((count * 8, part), F32), pltpu.VMEM((snaps * 8, part), F32)],
        compiler_params=pltpu.CompilerParams(vmem_limit_bytes=VMEM_LIMIT),
    )(codes, edges, low, mid, high, *inner, hist, gram)


def inner_sums(mid):
    count, _, part = mid.shape
    v = pl.BlockSpec(memory_space=pltpu.VMEM)

    def kernel(mid_ref, self_ref, side_ref):
        inner_part(mid_ref, 1, self_ref, side_ref)

    return pl.pallas_call(
        kernel, out_shape=inner_shapes(count - 2, part), in_specs=[v], out_specs=(v, v),
        compiler_params=pltpu.CompilerParams(vmem_limit_bytes=VMEM_LIMIT),
        cost_estimate=pl.CostEstimate(flops=1 << 30, bytes_accessed=1 << 20, transcendentals=0),
    )(mid)


def history_gram(hist):
    comps, snaps_old, count, part = hist.shape
    snaps = snaps_old + 2
    pitch = count + 8
    v = pl.BlockSpec(memory_space=pltpu.VMEM)

    def kernel(hist_ref, out_ref, wide):
        total = jnp.zeros((snaps_old, snaps_old), F32)
        for c in range(comps):
            def expand(s, _):
                wide[pl.ds(pl.multiple_of(pitch * s, 8), count), :] = hist_ref[c, s].astype(F32)
                return 0
            lax.fori_loop(0, snaps_old, expand, 0, unroll=max(u for u in range(1, 10) if snaps_old % u == 0))
            for b in range(0, count, 8):
                x = jnp.concatenate([wide[pl.ds(b + j, snaps_old, stride=pitch), :].astype(BF16) for j in range(8)], axis=1)
                total = total + lax.dot_general(x, x, (((1,), (1,)), ((), ())), preferred_element_type=F32)
        out_ref[...] = jnp.zeros_like(out_ref)
        out_ref[0:snaps_old, 0:snaps_old] = total

    return pl.pallas_call(
        kernel, out_shape=jax.ShapeDtypeStruct((snaps, snaps), F32),
        in_specs=[v], out_specs=v,
        scratch_shapes=[pltpu.VMEM((snaps_old * pitch, part), F32)],
        compiler_params=pltpu.CompilerParams(vmem_limit_bytes=VMEM_LIMIT),
        cost_estimate=pl.CostEstimate(flops=2 * comps * snaps * snaps * count * part, bytes_accessed=2 * comps * snaps * count * part, transcendentals=0),
    )(hist)


def early_row(hist, first, gram):
    comps, snaps_old, count, part = hist.shape
    snaps = snaps_old + 2
    v = pl.BlockSpec(memory_space=pltpu.VMEM)

    def kernel(hist_ref, first_ref, gram_ref, out_ref, flat, terms):
        out_ref[...] = gram_ref[...]
        new = load_new(first_ref, 1, count, flat)
        out_ref[snaps_old:snaps_old + 1] = cross_row(hist_ref, new, (new,), terms)

    return pl.pallas_call(
        kernel, out_shape=jax.ShapeDtypeStruct((snaps, snaps), F32),
        in_specs=[v, v, v], out_specs=v,
        scratch_shapes=[pltpu.VMEM((count * 8, part), F32), pltpu.VMEM((snaps * 8, part), F32)],
        compiler_params=pltpu.CompilerParams(vmem_limit_bytes=VMEM_LIMIT),
        cost_estimate=pl.CostEstimate(flops=1 << 30, bytes_accessed=2 * comps * snaps * count * part, transcendentals=0),
    )(hist, first, gram)


HIGHEST = lax.Precision.HIGHEST
REPEAT_BELOW = 1e-5
JOIN_ABOVE = 1e-4


def gram_of(m):
    return lax.dot_general(m, m, (((1,), (1,)), ((), ())), precision=HIGHEST, preferred_element_type=F32)


def orthonormal(m):
    n, wide = m.shape
    nb = n // 8
    s = gram_of(m)
    s = jnp.concatenate([s, jnp.zeros((n, wide - n), F32)], axis=1)
    sb = [s[8 * k:8 * k + 8] for k in range(nb)]
    mb = [m[8 * k:8 * k + 8] for k in range(nb)]
    sub = lax.broadcasted_iota(jnp.int32, (8, wide), 0)
    full = lambda x: jnp.broadcast_to(x, (8, wide))
    worst = None
    for k in range(nb):
        p = 8 * k
        norm0 = jnp.sum(m[8 * k:8 * k + 8] * m[8 * k:8 * k + 8], axis=1, keepdims=True)
        rs = [full(sb[k][i:i + 1]) for i in range(8)]
        rm = [full(mb[k][i:i + 1]) for i in range(8)]
        e = [[full(rs[i][:, p + j:p + j + 1]) for j in range(i + 1)] for i in range(8)]
        cols = [[full(sb[t][:, p + j:p + j + 1]) for j in range(8)] for t in range(k + 1, nb)]
        inv, low = [], [[None] * 8 for _ in range(8)]
        for j in range(8):
            inv.append(1.0 / e[j][j])
            for i in range(j + 1, 8):
                for t in range(j + 1, i + 1):
                    e[i][t] = e[i][t] - (e[i][j] * e[t][j]) * inv[j]
            for i in range(j + 1, 8):
                low[i][j] = e[i][j] * inv[j]
            for i in range(j + 1, 8):
                rs[i] = rs[i] - low[i][j] * rs[j]
                rm[i] = rm[i] - low[i][j] * rm[j]
        d = e[0][0]
        out = rm[0]
        for i in range(1, 8):
            d = jnp.where(sub == i, e[i][i], d)
            out = jnp.where(sub == i, rm[i], out)
        mb[k] = out * lax.rsqrt(d)
        ratio = d / norm0
        worst = ratio if worst is None else jnp.minimum(worst, ratio)
        if k == nb - 1:
            break
        us = [rs[j] * inv[j] for j in range(8)]
        um = [rm[j] * inv[j] for j in range(8)]
        for t in range(k + 1, nb):
            c = cols[t - k - 1]
            for j in range(8):
                for i in range(j + 1, 8):
                    c[i] = c[i] - low[i][j] * c[j]
                sb[t] = sb[t] - c[j] * us[j]
                mb[t] = mb[t] - c[j] * um[j]
    return jnp.concatenate(mb, 0), worst


def repeated(m, q_ref):
    q, worst = orthonormal(m)
    q_ref[...] = q

    @pl.when(jnp.logical_not(jnp.min(worst) >= REPEAT_BELOW))
    def _():
        q_ref[...] = orthonormal(q_ref[...])[0]


def start_basis(basis_t):
    v = pl.BlockSpec(memory_space=pltpu.VMEM)

    def kernel(b_ref, q_ref):
        repeated(b_ref[...], q_ref)

    return pl.pallas_call(
        kernel, out_shape=jax.ShapeDtypeStruct(basis_t.shape, F32), in_specs=[v], out_specs=v,
        cost_estimate=pl.CostEstimate(flops=1 << 30, bytes_accessed=1 << 20, transcendentals=0),
    )(basis_t)


def weigh(iters, packed_ref, g_ref, b_ref, q_ref):
    snaps = g_ref.shape[0]
    rows_in, cols_in = corner(snaps)
    g = unpack(packed_ref)
    trace = jnp.sum(jnp.where(rows_in == cols_in, g, 0.0), axis=(0, 1), keepdims=True)
    g_ref[...] = g * (1.0 / trace)
    q_ref[...] = b_ref[...]

    def product(q):
        return jnp.dot(q, g_ref[...], precision=HIGHEST, preferred_element_type=F32)

    q, checks = b_ref[...], []
    for k in range(iters - 1):
        q = product(q) if k < iters - 2 else product(product(q))
        q, worst = orthonormal(q)
        checks.append(worst * (1.0 / (REPEAT_BELOW if k < iters - 2 else JOIN_ABOVE)))
    good = jnp.min(functools.reduce(jnp.minimum, checks)) >= 1.0
    q_ref[...] = q

    @pl.when(jnp.logical_not(good))
    def _():
        q_ref[...] = b_ref[...]

        def iterate(i, _):
            repeated(product(q_ref[...]), q_ref)
            return 0

        lax.fori_loop(0, iters, iterate, 0)

    q = q_ref[...]
    last = (lax.broadcasted_iota(jnp.int32, (1, snaps), 1) == snaps - 1).astype(F32)
    w = jnp.zeros((1, snaps), F32)
    for _ in range(3):
        y = jnp.sum(q * (last - w), axis=1, keepdims=True)
        w = w + jnp.sum(q * y, axis=0, keepdims=True)
    return w


def filtered_field(gram, basis_t, hist, first, second):
    comps, snaps_old, count, part = hist.shape
    v = pl.BlockSpec(memory_space=pltpu.VMEM)

    def kernel(gram_ref, b_ref, hist_ref, first_ref, second_ref, out_ref, g_ref, q_ref, flat, table):
        w = weigh(POD_ITERS, gram_ref, g_ref, b_ref, q_ref)
        table[...] = jnp.broadcast_to(w, table.shape).T
        start = []
        for k, (ref, skip) in enumerate(((first_ref, 1), (second_ref, 0))):
            wk = table[snaps_old + k:snaps_old + k + 1]
            new = [wk * x for x in load_new(ref, skip, count, flat)]
            start = [x + y for x, y in zip(start, new)] if start else new

        def one(s, total):
            wk = table[pl.ds(s, 1), :]
            return [total[c] + wk * hist_ref[c, s].astype(F32) for c in range(comps)]
        total = lax.fori_loop(0, snaps_old, one, start, unroll=max(u for u in range(1, 10) if snaps_old % u == 0))
        for c in range(comps):
            out_ref[pl.ds(c, count, stride=comps), :] = total[c]

    return pl.pallas_call(
        kernel, out_shape=jax.ShapeDtypeStruct((count * comps, part), F32),
        in_specs=[v, v, v, v, v], out_specs=v,
        scratch_shapes=[pltpu.VMEM((snaps_old + 2, snaps_old + 2), F32), pltpu.VMEM(basis_t.shape, F32),
                        pltpu.VMEM((count * 8, part), F32), pltpu.VMEM((snaps_old + 2, snaps_old + 2), F32)],
        compiler_params=pltpu.CompilerParams(vmem_limit_bytes=VMEM_LIMIT),
    )(gram, basis_t, hist, first, second)


def shift(x, axis, by):
    count = lax.axis_size(axis)
    return lax.ppermute(x, axis, [(i, (i + by) % count) for i in range(count)])


def reduce_all(x):
    axes = ("stream", "vert")
    sizes = [lax.axis_size(a) for a in axes]
    if any(n & (n - 1) for n in sizes):
        return lax.psum(x, axes)
    bits = [(0, 1 << k) for k in range(sizes[1].bit_length() - 1)] + [(1 << k, 0) for k in range(sizes[0].bit_length() - 1)]
    start = len(bits) % 2
    for group in [bits[0:start]] * start + [bits[k:k + 2] for k in range(start, len(bits), 2)]:
        masks = [(0, 0)]
        for s, v in group:
            masks = masks + [(a ^ s, b ^ v) for a, b in masks]
        total = x
        for s, v in masks[1:]:
            total = total + lax.ppermute(x, axes, [
                (i * sizes[1] + j, (i ^ s) * sizes[1] + (j ^ v)) for i in range(sizes[0]) for j in range(sizes[1])])
        x = total
    return x


def body(particles, phase_flags, neighbours, history, basis_start):
    count = particles.shape[0]
    codes = neighbours[:, 0].T
    width = codes.shape[0]
    hist = history[:, 0].transpose(1, 2, 0, 3)
    s, v = lax.axis_index("stream"), lax.axis_index("vert")
    ns, nv = lax.axis_size("stream"), lax.axis_size("vert")
    one = jnp.ones((), jnp.int32)
    common = [v > 0, one, v < nv - 1, s > 0, s < ns - 1]
    edges1 = jnp.stack(common + [2 * one, 0 * one, one]).astype(jnp.int32)
    edges2 = jnp.stack(common + [one, one, one]).astype(jnp.int32)
    state, lo, hi = prepare(particles[:, 0], phase_flags[:, 0], codes)
    from_low = shift(hi, "stream", 1)
    from_high = shift(lo, "stream", -1)
    mid = jnp.concatenate([from_low[0:2], state, from_high[0:2]], axis=0)
    wide_codes = jnp.concatenate(
        [from_low[2, 0:width, 0:1].astype(jnp.int32), codes, from_high[2, 0:width, 0:1].astype(jnp.int32)], axis=1)
    low_mid, high_mid = shift(mid, "vert", 1), shift(mid, "vert", -1)
    basis = start_basis(basis_start.T)
    inner, hist = lax.optimization_barrier((inner_sums(mid), hist))
    hist_gram = history_gram(hist)
    wide_codes, basis, hist_gram = lax.optimization_barrier((wide_codes, basis, hist_gram))
    first = first_step(wide_codes, edges1, low_mid, mid, high_mid, inner)
    low, high = shift(first, "vert", 1), shift(first, "vert", -1)
    inner = inner_sums(first)
    gram = early_row(hist, first, hist_gram)
    new_state, second, gram = second_step(wide_codes, edges2, low, first, high, inner, hist, gram)
    gram = reduce_all(gram)
    out = filtered_field(gram, basis, hist, first, second)
    return (new_state.reshape(count, 1, 7, -1), out.reshape(count, 1, 3, -1))


def solution(mesh):
    in_specs = (
        P("stream", "vert", None, None),
        P("stream", "vert", None),
        P("stream", "vert", None),
        P("stream", "vert", None, None, None),
        P(),
    )
    out_specs = (P("stream", "vert", None, None), P("stream", "vert", None, None))
    return jax.shard_map(body, mesh=mesh, in_specs=in_specs, out_specs=out_specs, check_vma=False)
```

```python
import functools
import math

import jax
import jax.numpy as jnp
from jax import lax
from jax.experimental import pallas as pl
from jax.experimental.pallas import tpu as pltpu
from jax.sharding import PartitionSpec as P

POD_ITERS = 4
VMEM_LIMIT = 20 << 20
SEDIMENT_EXTRA = 1.65


ALPHA_KERNEL = 21.0 / (16.0 * math.pi)
VOLUME = 1.0 / 16.0
STIFFNESS = 100.0 / 7.0
TIME_STEP = 0.02
GRAVITY = 1.0
F32, BF16 = jnp.float32, jnp.bfloat16

def pieces(x):
    a = x.astype(BF16).astype(F32)
    r = x - a
    b = r.astype(BF16).astype(F32)
    return a, b, r - b

def rows(*parts):
    return jnp.concatenate(parts, axis=0)

def row_is(*which):
    index = lax.broadcasted_iota(jnp.int32, (8, 128), 0)
    hit = index == which[0]
    for w in which[1:]:
        hit = hit | (index == w)
    return hit

def spread(row):
    return jnp.broadcast_to(row, (8, row.shape[1]))

def base_rows(state, keep):
    centred = jnp.where(row_is(0, 1, 2), state - 1.0, state)
    r, rho = spread(state[6:7]), spread(state[7:8] * keep)
    live = rho > 0.0
    mass = rho * VOLUME
    r2 = r * r
    pressure = jnp.where(live, STIFFNESS * (r2 * r2 * r2 * r - 1.0) / (jnp.where(live, rho, 1.0) * r2), 0.0)
    return jnp.where(row_is(6), mass, jnp.where(row_is(7), mass * pressure, centred)), pressure


def features(base):
    place = jnp.where(row_is(0, 1, 2), base, 0.0)
    norm = 0.25 * jnp.sum(place * place, axis=0, keepdims=True)
    speed = jnp.where(row_is(0, 1, 2), pltpu.roll(base, 5, 0), 0.0)
    flux = jnp.sum(place * speed, axis=0, keepdims=True)
    own = jnp.where(row_is(3), norm, jnp.where(row_is(4), 1.0, place))
    near = jnp.where(row_is(3), 1.0, jnp.where(row_is(4), norm, -0.5 * place))
    moved = jnp.where(row_is(0), 1.0, jnp.where(row_is(7), flux, pltpu.roll(base, 1, 0)))
    sums_a = spread(base[6:7]) * moved
    sums_b = jnp.where(row_is(0, 1, 2, 3), spread(base[7:8]) * moved, 0.0)
    return own, rows(near, sums_a, sums_b)


def prep_kernel(particles_ref, flags_ref, codes_ref, state_ref, lo_ref, hi_ref, flat):
    count = flags_ref.shape[0]
    fields = particles_ref.shape[0] // count
    for i in range(fields):
        flat[pl.ds(i, count, stride=8), :] = particles_ref[pl.ds(i, count, stride=fields), :]
    flat[pl.ds(fields, count, stride=8), :] = 1.0 + SEDIMENT_EXTRA * flags_ref[...].astype(F32)
    for b in range(count):
        state_ref[b] = flat[8 * b:8 * b + 8]
    for ref, first, edge in ((lo_ref, 0, 0), (hi_ref, count - 2, count - 1)):
        for i in range(2):
            ref[i] = flat[8 * (first + i):8 * (first + i) + 8]
        ref[2] = jnp.zeros_like(ref[2])
        ref[2, 0:codes_ref.shape[0], 0:1] = codes_ref[:, edge:edge + 1].astype(F32)


def prepare(particles, flags, codes):
    count, fields, part = particles.shape
    v = pl.BlockSpec(memory_space=pltpu.VMEM)
    rim = jax.ShapeDtypeStruct((3, 8, part), F32)
    return pl.pallas_call(
        prep_kernel,
        out_shape=(jax.ShapeDtypeStruct((count, 8, part), F32), rim, rim),
        in_specs=[v, v, v], out_specs=(v, v, v),
        scratch_shapes=[pltpu.VMEM((count * 8, part), F32)],
    )(particles.reshape(count * fields, part), flags, codes)


def own_side(own):
    o1, o2, o3 = pieces(own)
    return rows(o1, o1, o2, o2, o1, o3).astype(BF16)


def near_side(g):
    p1, p2, p3 = pieces(g[0:8])
    f1 = g[8:24].astype(BF16)
    f2 = (g[8:24] - f1.astype(F32)).astype(BF16)
    return rows(p1, p2, p1, p2, p3, p1).astype(BF16), rows(f1, f2)


def weighted_sums(group):
    width = len(group)
    zero = jnp.zeros_like(group[0][0])
    rhs = rows(*[jnp.concatenate([g[0] if m == k else zero for m in range(width)], axis=1) for k, g in enumerate(group)])
    s = lax.dot_general(rows(*[g[1] for g in group]), rhs, (((0,), (0,)), ((), ())), preferred_element_type=F32)
    s = jnp.maximum(s, 1e-20)
    k = jnp.maximum(1.0 - s * lax.rsqrt(s), 0.0)
    wgt = k * k * k
    wh = wgt.astype(BF16)
    wl = (wgt - wh.astype(F32)).astype(BF16)
    f = rows(*[jnp.concatenate([g[2], g[2]], axis=1) for g in group])
    acc = jnp.dot(f, rows(wh, wl), preferred_element_type=F32)
    part = zero.shape[1]
    cut = [acc[32 * k:32 * (k + 1), part * k:part * (k + 1)] for k in range(width)]
    return [t[0:16] + t[16:32] for t in cut]


def in_groups(count, run):
    width = 2 if count % 2 == 0 else 1
    trips = count // width

    def trip(i, _):
        run([width * i + k for k in range(width)])
        return 0
    lax.fori_loop(0, trips, trip, 0, unroll=max(u for u in range(1, 18) if trips % u == 0))


def inner_part(state_ref, skip, self_ref, side_ref):
    def run(blocks):
        group = []
        for b in blocks:
            base, pressure = base_rows(state_ref[b + skip], 1.0)
            own, g_self = features(base)
            side = own_side(own)
            side_ref[b] = side
            self_ref[b, 16:24] = pressure
            group.append((side,) + near_side(g_self))
        for b, t in zip(blocks, weighted_sums(group)):
            self_ref[b, 0:16] = t
    in_groups(self_ref.shape[0], run)


def inner_shapes(count, part):
    return (jax.ShapeDtypeStruct((count, 24, part), F32), jax.ShapeDtypeStruct((count, 48, part), BF16))


def step_blocks(codes_ref, edge_ref, low_ref, mid_ref, high_ref, self_ref, side_ref, store, base_ref):
    ext, _, part = mid_ref.shape
    count = ext - 2
    rim, skip = edge_ref[5], edge_ref[6]
    along = row_is(0).astype(F32)
    upward = row_is(2).astype(F32)

    def prep(i):
        rowon = jnp.where(i < rim, edge_ref[3], jnp.where(i >= ext - rim, edge_ref[4], 1))
        for col, ref in ((0, low_ref), (1, mid_ref), (2, high_ref)):
            base_ref[col * ext + i] = base_rows(ref[i], (edge_ref[col] * rowon).astype(F32))[0]

    for i in range(3):
        prep(i)

    def operands(b):
        st = mid_ref[b + 1]
        gs = []
        for n in range(codes_ref.shape[0]):
            c = codes_ref[n, b + skip]
            o = c + jnp.where(c >= 4, 1, 0)
            ds1 = (o * 11) >> 5
            dv1 = o - 3 * ds1
            idx = dv1 * ext + b + ds1
            tx = 2.0 * (ds1 - 1).astype(F32)
            tz = 2.0 * (dv1 - 1).astype(F32)
            gs.append(features(base_ref[idx] + (tx * along + tz * upward))[1])
        prep(jnp.minimum(b + 3, ext - 1))
        near = [near_side(g) for g in gs]
        return st, (side_ref[b],) + tuple(jnp.concatenate(x, axis=1) for x in zip(*near))

    def finish(b, st, pressure, t):
        x, vel = st[0:3] - 1.0, st[3:6]
        coef = -5.0 * ALPHA_KERNEL
        sw, swx, swv, swf = t[0:1], t[1:4], t[4:7], t[7:8]
        swp, swpx = t[8:9], t[9:12]
        dens = coef * (jnp.sum(vel * (x * sw - swx) - x * swv, axis=0, keepdims=True) + swf)
        acc3 = -coef * (pressure * (x * sw - swx) + x * swp - swpx)
        grav = jnp.where(lax.broadcasted_iota(jnp.int32, (3, 1), 0) == 2, -GRAVITY, 0.0)
        vel2 = vel + TIME_STEP * (acc3 + grav)
        pos2 = st[0:3] + TIME_STEP * vel2
        rho = st[7:8]
        r2 = st[6:7] + TIME_STEP * dens / rho
        store(b, rows(pos2, vel2, r2, rho))

    def run(blocks):
        group = [operands(b) for b in blocks]
        for b, (st, _), t in zip(blocks, group, weighted_sums([g[1] for g in group])):
            finish(b, st, self_ref[b, 16:17], t + self_ref[b, 0:16])
    in_groups(count, run)


def step_scratch(ext, part):
    return [pltpu.VMEM((3 * ext, 8, part), F32)]


def first_step(codes, edges, low, mid, high, inner):
    ext, _, part = mid.shape
    v = pl.BlockSpec(memory_space=pltpu.VMEM)
    sm = pl.BlockSpec(memory_space=pltpu.SMEM)
    def kernel(codes_ref, edge_ref, low_ref, mid_ref, high_ref, self_ref, side_ref, out_ref, base_ref):
        def store(b, value):
            out_ref[b] = value
        step_blocks(codes_ref, edge_ref, low_ref, mid_ref, high_ref, self_ref, side_ref, store, base_ref)

    return pl.pallas_call(
        kernel, out_shape=jax.ShapeDtypeStruct((ext - 2, 8, part), F32),
        in_specs=[sm, sm, v, v, v, v, v], out_specs=v,
        scratch_shapes=step_scratch(ext, part),
        compiler_params=pltpu.CompilerParams(vmem_limit_bytes=VMEM_LIMIT),
    )(codes, edges, low, mid, high, *inner)


def cross_row(hist_ref, new, others, terms):
    comps, hist = hist_ref.shape[0], hist_ref.shape[1]
    groups = new[0].shape[0] // 8

    def fold(x):
        total = x[0:8]
        for g in range(1, groups):
            total = total + x[8 * g:8 * g + 8]
        return total

    def one(s, _):
        total = hist_ref[0, s].astype(F32) * new[0]
        for c in range(1, comps):
            total = total + hist_ref[c, s].astype(F32) * new[c]
        terms[pl.ds(pl.multiple_of(8 * s, 8), 8), :] = fold(total)
        return 0
    lax.fori_loop(0, hist, one, 0, unroll=max(u for u in range(1, 10) if hist % u == 0))
    snaps = terms.shape[0] // 8
    for k in range(snaps - hist):
        if k < len(others):
            total = others[k][0] * new[0]
            for c in range(1, comps):
                total = total + others[k][c] * new[c]
            terms[8 * (hist + k):8 * (hist + k) + 8] = fold(total)
        else:
            terms[8 * (hist + k):8 * (hist + k) + 8] = jnp.zeros_like(terms[0:8])
    by_snap = terms[pl.ds(0, snaps, stride=8), :]
    for i in range(1, 8):
        by_snap = by_snap + terms[pl.ds(i, snaps, stride=8), :]
    ones = jnp.ones((8, by_snap.shape[1]), F32)
    return lax.dot_general(ones, by_snap, (((1,), (1,)), ((), ())), precision=HIGHEST, preferred_element_type=F32)[0:1]


def new_snapshot(flat, count):
    return [flat[pl.ds(3 + c, count, stride=8), :].astype(BF16).astype(F32) for c in range(3)]


def corner(n):
    rows_in = lax.broadcasted_iota(jnp.int32, (n, n), 0)
    cols_in = lax.broadcasted_iota(jnp.int32, (n, n), 1)
    return rows_in, cols_in


def pack(g, out_ref):
    n = g.shape[0] // 2
    rows_in, cols_in = corner(n)
    right = g[n:, n:]
    out_ref[0:n, 0:n] = jnp.where(rows_in >= cols_in, g[0:n, 0:n], right.T)
    out_ref[0:n, n:] = g[n:, 0:n]
    diagonal = jnp.sum(jnp.where(rows_in == cols_in, right, 0.0), axis=0, keepdims=True)
    out_ref[n:] = jnp.broadcast_to(jnp.concatenate([diagonal, diagonal], axis=1), (8, 2 * n))


def unpack(p_ref):
    n = p_ref.shape[1] // 2
    rows_in, cols_in = corner(n)
    both = p_ref[0:n, 0:n]
    turned = both.T
    left = jnp.where(rows_in >= cols_in, both, turned)
    right = jnp.where(rows_in < cols_in, both, turned)
    right = jnp.where(rows_in == cols_in, p_ref[n:n + 1, 0:n], right)
    below = p_ref[0:n, n:]
    return rows(jnp.concatenate([left, below.T], axis=1), jnp.concatenate([below, right], axis=1))


def second_step(codes, edges, low, mid, high, inner, hist, first, gram):
    ext, _, part = mid.shape
    count = ext - 2
    snaps = gram.shape[0]
    v = pl.BlockSpec(memory_space=pltpu.VMEM)
    sm = pl.BlockSpec(memory_space=pltpu.SMEM)

    def kernel(codes_ref, edge_ref, low_ref, mid_ref, high_ref, self_ref, side_ref, hist_ref, first_ref, gram_ref,
               new_ref, second_ref, gram_out, base_ref, flat, terms):
        def store(b, value):
            flat[pl.ds(pl.multiple_of(8 * b, 8), 8), :] = value
        step_blocks(codes_ref, edge_ref, low_ref, mid_ref, high_ref, self_ref, side_ref, store, base_ref)
        first = [first_ref[count * c:count * (c + 1)] for c in range(3)]
        second = new_snapshot(flat, count)
        for c in range(3):
            second_ref[count * c:count * (c + 1)] = second[c]
        for i in range(7):
            new_ref[pl.ds(i, count, stride=7), :] = flat[pl.ds(i, count, stride=8), :]
        row = cross_row(hist_ref, second, (first, second), terms)
        last = lax.broadcasted_iota(jnp.int32, (snaps, 1), 0) == snaps - 1
        pack(jnp.where(last, row, gram_ref[...]), gram_out)

    return pl.pallas_call(
        kernel,
        out_shape=(jax.ShapeDtypeStruct((count * 7, part), F32), jax.ShapeDtypeStruct(first.shape, F32),
                   jax.ShapeDtypeStruct((snaps // 2 + 8, snaps), F32)),
        in_specs=[sm, sm] + [v] * 8, out_specs=(v, v, v),
        scratch_shapes=step_scratch(ext, part) + [
            pltpu.VMEM((count * 8, part), F32), pltpu.VMEM((snaps * 8, part), F32)],
        compiler_params=pltpu.CompilerParams(vmem_limit_bytes=VMEM_LIMIT),
    )(codes, edges, low, mid, high, *inner, hist, first, gram)


def inner_sums(mid):
    count, _, part = mid.shape
    v = pl.BlockSpec(memory_space=pltpu.VMEM)

    def kernel(mid_ref, self_ref, side_ref):
        inner_part(mid_ref, 1, self_ref, side_ref)

    return pl.pallas_call(
        kernel, out_shape=inner_shapes(count - 2, part), in_specs=[v], out_specs=(v, v),
        compiler_params=pltpu.CompilerParams(vmem_limit_bytes=VMEM_LIMIT),
        cost_estimate=pl.CostEstimate(flops=1 << 30, bytes_accessed=1 << 20, transcendentals=0),
    )(mid)


def history_gram(hist):
    comps, snaps_old, count, part = hist.shape
    snaps = snaps_old + 2
    pitch = count + 8
    v = pl.BlockSpec(memory_space=pltpu.VMEM)

    def kernel(hist_ref, out_ref, wide):
        total = jnp.zeros((snaps_old, snaps_old), F32)
        for c in range(comps):
            def expand(s, _):
                wide[pl.ds(pl.multiple_of(pitch * s, 8), count), :] = hist_ref[c, s].astype(F32)
                return 0
            lax.fori_loop(0, snaps_old, expand, 0, unroll=max(u for u in range(1, 10) if snaps_old % u == 0))
            for b in range(0, count, 8):
                x = jnp.concatenate([wide[pl.ds(b + j, snaps_old, stride=pitch), :].astype(BF16) for j in range(8)], axis=1)
                total = total + lax.dot_general(x, x, (((1,), (1,)), ((), ())), preferred_element_type=F32)
        out_ref[...] = jnp.zeros_like(out_ref)
        out_ref[0:snaps_old, 0:snaps_old] = total

    return pl.pallas_call(
        kernel, out_shape=jax.ShapeDtypeStruct((snaps, snaps), F32),
        in_specs=[v], out_specs=v,
        scratch_shapes=[pltpu.VMEM((snaps_old * pitch, part), F32)],
        compiler_params=pltpu.CompilerParams(vmem_limit_bytes=VMEM_LIMIT),
        cost_estimate=pl.CostEstimate(flops=2 * comps * snaps * snaps * count * part, bytes_accessed=2 * comps * snaps * count * part, transcendentals=0),
    )(hist)


def early_row(hist, first, gram):
    comps, snaps_old, count, part = hist.shape
    snaps = snaps_old + 2
    v = pl.BlockSpec(memory_space=pltpu.VMEM)

    def kernel(hist_ref, first_ref, gram_ref, out_ref, new_ref, flat, terms):
        out_ref[...] = gram_ref[...]
        for b in range(count):
            flat[8 * b:8 * b + 8] = first_ref[b + 1]
        new = new_snapshot(flat, count)
        for c in range(3):
            new_ref[count * c:count * (c + 1)] = new[c]
        out_ref[snaps_old:snaps_old + 1] = cross_row(hist_ref, new, (new,), terms)

    return pl.pallas_call(
        kernel, out_shape=(jax.ShapeDtypeStruct((snaps, snaps), F32), jax.ShapeDtypeStruct((count * 3, part), F32)),
        in_specs=[v, v, v], out_specs=(v, v),
        scratch_shapes=[pltpu.VMEM((count * 8, part), F32), pltpu.VMEM((snaps * 8, part), F32)],
        compiler_params=pltpu.CompilerParams(vmem_limit_bytes=VMEM_LIMIT),
        cost_estimate=pl.CostEstimate(flops=1 << 30, bytes_accessed=2 * comps * snaps * count * part, transcendentals=0),
    )(hist, first, gram)


HIGHEST = lax.Precision.HIGHEST
REPEAT_BELOW = 1e-5
JOIN_ABOVE = 1e-4


def gram_of(m):
    return lax.dot_general(m, m, (((1,), (1,)), ((), ())), precision=HIGHEST, preferred_element_type=F32)


def orthonormal(m):
    n, wide = m.shape
    nb = n // 8
    s = gram_of(m)
    s = jnp.concatenate([s, jnp.zeros((n, wide - n), F32)], axis=1)
    sb = [s[8 * k:8 * k + 8] for k in range(nb)]
    mb = [m[8 * k:8 * k + 8] for k in range(nb)]
    sub = lax.broadcasted_iota(jnp.int32, (8, wide), 0)
    full = lambda x: jnp.broadcast_to(x, (8, wide))
    worst = None
    for k in range(nb):
        p = 8 * k
        norm0 = jnp.sum(m[8 * k:8 * k + 8] * m[8 * k:8 * k + 8], axis=1, keepdims=True)
        rs = [full(sb[k][i:i + 1]) for i in range(8)]
        rm = [full(mb[k][i:i + 1]) for i in range(8)]
        e = [[full(rs[i][:, p + j:p + j + 1]) for j in range(i + 1)] for i in range(8)]
        cols = [[full(sb[t][:, p + j:p + j + 1]) for j in range(8)] for t in range(k + 1, nb)]
        inv, low = [], [[None] * 8 for _ in range(8)]
        for j in range(8):
            inv.append(1.0 / e[j][j])
            for i in range(j + 1, 8):
                for t in range(j + 1, i + 1):
                    e[i][t] = e[i][t] - (e[i][j] * e[t][j]) * inv[j]
            for i in range(j + 1, 8):
                low[i][j] = e[i][j] * inv[j]
            for i in range(j + 1, 8):
                rs[i] = rs[i] - low[i][j] * rs[j]
                rm[i] = rm[i] - low[i][j] * rm[j]
        d = e[0][0]
        out = rm[0]
        for i in range(1, 8):
            d = jnp.where(sub == i, e[i][i], d)
            out = jnp.where(sub == i, rm[i], out)
        mb[k] = out * lax.rsqrt(d)
        ratio = d / norm0
        worst = ratio if worst is None else jnp.minimum(worst, ratio)
        if k == nb - 1:
            break
        us = [rs[j] * inv[j] for j in range(8)]
        um = [rm[j] * inv[j] for j in range(8)]
        for t in range(k + 1, nb):
            c = cols[t - k - 1]
            for j in range(8):
                for i in range(j + 1, 8):
                    c[i] = c[i] - low[i][j] * c[j]
                sb[t] = sb[t] - c[j] * us[j]
                mb[t] = mb[t] - c[j] * um[j]
    return jnp.concatenate(mb, 0), worst


def repeated(m, q_ref):
    q, worst = orthonormal(m)
    q_ref[...] = q

    @pl.when(jnp.logical_not(jnp.min(worst) >= REPEAT_BELOW))
    def _():
        q_ref[...] = orthonormal(q_ref[...])[0]


def start_basis(basis_t):
    v = pl.BlockSpec(memory_space=pltpu.VMEM)

    def kernel(b_ref, q_ref):
        repeated(b_ref[...], q_ref)

    return pl.pallas_call(
        kernel, out_shape=jax.ShapeDtypeStruct(basis_t.shape, F32), in_specs=[v], out_specs=v,
        cost_estimate=pl.CostEstimate(flops=1 << 30, bytes_accessed=1 << 20, transcendentals=0),
    )(basis_t)


def weigh(iters, packed_ref, g_ref, b_ref, q_ref):
    snaps = g_ref.shape[0]
    rows_in, cols_in = corner(snaps)
    g = unpack(packed_ref)
    trace = jnp.sum(jnp.where(rows_in == cols_in, g, 0.0), axis=(0, 1), keepdims=True)
    g_ref[...] = g * (1.0 / trace)
    q_ref[...] = b_ref[...]

    def product(q):
        return jnp.dot(q, g_ref[...], precision=HIGHEST, preferred_element_type=F32)

    q, checks = b_ref[...], []
    for k in range(iters - 1):
        q = product(q) if k < iters - 2 else product(product(q))
        q, worst = orthonormal(q)
        checks.append(worst * (1.0 / (REPEAT_BELOW if k < iters - 2 else JOIN_ABOVE)))
    good = jnp.min(functools.reduce(jnp.minimum, checks)) >= 1.0
    q_ref[...] = q

    @pl.when(jnp.logical_not(good))
    def _():
        q_ref[...] = b_ref[...]

        def iterate(i, _):
            repeated(product(q_ref[...]), q_ref)
            return 0

        lax.fori_loop(0, iters, iterate, 0)

    q = q_ref[...]
    last = (lax.broadcasted_iota(jnp.int32, (1, snaps), 1) == snaps - 1).astype(F32)
    w = jnp.zeros((1, snaps), F32)
    for _ in range(3):
        y = jnp.sum(q * (last - w), axis=1, keepdims=True)
        w = w + jnp.sum(q * y, axis=0, keepdims=True)
    return w


def filtered_field(gram, basis_t, hist, first, second):
    comps, snaps_old, count, part = hist.shape
    v = pl.BlockSpec(memory_space=pltpu.VMEM)

    def kernel(gram_ref, b_ref, hist_ref, first_ref, second_ref, out_ref, g_ref, q_ref, table):
        w = weigh(POD_ITERS, gram_ref, g_ref, b_ref, q_ref)
        table[...] = jnp.broadcast_to(w, table.shape).T
        w1, w2 = (table[snaps_old + k:snaps_old + k + 1] for k in range(2))
        parts = [slice(count * c, count * (c + 1)) for c in range(comps)]
        start = [w1 * first_ref[p] + w2 * second_ref[p] for p in parts]

        def one(s, total):
            wk = table[pl.ds(s, 1), :]
            return [total[c] + wk * hist_ref[c, s].astype(F32) for c in range(comps)]
        total = lax.fori_loop(0, snaps_old, one, start, unroll=max(u for u in range(1, 10) if snaps_old % u == 0))
        for c in range(comps):
            out_ref[pl.ds(c, count, stride=comps), :] = total[c]

    return pl.pallas_call(
        kernel, out_shape=jax.ShapeDtypeStruct((count * comps, part), F32),
        in_specs=[v, v, v, v, v], out_specs=v,
        scratch_shapes=[pltpu.VMEM((snaps_old + 2, snaps_old + 2), F32), pltpu.VMEM(basis_t.shape, F32),
                        pltpu.VMEM((snaps_old + 2, snaps_old + 2), F32)],
        compiler_params=pltpu.CompilerParams(vmem_limit_bytes=VMEM_LIMIT),
    )(gram, basis_t, hist, first, second)


def shift(x, axis, by):
    count = lax.axis_size(axis)
    return lax.ppermute(x, axis, [(i, (i + by) % count) for i in range(count)])


def reduce_all(x):
    axes = ("stream", "vert")
    sizes = [lax.axis_size(a) for a in axes]
    if any(n & (n - 1) for n in sizes):
        return lax.psum(x, axes)
    bits = [(0, 1 << k) for k in range(sizes[1].bit_length() - 1)] + [(1 << k, 0) for k in range(sizes[0].bit_length() - 1)]
    start = len(bits) % 2
    for group in [bits[0:start]] * start + [bits[k:k + 2] for k in range(start, len(bits), 2)]:
        masks = [(0, 0)]
        for s, v in group:
            masks = masks + [(a ^ s, b ^ v) for a, b in masks]
        total = x
        for s, v in masks[1:]:
            total = total + lax.ppermute(x, axes, [
                (i * sizes[1] + j, (i ^ s) * sizes[1] + (j ^ v)) for i in range(sizes[0]) for j in range(sizes[1])])
        x = total
    return x


def body(particles, phase_flags, neighbours, history, basis_start):
    count = particles.shape[0]
    codes = neighbours[:, 0].T
    width = codes.shape[0]
    hist = history[:, 0].transpose(1, 2, 0, 3)
    s, v = lax.axis_index("stream"), lax.axis_index("vert")
    ns, nv = lax.axis_size("stream"), lax.axis_size("vert")
    one = jnp.ones((), jnp.int32)
    common = [v > 0, one, v < nv - 1, s > 0, s < ns - 1]
    edges1 = jnp.stack(common + [2 * one, 0 * one, one]).astype(jnp.int32)
    edges2 = jnp.stack(common + [one, one, one]).astype(jnp.int32)
    state, lo, hi = prepare(particles[:, 0], phase_flags[:, 0], codes)
    from_low = shift(hi, "stream", 1)
    from_high = shift(lo, "stream", -1)
    mid = jnp.concatenate([from_low[0:2], state, from_high[0:2]], axis=0)
    wide_codes = jnp.concatenate(
        [from_low[2, 0:width, 0:1].astype(jnp.int32), codes, from_high[2, 0:width, 0:1].astype(jnp.int32)], axis=1)
    low_mid, high_mid = shift(mid, "vert", 1), shift(mid, "vert", -1)
    basis = start_basis(basis_start.T)
    inner, hist = lax.optimization_barrier((inner_sums(mid), hist))
    hist_gram = history_gram(hist)
    wide_codes, basis, hist_gram = lax.optimization_barrier((wide_codes, basis, hist_gram))
    first = first_step(wide_codes, edges1, low_mid, mid, high_mid, inner)
    low, high = shift(first, "vert", 1), shift(first, "vert", -1)
    inner = inner_sums(first)
    gram, first_new = early_row(hist, first, hist_gram)
    new_state, second_new, gram = second_step(wide_codes, edges2, low, first, high, inner, hist, first_new, gram)
    gram = reduce_all(gram)
    out = filtered_field(gram, basis, hist, first_new, second_new)
    return (new_state.reshape(count, 1, 7, -1), out.reshape(count, 1, 3, -1))


def solution(mesh):
    in_specs = (
        P("stream", "vert", None, None),
        P("stream", "vert", None),
        P("stream", "vert", None),
        P("stream", "vert", None, None, None),
        P(),
    )
    out_specs = (P("stream", "vert", None, None), P("stream", "vert", None, None))
    return jax.shard_map(body, mesh=mesh, in_specs=in_specs, out_specs=out_specs, check_vma=False)
```

```python
import functools
import math

import jax
import jax.numpy as jnp
from jax import lax
from jax.experimental import pallas as pl
from jax.experimental.pallas import tpu as pltpu
from jax.sharding import PartitionSpec as P

POD_ITERS = 4
VMEM_LIMIT = 20 << 20
SEDIMENT_EXTRA = 1.65


ALPHA_KERNEL = 21.0 / (16.0 * math.pi)
VOLUME = 1.0 / 16.0
STIFFNESS = 100.0 / 7.0
TIME_STEP = 0.02
GRAVITY = 1.0
F32, BF16 = jnp.float32, jnp.bfloat16

def pieces(x):
    a = x.astype(BF16).astype(F32)
    r = x - a
    b = r.astype(BF16).astype(F32)
    return a, b, r - b

def rows(*parts):
    return jnp.concatenate(parts, axis=0)

def row_is(*which):
    index = lax.broadcasted_iota(jnp.int32, (8, 128), 0)
    hit = index == which[0]
    for w in which[1:]:
        hit = hit | (index == w)
    return hit

def spread(row):
    return jnp.broadcast_to(row, (8, row.shape[1]))

def base_rows(state, keep):
    centred = jnp.where(row_is(0, 1, 2), state - 1.0, state)
    r, rho = spread(state[6:7]), spread(state[7:8] * keep)
    live = rho > 0.0
    mass = rho * VOLUME
    r2 = r * r
    pressure = jnp.where(live, STIFFNESS * (r2 * r2 * r2 * r - 1.0) / (jnp.where(live, rho, 1.0) * r2), 0.0)
    return jnp.where(row_is(6), mass, jnp.where(row_is(7), mass * pressure, centred)), pressure


def features(base):
    place = jnp.where(row_is(0, 1, 2), base, 0.0)
    norm = 0.25 * jnp.sum(place * place, axis=0, keepdims=True)
    speed = jnp.where(row_is(0, 1, 2), pltpu.roll(base, 5, 0), 0.0)
    flux = jnp.sum(place * speed, axis=0, keepdims=True)
    own = jnp.where(row_is(3), norm, jnp.where(row_is(4), 1.0, place))
    near = jnp.where(row_is(3), 1.0, jnp.where(row_is(4), norm, -0.5 * place))
    moved = jnp.where(row_is(0), 1.0, jnp.where(row_is(7), flux, pltpu.roll(base, 1, 0)))
    sums_a = spread(base[6:7]) * moved
    sums_b = jnp.where(row_is(0, 1, 2, 3), spread(base[7:8]) * moved, 0.0)
    return own, rows(near, sums_a, sums_b)


def prep_kernel(particles_ref, flags_ref, codes_ref, state_ref, lo_ref, hi_ref, flat):
    count = flags_ref.shape[0]
    fields = particles_ref.shape[0] // count
    for i in range(fields):
        flat[pl.ds(i, count, stride=8), :] = particles_ref[pl.ds(i, count, stride=fields), :]
    flat[pl.ds(fields, count, stride=8), :] = 1.0 + SEDIMENT_EXTRA * flags_ref[...].astype(F32)
    for b in range(count):
        state_ref[b] = flat[8 * b:8 * b + 8]
    for ref, first, edge in ((lo_ref, 0, 0), (hi_ref, count - 2, count - 1)):
        for i in range(2):
            ref[i] = flat[8 * (first + i):8 * (first + i) + 8]
        ref[2] = jnp.zeros_like(ref[2])
        ref[2, 0:codes_ref.shape[0], 0:1] = codes_ref[:, edge:edge + 1].astype(F32)


def prepare(particles, flags, codes):
    count, fields, part = particles.shape
    v = pl.BlockSpec(memory_space=pltpu.VMEM)
    rim = jax.ShapeDtypeStruct((3, 8, part), F32)
    return pl.pallas_call(
        prep_kernel,
        out_shape=(jax.ShapeDtypeStruct((count, 8, part), F32), rim, rim),
        in_specs=[v, v, v], out_specs=(v, v, v),
        scratch_shapes=[pltpu.VMEM((count * 8, part), F32)],
    )(particles.reshape(count * fields, part), flags, codes)


def own_side(own):
    o1, o2, o3 = pieces(own)
    return rows(o1, o1, o2, o2, o1, o3).astype(BF16)


def near_side(g):
    p1, p2, p3 = pieces(g[0:8])
    f1 = g[8:24].astype(BF16)
    f2 = (g[8:24] - f1.astype(F32)).astype(BF16)
    return rows(p1, p2, p1, p2, p3, p1).astype(BF16), rows(f1, f2)


def weighted_sums(group):
    width = len(group)
    zero = jnp.zeros_like(group[0][0])
    rhs = rows(*[jnp.concatenate([g[0] if m == k else zero for m in range(width)], axis=1) for k, g in enumerate(group)])
    s = lax.dot_general(rows(*[g[1] for g in group]), rhs, (((0,), (0,)), ((), ())), preferred_element_type=F32)
    s = jnp.maximum(s, 1e-20)
    k = jnp.maximum(1.0 - s * lax.rsqrt(s), 0.0)
    wgt = k * k * k
    wh = wgt.astype(BF16)
    wl = (wgt - wh.astype(F32)).astype(BF16)
    f = rows(*[jnp.concatenate([g[2], g[2]], axis=1) for g in group])
    acc = jnp.dot(f, rows(wh, wl), preferred_element_type=F32)
    part = zero.shape[1]
    cut = [acc[32 * k:32 * (k + 1), part * k:part * (k + 1)] for k in range(width)]
    return [t[0:16] + t[16:32] for t in cut]


def in_groups(count, run):
    width = 2 if count % 2 == 0 else 1
    trips = count // width

    def trip(i, _):
        run([width * i + k for k in range(width)])
        return 0
    lax.fori_loop(0, trips, trip, 0, unroll=max(u for u in range(1, 18) if trips % u == 0))


def inner_part(state_ref, skip, self_ref, side_ref):
    def run(blocks):
        group = []
        for b in blocks:
            base, pressure = base_rows(state_ref[b + skip], 1.0)
            own, g_self = features(base)
            side = own_side(own)
            side_ref[b] = side
            self_ref[b, 16:24] = pressure
            group.append((side,) + near_side(g_self))
        for b, t in zip(blocks, weighted_sums(group)):
            self_ref[b, 0:16] = t
    in_groups(self_ref.shape[0], run)


def inner_shapes(count, part):
    return (jax.ShapeDtypeStruct((count, 24, part), F32), jax.ShapeDtypeStruct((count, 48, part), BF16))


def step_blocks(codes_ref, edge_ref, low_ref, mid_ref, high_ref, self_ref, side_ref, store, base_ref):
    ext, _, part = mid_ref.shape
    count = ext - 2
    rim, skip = edge_ref[5], edge_ref[6]
    along = row_is(0).astype(F32)
    upward = row_is(2).astype(F32)

    def prep(i):
        rowon = jnp.where(i < rim, edge_ref[3], jnp.where(i >= ext - rim, edge_ref[4], 1))
        for col, ref in ((0, low_ref), (1, mid_ref), (2, high_ref)):
            base_ref[col * ext + i] = base_rows(ref[i], (edge_ref[col] * rowon).astype(F32))[0]

    for i in range(3):
        prep(i)

    def operands(b):
        st = mid_ref[b + 1]
        gs = []
        for n in range(codes_ref.shape[0]):
            c = codes_ref[n, b + skip]
            o = c + jnp.where(c >= 4, 1, 0)
            ds1 = (o * 11) >> 5
            dv1 = o - 3 * ds1
            idx = dv1 * ext + b + ds1
            tx = 2.0 * (ds1 - 1).astype(F32)
            tz = 2.0 * (dv1 - 1).astype(F32)
            gs.append(features(base_ref[idx] + (tx * along + tz * upward))[1])
        prep(jnp.minimum(b + 3, ext - 1))
        near = [near_side(g) for g in gs]
        return st, (side_ref[b],) + tuple(jnp.concatenate(x, axis=1) for x in zip(*near))

    def finish(b, st, pressure, t):
        x, vel = st[0:3] - 1.0, st[3:6]
        coef = -5.0 * ALPHA_KERNEL
        sw, swx, swv, swf = t[0:1], t[1:4], t[4:7], t[7:8]
        swp, swpx = t[8:9], t[9:12]
        dens = coef * (jnp.sum(vel * (x * sw - swx) - x * swv, axis=0, keepdims=True) + swf)
        acc3 = -coef * (pressure * (x * sw - swx) + x * swp - swpx)
        grav = jnp.where(lax.broadcasted_iota(jnp.int32, (3, 1), 0) == 2, -GRAVITY, 0.0)
        vel2 = vel + TIME_STEP * (acc3 + grav)
        pos2 = st[0:3] + TIME_STEP * vel2
        rho = st[7:8]
        r2 = st[6:7] + TIME_STEP * dens / rho
        store(b, rows(pos2, vel2, r2, rho))

    def run(blocks):
        group = [operands(b) for b in blocks]
        for b, (st, _), t in zip(blocks, group, weighted_sums([g[1] for g in group])):
            finish(b, st, self_ref[b, 16:17], t + self_ref[b, 0:16])
    in_groups(count, run)


def step_scratch(ext, part):
    return [pltpu.VMEM((3 * ext, 8, part), F32)]


def first_step(codes, edges, low, mid, high, inner):
    ext, _, part = mid.shape
    v = pl.BlockSpec(memory_space=pltpu.VMEM)
    sm = pl.BlockSpec(memory_space=pltpu.SMEM)
    def kernel(codes_ref, edge_ref, low_ref, mid_ref, high_ref, self_ref, side_ref, out_ref, base_ref):
        def store(b, value):
            out_ref[b] = value
        step_blocks(codes_ref, edge_ref, low_ref, mid_ref, high_ref, self_ref, side_ref, store, base_ref)

    return pl.pallas_call(
        kernel, out_shape=jax.ShapeDtypeStruct((ext - 2, 8, part), F32),
        in_specs=[sm, sm, v, v, v, v, v], out_specs=v,
        scratch_shapes=step_scratch(ext, part),
        compiler_params=pltpu.CompilerParams(vmem_limit_bytes=VMEM_LIMIT),
    )(codes, edges, low, mid, high, *inner)


def cross_row(hist_ref, new, others, terms):
    comps, hist = hist_ref.shape[0], hist_ref.shape[1]
    groups = new[0].shape[0] // 8

    def fold(x):
        total = x[0:8]
        for g in range(1, groups):
            total = total + x[8 * g:8 * g + 8]
        return total

    def one(s, _):
        total = hist_ref[0, s].astype(F32) * new[0]
        for c in range(1, comps):
            total = total + hist_ref[c, s].astype(F32) * new[c]
        terms[pl.ds(pl.multiple_of(8 * s, 8), 8), :] = fold(total)
        return 0
    lax.fori_loop(0, hist, one, 0, unroll=max(u for u in range(1, 43) if hist % u == 0))
    snaps = terms.shape[0] // 8
    for k in range(snaps - hist):
        if k < len(others):
            total = others[k][0] * new[0]
            for c in range(1, comps):
                total = total + others[k][c] * new[c]
            terms[8 * (hist + k):8 * (hist + k) + 8] = fold(total)
        else:
            terms[8 * (hist + k):8 * (hist + k) + 8] = jnp.zeros_like(terms[0:8])
    by_snap = terms[pl.ds(0, snaps, stride=8), :]
    for i in range(1, 8):
        by_snap = by_snap + terms[pl.ds(i, snaps, stride=8), :]
    ones = jnp.ones((8, by_snap.shape[1]), F32)
    return lax.dot_general(ones, by_snap, (((1,), (1,)), ((), ())), precision=HIGHEST, preferred_element_type=F32)[0:1]


def new_snapshot(flat, count):
    return [flat[pl.ds(3 + c, count, stride=8), :].astype(BF16).astype(F32) for c in range(3)]


def corner(n):
    rows_in = lax.broadcasted_iota(jnp.int32, (n, n), 0)
    cols_in = lax.broadcasted_iota(jnp.int32, (n, n), 1)
    return rows_in, cols_in


def pack(g, out_ref):
    n = g.shape[0] // 2
    rows_in, cols_in = corner(n)
    right = g[n:, n:]
    out_ref[0:n, 0:n] = jnp.where(rows_in >= cols_in, g[0:n, 0:n], right.T)
    out_ref[0:n, n:] = g[n:, 0:n]
    diagonal = jnp.sum(jnp.where(rows_in == cols_in, right, 0.0), axis=0, keepdims=True)
    out_ref[n:] = jnp.broadcast_to(jnp.concatenate([diagonal, diagonal], axis=1), (8, 2 * n))


def unpack(p_ref):
    n = p_ref.shape[1] // 2
    rows_in, cols_in = corner(n)
    both = p_ref[0:n, 0:n]
    turned = both.T
    left = jnp.where(rows_in >= cols_in, both, turned)
    right = jnp.where(rows_in < cols_in, both, turned)
    right = jnp.where(rows_in == cols_in, p_ref[n:n + 1, 0:n], right)
    below = p_ref[0:n, n:]
    return rows(jnp.concatenate([left, below.T], axis=1), jnp.concatenate([below, right], axis=1))


def second_step(codes, edges, low, mid, high, inner, hist, first, gram):
    ext, _, part = mid.shape
    count = ext - 2
    snaps = gram.shape[0]
    v = pl.BlockSpec(memory_space=pltpu.VMEM)
    sm = pl.BlockSpec(memory_space=pltpu.SMEM)

    def kernel(codes_ref, edge_ref, low_ref, mid_ref, high_ref, self_ref, side_ref, hist_ref, first_ref, gram_ref,
               new_ref, second_ref, gram_out, base_ref, flat, terms):
        def store(b, value):
            flat[pl.ds(pl.multiple_of(8 * b, 8), 8), :] = value
        step_blocks(codes_ref, edge_ref, low_ref, mid_ref, high_ref, self_ref, side_ref, store, base_ref)
        first = [first_ref[count * c:count * (c + 1)] for c in range(3)]
        second = new_snapshot(flat, count)
        for c in range(3):
            second_ref[count * c:count * (c + 1)] = second[c]
        for i in range(7):
            new_ref[pl.ds(i, count, stride=7), :] = flat[pl.ds(i, count, stride=8), :]
        row = cross_row(hist_ref, second, (first, second), terms)
        last = lax.broadcasted_iota(jnp.int32, (snaps, 1), 0) == snaps - 1
        pack(jnp.where(last, row, gram_ref[...]), gram_out)

    return pl.pallas_call(
        kernel,
        out_shape=(jax.ShapeDtypeStruct((count * 7, part), F32), jax.ShapeDtypeStruct(first.shape, F32),
                   jax.ShapeDtypeStruct((snaps // 2 + 8, snaps), F32)),
        in_specs=[sm, sm] + [v] * 8, out_specs=(v, v, v),
        scratch_shapes=step_scratch(ext, part) + [
            pltpu.VMEM((count * 8, part), F32), pltpu.VMEM((snaps * 8, part), F32)],
        compiler_params=pltpu.CompilerParams(vmem_limit_bytes=VMEM_LIMIT),
    )(codes, edges, low, mid, high, *inner, hist, first, gram)


def inner_sums(mid):
    count, _, part = mid.shape
    v = pl.BlockSpec(memory_space=pltpu.VMEM)

    def kernel(mid_ref, self_ref, side_ref):
        inner_part(mid_ref, 1, self_ref, side_ref)

    return pl.pallas_call(
        kernel, out_shape=inner_shapes(count - 2, part), in_specs=[v], out_specs=(v, v),
        compiler_params=pltpu.CompilerParams(vmem_limit_bytes=VMEM_LIMIT),
        cost_estimate=pl.CostEstimate(flops=1 << 30, bytes_accessed=1 << 20, transcendentals=0),
    )(mid)


def history_gram(hist):
    comps, snaps_old, count, part = hist.shape
    snaps = snaps_old + 2
    pitch = count + 8
    v = pl.BlockSpec(memory_space=pltpu.VMEM)

    def kernel(hist_ref, out_ref, wide):
        total = jnp.zeros((snaps_old, snaps_old), F32)
        for c in range(comps):
            def expand(s, _):
                wide[pl.ds(pl.multiple_of(pitch * s, 8), count), :] = hist_ref[c, s].astype(F32)
                return 0
            lax.fori_loop(0, snaps_old, expand, 0, unroll=max(u for u in range(1, 43) if snaps_old % u == 0))
            for b in range(0, count, 8):
                x = jnp.concatenate([wide[pl.ds(b + j, snaps_old, stride=pitch), :].astype(BF16) for j in range(8)], axis=1)
                total = total + lax.dot_general(x, x, (((1,), (1,)), ((), ())), preferred_element_type=F32)
        out_ref[...] = jnp.zeros_like(out_ref)
        out_ref[0:snaps_old, 0:snaps_old] = total

    return pl.pallas_call(
        kernel, out_shape=jax.ShapeDtypeStruct((snaps, snaps), F32),
        in_specs=[v], out_specs=v,
        scratch_shapes=[pltpu.VMEM((snaps_old * pitch, part), F32)],
        compiler_params=pltpu.CompilerParams(vmem_limit_bytes=VMEM_LIMIT),
        cost_estimate=pl.CostEstimate(flops=2 * comps * snaps * snaps * count * part, bytes_accessed=2 * comps * snaps * count * part, transcendentals=0),
    )(hist)


def early_row(hist, first, gram):
    comps, snaps_old, count, part = hist.shape
    snaps = snaps_old + 2
    v = pl.BlockSpec(memory_space=pltpu.VMEM)

    def kernel(hist_ref, first_ref, gram_ref, out_ref, new_ref, flat, terms):
        out_ref[...] = gram_ref[...]
        for b in range(count):
            flat[8 * b:8 * b + 8] = first_ref[b + 1]
        new = new_snapshot(flat, count)
        for c in range(3):
            new_ref[count * c:count * (c + 1)] = new[c]
        out_ref[snaps_old:snaps_old + 1] = cross_row(hist_ref, new, (new,), terms)

    return pl.pallas_call(
        kernel, out_shape=(jax.ShapeDtypeStruct((snaps, snaps), F32), jax.ShapeDtypeStruct((count * 3, part), F32)),
        in_specs=[v, v, v], out_specs=(v, v),
        scratch_shapes=[pltpu.VMEM((count * 8, part), F32), pltpu.VMEM((snaps * 8, part), F32)],
        compiler_params=pltpu.CompilerParams(vmem_limit_bytes=VMEM_LIMIT),
        cost_estimate=pl.CostEstimate(flops=1 << 30, bytes_accessed=2 * comps * snaps * count * part, transcendentals=0),
    )(hist, first, gram)


HIGHEST = lax.Precision.HIGHEST
REPEAT_BELOW = 1e-5
JOIN_ABOVE = 1e-4


def gram_of(m):
    return lax.dot_general(m, m, (((1,), (1,)), ((), ())), precision=HIGHEST, preferred_element_type=F32)


def orthonormal(m):
    n, wide = m.shape
    nb = n // 8
    s = gram_of(m)
    s = jnp.concatenate([s, jnp.zeros((n, wide - n), F32)], axis=1)
    sb = [s[8 * k:8 * k + 8] for k in range(nb)]
    mb = [m[8 * k:8 * k + 8] for k in range(nb)]
    sub = lax.broadcasted_iota(jnp.int32, (8, wide), 0)
    full = lambda x: jnp.broadcast_to(x, (8, wide))
    worst = None
    for k in range(nb):
        p = 8 * k
        norm0 = jnp.sum(m[8 * k:8 * k + 8] * m[8 * k:8 * k + 8], axis=1, keepdims=True)
        rs = [full(sb[k][i:i + 1]) for i in range(8)]
        rm = [full(mb[k][i:i + 1]) for i in range(8)]
        e = [[full(rs[i][:, p + j:p + j + 1]) for j in range(i + 1)] for i in range(8)]
        cols = [[full(sb[t][:, p + j:p + j + 1]) for j in range(8)] for t in range(k + 1, nb)]
        inv, low = [], [[None] * 8 for _ in range(8)]
        for j in range(8):
            inv.append(1.0 / e[j][j])
            for i in range(j + 1, 8):
                for t in range(j + 1, i + 1):
                    e[i][t] = e[i][t] - (e[i][j] * e[t][j]) * inv[j]
            for i in range(j + 1, 8):
                low[i][j] = e[i][j] * inv[j]
            for i in range(j + 1, 8):
                rs[i] = rs[i] - low[i][j] * rs[j]
                rm[i] = rm[i] - low[i][j] * rm[j]
        d = e[0][0]
        out = rm[0]
        for i in range(1, 8):
            d = jnp.where(sub == i, e[i][i], d)
            out = jnp.where(sub == i, rm[i], out)
        mb[k] = out * lax.rsqrt(d)
        ratio = d / norm0
        worst = ratio if worst is None else jnp.minimum(worst, ratio)
        if k == nb - 1:
            break
        us = [rs[j] * inv[j] for j in range(8)]
        um = [rm[j] * inv[j] for j in range(8)]
        for t in range(k + 1, nb):
            c = cols[t - k - 1]
            for j in range(8):
                for i in range(j + 1, 8):
                    c[i] = c[i] - low[i][j] * c[j]
                sb[t] = sb[t] - c[j] * us[j]
                mb[t] = mb[t] - c[j] * um[j]
    return jnp.concatenate(mb, 0), worst


def repeated(m, q_ref):
    q, worst = orthonormal(m)
    q_ref[...] = q

    @pl.when(jnp.logical_not(jnp.min(worst) >= REPEAT_BELOW))
    def _():
        q_ref[...] = orthonormal(q_ref[...])[0]


def start_basis(basis_t):
    v = pl.BlockSpec(memory_space=pltpu.VMEM)

    def kernel(b_ref, q_ref):
        repeated(b_ref[...], q_ref)

    return pl.pallas_call(
        kernel, out_shape=jax.ShapeDtypeStruct(basis_t.shape, F32), in_specs=[v], out_specs=v,
        cost_estimate=pl.CostEstimate(flops=1 << 30, bytes_accessed=1 << 20, transcendentals=0),
    )(basis_t)


def weigh(iters, packed_ref, g_ref, b_ref, q_ref):
    snaps = g_ref.shape[0]
    rows_in, cols_in = corner(snaps)
    g = unpack(packed_ref)
    trace = jnp.sum(jnp.where(rows_in == cols_in, g, 0.0), axis=(0, 1), keepdims=True)
    g_ref[...] = g * (1.0 / trace)
    q_ref[...] = b_ref[...]

    def product(q):
        return jnp.dot(q, g_ref[...], precision=HIGHEST, preferred_element_type=F32)

    q, checks = b_ref[...], []
    for k in range(iters - 1):
        q = product(q) if k < iters - 2 else product(product(q))
        q, worst = orthonormal(q)
        checks.append(worst * (1.0 / (REPEAT_BELOW if k < iters - 2 else JOIN_ABOVE)))
    good = jnp.min(functools.reduce(jnp.minimum, checks)) >= 1.0
    q_ref[...] = q

    @pl.when(jnp.logical_not(good))
    def _():
        q_ref[...] = b_ref[...]

        def iterate(i, _):
            repeated(product(q_ref[...]), q_ref)
            return 0

        lax.fori_loop(0, iters, iterate, 0)

    q = q_ref[...]
    last = (lax.broadcasted_iota(jnp.int32, (1, snaps), 1) == snaps - 1).astype(F32)
    w = jnp.zeros((1, snaps), F32)
    for _ in range(3):
        y = jnp.sum(q * (last - w), axis=1, keepdims=True)
        w = w + jnp.sum(q * y, axis=0, keepdims=True)
    return w


def filtered_field(gram, basis_t, hist, first, second):
    comps, snaps_old, count, part = hist.shape
    v = pl.BlockSpec(memory_space=pltpu.VMEM)

    def kernel(gram_ref, b_ref, hist_ref, first_ref, second_ref, out_ref, g_ref, q_ref, table):
        w = weigh(POD_ITERS, gram_ref, g_ref, b_ref, q_ref)
        table[...] = jnp.broadcast_to(w, table.shape).T
        w1, w2 = (table[snaps_old + k:snaps_old + k + 1] for k in range(2))
        parts = [slice(count * c, count * (c + 1)) for c in range(comps)]
        start = [w1 * first_ref[p] + w2 * second_ref[p] for p in parts]

        def one(s, total):
            wk = table[pl.ds(s, 1), :]
            return [total[c] + wk * hist_ref[c, s].astype(F32) for c in range(comps)]
        total = lax.fori_loop(0, snaps_old, one, start, unroll=max(u for u in range(1, 43) if snaps_old % u == 0))
        for c in range(comps):
            out_ref[pl.ds(c, count, stride=comps), :] = total[c]

    return pl.pallas_call(
        kernel, out_shape=jax.ShapeDtypeStruct((count * comps, part), F32),
        in_specs=[v, v, v, v, v], out_specs=v,
        scratch_shapes=[pltpu.VMEM((snaps_old + 2, snaps_old + 2), F32), pltpu.VMEM(basis_t.shape, F32),
                        pltpu.VMEM((snaps_old + 2, snaps_old + 2), F32)],
        compiler_params=pltpu.CompilerParams(vmem_limit_bytes=VMEM_LIMIT),
    )(gram, basis_t, hist, first, second)


def shift(x, axis, by):
    count = lax.axis_size(axis)
    return lax.ppermute(x, axis, [(i, (i + by) % count) for i in range(count)])


def reduce_all(x):
    axes = ("stream", "vert")
    sizes = [lax.axis_size(a) for a in axes]
    if any(n & (n - 1) for n in sizes):
        return lax.psum(x, axes)
    bits = [(0, 1 << k) for k in range(sizes[1].bit_length() - 1)] + [(1 << k, 0) for k in range(sizes[0].bit_length() - 1)]
    start = len(bits) % 2
    for group in [bits[0:start]] * start + [bits[k:k + 2] for k in range(start, len(bits), 2)]:
        masks = [(0, 0)]
        for s, v in group:
            masks = masks + [(a ^ s, b ^ v) for a, b in masks]
        total = x
        for s, v in masks[1:]:
            total = total + lax.ppermute(x, axes, [
                (i * sizes[1] + j, (i ^ s) * sizes[1] + (j ^ v)) for i in range(sizes[0]) for j in range(sizes[1])])
        x = total
    return x


def body(particles, phase_flags, neighbours, history, basis_start):
    count = particles.shape[0]
    codes = neighbours[:, 0].T
    width = codes.shape[0]
    hist = history[:, 0].transpose(1, 2, 0, 3)
    s, v = lax.axis_index("stream"), lax.axis_index("vert")
    ns, nv = lax.axis_size("stream"), lax.axis_size("vert")
    one = jnp.ones((), jnp.int32)
    common = [v > 0, one, v < nv - 1, s > 0, s < ns - 1]
    edges1 = jnp.stack(common + [2 * one, 0 * one, one]).astype(jnp.int32)
    edges2 = jnp.stack(common + [one, one, one]).astype(jnp.int32)
    state, lo, hi = prepare(particles[:, 0], phase_flags[:, 0], codes)
    from_low = shift(hi, "stream", 1)
    from_high = shift(lo, "stream", -1)
    mid = jnp.concatenate([from_low[0:2], state, from_high[0:2]], axis=0)
    wide_codes = jnp.concatenate(
        [from_low[2, 0:width, 0:1].astype(jnp.int32), codes, from_high[2, 0:width, 0:1].astype(jnp.int32)], axis=1)
    low_mid, high_mid = shift(mid, "vert", 1), shift(mid, "vert", -1)
    basis = start_basis(basis_start.T)
    inner, hist = lax.optimization_barrier((inner_sums(mid), hist))
    hist_gram = history_gram(hist)
    wide_codes, basis, hist_gram = lax.optimization_barrier((wide_codes, basis, hist_gram))
    first = first_step(wide_codes, edges1, low_mid, mid, high_mid, inner)
    low, high = shift(first, "vert", 1), shift(first, "vert", -1)
    inner = inner_sums(first)
    gram, first_new = early_row(hist, first, hist_gram)
    new_state, second_new, gram = second_step(wide_codes, edges2, low, first, high, inner, hist, first_new, gram)
    gram = reduce_all(gram)
    out = filtered_field(gram, basis, hist, first_new, second_new)
    return (new_state.reshape(count, 1, 7, -1), out.reshape(count, 1, 3, -1))


def solution(mesh):
    in_specs = (
        P("stream", "vert", None, None),
        P("stream", "vert", None),
        P("stream", "vert", None),
        P("stream", "vert", None, None, None),
        P(),
    )
    out_specs = (P("stream", "vert", None, None), P("stream", "vert", None, None))
    return jax.shard_map(body, mesh=mesh, in_specs=in_specs, out_specs=out_specs, check_vma=False)
```

```python
import functools
import math

import jax
import jax.numpy as jnp
from jax import lax
from jax.experimental import pallas as pl
from jax.experimental.pallas import tpu as pltpu
from jax.sharding import PartitionSpec as P

POD_ITERS = 4
VMEM_LIMIT = 20 << 20
SEDIMENT_EXTRA = 1.65


ALPHA_KERNEL = 21.0 / (16.0 * math.pi)
VOLUME = 1.0 / 16.0
STIFFNESS = 100.0 / 7.0
TIME_STEP = 0.02
GRAVITY = 1.0
F32, BF16 = jnp.float32, jnp.bfloat16

def pieces(x):
    a = x.astype(BF16).astype(F32)
    r = x - a
    b = r.astype(BF16).astype(F32)
    return a, b, r - b

def rows(*parts):
    return jnp.concatenate(parts, axis=0)

def row_is(*which):
    index = lax.broadcasted_iota(jnp.int32, (8, 128), 0)
    hit = index == which[0]
    for w in which[1:]:
        hit = hit | (index == w)
    return hit

def spread(row):
    return jnp.broadcast_to(row, (8, row.shape[1]))

def base_rows(state, keep):
    centred = jnp.where(row_is(0, 1, 2), state - 1.0, state)
    r, rho = spread(state[6:7]), spread(state[7:8] * keep)
    live = rho > 0.0
    mass = rho * VOLUME
    r2 = r * r
    pressure = jnp.where(live, STIFFNESS * (r2 * r2 * r2 * r - 1.0) / (jnp.where(live, rho, 1.0) * r2), 0.0)
    return jnp.where(row_is(6), mass, jnp.where(row_is(7), mass * pressure, centred)), pressure


def features(base):
    place = jnp.where(row_is(0, 1, 2), base, 0.0)
    norm = 0.25 * jnp.sum(place * place, axis=0, keepdims=True)
    speed = jnp.where(row_is(0, 1, 2), pltpu.roll(base, 5, 0), 0.0)
    flux = jnp.sum(place * speed, axis=0, keepdims=True)
    own = jnp.where(row_is(3), norm, jnp.where(row_is(4), 1.0, place))
    near = jnp.where(row_is(3), 1.0, jnp.where(row_is(4), norm, -0.5 * place))
    moved = jnp.where(row_is(0), 1.0, jnp.where(row_is(7), flux, pltpu.roll(base, 1, 0)))
    sums_a = spread(base[6:7]) * moved
    sums_b = jnp.where(row_is(0, 1, 2, 3), spread(base[7:8]) * moved, 0.0)
    return own, rows(near, sums_a, sums_b)


def prep_kernel(particles_ref, flags_ref, codes_ref, state_ref, lo_ref, hi_ref, flat):
    count = flags_ref.shape[0]
    fields = particles_ref.shape[0] // count
    for i in range(fields):
        flat[pl.ds(i, count, stride=8), :] = particles_ref[pl.ds(i, count, stride=fields), :]
    flat[pl.ds(fields, count, stride=8), :] = 1.0 + SEDIMENT_EXTRA * flags_ref[...].astype(F32)
    for b in range(count):
        state_ref[b] = flat[8 * b:8 * b + 8]
    for ref, first, edge in ((lo_ref, 0, 0), (hi_ref, count - 2, count - 1)):
        for i in range(2):
            ref[i] = flat[8 * (first + i):8 * (first + i) + 8]
        ref[2] = jnp.zeros_like(ref[2])
        ref[2, 0:codes_ref.shape[0], 0:1] = codes_ref[:, edge:edge + 1].astype(F32)


def prepare(particles, flags, codes):
    count, fields, part = particles.shape
    v = pl.BlockSpec(memory_space=pltpu.VMEM)
    rim = jax.ShapeDtypeStruct((3, 8, part), F32)
    return pl.pallas_call(
        prep_kernel,
        out_shape=(jax.ShapeDtypeStruct((count, 8, part), F32), rim, rim),
        in_specs=[v, v, v], out_specs=(v, v, v),
        scratch_shapes=[pltpu.VMEM((count * 8, part), F32)],
    )(particles.reshape(count * fields, part), flags, codes)


def own_side(own):
    o1, o2, o3 = pieces(own)
    return rows(o1, o1, o2, o2, o1, o3).astype(BF16)


def near_side(g):
    p1, p2, p3 = pieces(g[0:8])
    f1 = g[8:24].astype(BF16)
    f2 = (g[8:24] - f1.astype(F32)).astype(BF16)
    return rows(p1, p2, p1, p2, p3, p1).astype(BF16), rows(f1, f2)


def weighted_sums(group):
    width = len(group)
    zero = jnp.zeros_like(group[0][0])
    rhs = rows(*[jnp.concatenate([g[0] if m == k else zero for m in range(width)], axis=1) for k, g in enumerate(group)])
    s = lax.dot_general(rows(*[g[1] for g in group]), rhs, (((0,), (0,)), ((), ())), preferred_element_type=F32)
    s = jnp.maximum(s, 1e-20)
    k = jnp.maximum(1.0 - s * lax.rsqrt(s), 0.0)
    wgt = k * k * k
    wh = wgt.astype(BF16)
    wl = (wgt - wh.astype(F32)).astype(BF16)
    f = rows(*[jnp.concatenate([g[2], g[2]], axis=1) for g in group])
    acc = jnp.dot(f, rows(wh, wl), preferred_element_type=F32)
    part = zero.shape[1]
    cut = [acc[32 * k:32 * (k + 1), part * k:part * (k + 1)] for k in range(width)]
    return [t[0:16] + t[16:32] for t in cut]


def in_groups(count, run):
    width = 2 if count % 2 == 0 else 1
    trips = count // width

    def trip(i, _):
        run([width * i + k for k in range(width)])
        return 0
    lax.fori_loop(0, trips, trip, 0, unroll=max(u for u in range(1, 18) if trips % u == 0))


def inner_part(state_ref, skip, self_ref, side_ref):
    def run(blocks):
        group = []
        for b in blocks:
            base, pressure = base_rows(state_ref[b + skip], 1.0)
            own, g_self = features(base)
            side = own_side(own)
            side_ref[b] = side
            self_ref[b, 16:24] = pressure
            group.append((side,) + near_side(g_self))
        for b, t in zip(blocks, weighted_sums(group)):
            self_ref[b, 0:16] = t
    in_groups(self_ref.shape[0], run)


def inner_shapes(count, part):
    return (jax.ShapeDtypeStruct((count, 24, part), F32), jax.ShapeDtypeStruct((count, 48, part), BF16))


def step_blocks(codes_ref, edge_ref, low_ref, mid_ref, high_ref, self_ref, side_ref, store, base_ref):
    ext, _, part = mid_ref.shape
    count = ext - 2
    rim, skip = edge_ref[5], edge_ref[6]
    along = row_is(0).astype(F32)
    upward = row_is(2).astype(F32)

    def prep(i):
        rowon = jnp.where(i < rim, edge_ref[3], jnp.where(i >= ext - rim, edge_ref[4], 1))
        for col, ref in ((0, low_ref), (1, mid_ref), (2, high_ref)):
            base_ref[col * ext + i] = base_rows(ref[i], (edge_ref[col] * rowon).astype(F32))[0]

    for i in range(3):
        prep(i)

    def operands(b):
        st = mid_ref[b + 1]
        gs = []
        for n in range(codes_ref.shape[0]):
            c = codes_ref[n, b + skip]
            o = c + jnp.where(c >= 4, 1, 0)
            ds1 = (o * 11) >> 5
            dv1 = o - 3 * ds1
            idx = dv1 * ext + b + ds1
            tx = 2.0 * (ds1 - 1).astype(F32)
            tz = 2.0 * (dv1 - 1).astype(F32)
            gs.append(features(base_ref[idx] + (tx * along + tz * upward))[1])
        prep(jnp.minimum(b + 3, ext - 1))
        near = [near_side(g) for g in gs]
        return st, (side_ref[b],) + tuple(jnp.concatenate(x, axis=1) for x in zip(*near))

    def finish(b, st, pressure, t):
        x, vel = st[0:3] - 1.0, st[3:6]
        coef = -5.0 * ALPHA_KERNEL
        sw, swx, swv, swf = t[0:1], t[1:4], t[4:7], t[7:8]
        swp, swpx = t[8:9], t[9:12]
        dens = coef * (jnp.sum(vel * (x * sw - swx) - x * swv, axis=0, keepdims=True) + swf)
        acc3 = -coef * (pressure * (x * sw - swx) + x * swp - swpx)
        grav = jnp.where(lax.broadcasted_iota(jnp.int32, (3, 1), 0) == 2, -GRAVITY, 0.0)
        vel2 = vel + TIME_STEP * (acc3 + grav)
        pos2 = st[0:3] + TIME_STEP * vel2
        rho = st[7:8]
        r2 = st[6:7] + TIME_STEP * dens / rho
        store(b, rows(pos2, vel2, r2, rho))

    def run(blocks):
        group = [operands(b) for b in blocks]
        for b, (st, _), t in zip(blocks, group, weighted_sums([g[1] for g in group])):
            finish(b, st, self_ref[b, 16:17], t + self_ref[b, 0:16])
    in_groups(count, run)


def step_scratch(ext, part):
    return [pltpu.VMEM((3 * ext, 8, part), F32)]


def first_step(codes, edges, low, mid, high, inner):
    ext, _, part = mid.shape
    v = pl.BlockSpec(memory_space=pltpu.VMEM)
    sm = pl.BlockSpec(memory_space=pltpu.SMEM)
    def kernel(codes_ref, edge_ref, low_ref, mid_ref, high_ref, self_ref, side_ref, out_ref, base_ref):
        def store(b, value):
            out_ref[b] = value
        step_blocks(codes_ref, edge_ref, low_ref, mid_ref, high_ref, self_ref, side_ref, store, base_ref)

    return pl.pallas_call(
        kernel, out_shape=jax.ShapeDtypeStruct((ext - 2, 8, part), F32),
        in_specs=[sm, sm, v, v, v, v, v], out_specs=v,
        scratch_shapes=step_scratch(ext, part),
        compiler_params=pltpu.CompilerParams(vmem_limit_bytes=VMEM_LIMIT),
    )(codes, edges, low, mid, high, *inner)


def cross_row(hist_ref, new, others, terms):
    comps, hist = hist_ref.shape[0], hist_ref.shape[1]
    groups = new[0].shape[0] // 8

    def fold(x):
        total = x[0:8]
        for g in range(1, groups):
            total = total + x[8 * g:8 * g + 8]
        return total

    def one(s, _):
        total = hist_ref[0, s].astype(F32) * new[0]
        for c in range(1, comps):
            total = total + hist_ref[c, s].astype(F32) * new[c]
        terms[pl.ds(pl.multiple_of(8 * s, 8), 8), :] = fold(total)
        return 0
    lax.fori_loop(0, hist, one, 0, unroll=max(u for u in range(1, 43) if hist % u == 0))
    snaps = terms.shape[0] // 8
    for k in range(snaps - hist):
        if k < len(others):
            total = others[k][0] * new[0]
            for c in range(1, comps):
                total = total + others[k][c] * new[c]
            terms[8 * (hist + k):8 * (hist + k) + 8] = fold(total)
        else:
            terms[8 * (hist + k):8 * (hist + k) + 8] = jnp.zeros_like(terms[0:8])
    by_snap = terms[pl.ds(0, snaps, stride=8), :]
    for i in range(1, 8):
        by_snap = by_snap + terms[pl.ds(i, snaps, stride=8), :]
    ones = jnp.ones((8, by_snap.shape[1]), F32)
    return lax.dot_general(ones, by_snap, (((1,), (1,)), ((), ())), precision=HIGHEST, preferred_element_type=F32)[0:1]


def new_snapshot(flat, count):
    return [flat[pl.ds(3 + c, count, stride=8), :].astype(BF16).astype(F32) for c in range(3)]


def corner(n):
    rows_in = lax.broadcasted_iota(jnp.int32, (n, n), 0)
    cols_in = lax.broadcasted_iota(jnp.int32, (n, n), 1)
    return rows_in, cols_in


def pack(g, out_ref):
    n = g.shape[0] // 2
    rows_in, cols_in = corner(n)
    right = g[n:, n:]
    out_ref[0:n, 0:n] = jnp.where(rows_in >= cols_in, g[0:n, 0:n], right.T)
    out_ref[0:n, n:] = g[n:, 0:n]
    diagonal = jnp.sum(jnp.where(rows_in == cols_in, right, 0.0), axis=0, keepdims=True)
    out_ref[n:] = jnp.broadcast_to(jnp.concatenate([diagonal, diagonal], axis=1), (8, 2 * n))


def unpack(p_ref):
    n = p_ref.shape[1] // 2
    rows_in, cols_in = corner(n)
    both = p_ref[0:n, 0:n]
    turned = both.T
    left = jnp.where(rows_in >= cols_in, both, turned)
    right = jnp.where(rows_in < cols_in, both, turned)
    right = jnp.where(rows_in == cols_in, p_ref[n:n + 1, 0:n], right)
    below = p_ref[0:n, n:]
    return rows(jnp.concatenate([left, below.T], axis=1), jnp.concatenate([below, right], axis=1))


def second_step(codes, edges, low, mid, high, inner, hist, first, gram):
    ext, _, part = mid.shape
    count = ext - 2
    snaps = gram.shape[0]
    v = pl.BlockSpec(memory_space=pltpu.VMEM)
    sm = pl.BlockSpec(memory_space=pltpu.SMEM)

    def kernel(codes_ref, edge_ref, low_ref, mid_ref, high_ref, self_ref, side_ref, hist_ref, first_ref, gram_ref,
               new_ref, second_ref, gram_out, base_ref, flat, terms):
        def store(b, value):
            flat[pl.ds(pl.multiple_of(8 * b, 8), 8), :] = value
        step_blocks(codes_ref, edge_ref, low_ref, mid_ref, high_ref, self_ref, side_ref, store, base_ref)
        first = [first_ref[count * c:count * (c + 1)] for c in range(3)]
        second = new_snapshot(flat, count)
        for c in range(3):
            second_ref[count * c:count * (c + 1)] = second[c]
        for i in range(7):
            new_ref[pl.ds(i, count, stride=7), :] = flat[pl.ds(i, count, stride=8), :]
        row = cross_row(hist_ref, second, (first, second), terms)
        last = lax.broadcasted_iota(jnp.int32, (snaps, 1), 0) == snaps - 1
        pack(jnp.where(last, row, gram_ref[...]), gram_out)

    return pl.pallas_call(
        kernel,
        out_shape=(jax.ShapeDtypeStruct((count * 7, part), F32), jax.ShapeDtypeStruct(first.shape, F32),
                   jax.ShapeDtypeStruct((snaps // 2 + 8, snaps), F32)),
        in_specs=[sm, sm] + [v] * 8, out_specs=(v, v, v),
        scratch_shapes=step_scratch(ext, part) + [
            pltpu.VMEM((count * 8, part), F32), pltpu.VMEM((snaps * 8, part), F32)],
        compiler_params=pltpu.CompilerParams(vmem_limit_bytes=VMEM_LIMIT),
    )(codes, edges, low, mid, high, *inner, hist, first, gram)


def inner_sums(mid):
    count, _, part = mid.shape
    v = pl.BlockSpec(memory_space=pltpu.VMEM)

    def kernel(mid_ref, self_ref, side_ref):
        inner_part(mid_ref, 1, self_ref, side_ref)

    return pl.pallas_call(
        kernel, out_shape=inner_shapes(count - 2, part), in_specs=[v], out_specs=(v, v),
        compiler_params=pltpu.CompilerParams(vmem_limit_bytes=VMEM_LIMIT),
        cost_estimate=pl.CostEstimate(flops=1 << 30, bytes_accessed=1 << 20, transcendentals=0),
    )(mid)


def history_gram(hist):
    comps, snaps_old, count, part = hist.shape
    snaps = snaps_old + 2
    pitch = count + 8
    v = pl.BlockSpec(memory_space=pltpu.VMEM)

    def kernel(hist_ref, out_ref, wide):
        total = jnp.zeros((snaps_old, snaps_old), F32)
        for c in range(comps):
            def expand(s, _):
                wide[pl.ds(pl.multiple_of(pitch * s, 8), count), :] = hist_ref[c, s].astype(F32)
                return 0
            lax.fori_loop(0, snaps_old, expand, 0, unroll=max(u for u in range(1, 43) if snaps_old % u == 0))
            for b in range(0, count, 8):
                x = jnp.concatenate([wide[pl.ds(b + j, snaps_old, stride=pitch), :].astype(BF16) for j in range(8)], axis=1)
                total = total + lax.dot_general(x, x, (((1,), (1,)), ((), ())), preferred_element_type=F32)
        out_ref[...] = jnp.zeros_like(out_ref)
        out_ref[0:snaps_old, 0:snaps_old] = total

    return pl.pallas_call(
        kernel, out_shape=jax.ShapeDtypeStruct((snaps, snaps), F32),
        in_specs=[v], out_specs=v,
        scratch_shapes=[pltpu.VMEM((snaps_old * pitch, part), F32)],
        compiler_params=pltpu.CompilerParams(vmem_limit_bytes=VMEM_LIMIT),
        cost_estimate=pl.CostEstimate(flops=2 * comps * snaps * snaps * count * part, bytes_accessed=2 * comps * snaps * count * part, transcendentals=0),
    )(hist)


def early_row(hist, first, gram):
    comps, snaps_old, count, part = hist.shape
    snaps = snaps_old + 2
    v = pl.BlockSpec(memory_space=pltpu.VMEM)

    def kernel(hist_ref, first_ref, gram_ref, out_ref, new_ref, flat, terms):
        out_ref[...] = gram_ref[...]
        for b in range(count):
            flat[8 * b:8 * b + 8] = first_ref[b + 1]
        new = new_snapshot(flat, count)
        for c in range(3):
            new_ref[count * c:count * (c + 1)] = new[c]
        out_ref[snaps_old:snaps_old + 1] = cross_row(hist_ref, new, (new,), terms)

    return pl.pallas_call(
        kernel, out_shape=(jax.ShapeDtypeStruct((snaps, snaps), F32), jax.ShapeDtypeStruct((count * 3, part), F32)),
        in_specs=[v, v, v], out_specs=(v, v),
        scratch_shapes=[pltpu.VMEM((count * 8, part), F32), pltpu.VMEM((snaps * 8, part), F32)],
        compiler_params=pltpu.CompilerParams(vmem_limit_bytes=VMEM_LIMIT),
        cost_estimate=pl.CostEstimate(flops=1 << 30, bytes_accessed=2 * comps * snaps * count * part, transcendentals=0),
    )(hist, first, gram)


HIGHEST = lax.Precision.HIGHEST
REPEAT_BELOW = 1e-5
JOIN_ABOVE = 1e-4


def left_pieces(x, axis):
    a, b, c = pieces(x)
    return jnp.concatenate([a, a, b, b, a, c], axis=axis).astype(BF16)


def right_pieces(x, axis):
    a, b, c = pieces(x)
    return jnp.concatenate([a, b, a, b, c, a], axis=axis).astype(BF16)


def gram_of(m):
    return lax.dot_general(left_pieces(m, 1), right_pieces(m, 1), (((1,), (1,)), ((), ())), preferred_element_type=F32)


def orthonormal(m):
    n, wide = m.shape
    nb = n // 8
    s = gram_of(m)
    s = jnp.concatenate([s, jnp.zeros((n, wide - n), F32)], axis=1)
    sb = [s[8 * k:8 * k + 8] for k in range(nb)]
    mb = [m[8 * k:8 * k + 8] for k in range(nb)]
    sub = lax.broadcasted_iota(jnp.int32, (8, wide), 0)
    full = lambda x: jnp.broadcast_to(x, (8, wide))
    worst = None
    for k in range(nb):
        p = 8 * k
        norm0 = jnp.sum(m[8 * k:8 * k + 8] * m[8 * k:8 * k + 8], axis=1, keepdims=True)
        rs = [full(sb[k][i:i + 1]) for i in range(8)]
        rm = [full(mb[k][i:i + 1]) for i in range(8)]
        e = [[full(rs[i][:, p + j:p + j + 1]) for j in range(i + 1)] for i in range(8)]
        cols = [[full(sb[t][:, p + j:p + j + 1]) for j in range(8)] for t in range(k + 1, nb)]
        inv, low = [], [[None] * 8 for _ in range(8)]
        for j in range(8):
            inv.append(1.0 / e[j][j])
            for i in range(j + 1, 8):
                for t in range(j + 1, i + 1):
                    e[i][t] = e[i][t] - (e[i][j] * e[t][j]) * inv[j]
            for i in range(j + 1, 8):
                low[i][j] = e[i][j] * inv[j]
            for i in range(j + 1, 8):
                rs[i] = rs[i] - low[i][j] * rs[j]
                rm[i] = rm[i] - low[i][j] * rm[j]
        d = e[0][0]
        out = rm[0]
        for i in range(1, 8):
            d = jnp.where(sub == i, e[i][i], d)
            out = jnp.where(sub == i, rm[i], out)
        mb[k] = out * lax.rsqrt(d)
        ratio = d / norm0
        worst = ratio if worst is None else jnp.minimum(worst, ratio)
        if k == nb - 1:
            break
        us = [rs[j] * inv[j] for j in range(8)]
        um = [rm[j] * inv[j] for j in range(8)]
        for t in range(k + 1, nb):
            c = cols[t - k - 1]
            for j in range(8):
                for i in range(j + 1, 8):
                    c[i] = c[i] - low[i][j] * c[j]
                sb[t] = sb[t] - c[j] * us[j]
                mb[t] = mb[t] - c[j] * um[j]
    return jnp.concatenate(mb, 0), worst


def repeated(m, q_ref):
    q, worst = orthonormal(m)
    q_ref[...] = q

    @pl.when(jnp.logical_not(jnp.min(worst) >= REPEAT_BELOW))
    def _():
        q_ref[...] = orthonormal(q_ref[...])[0]


def start_basis(basis_t):
    v = pl.BlockSpec(memory_space=pltpu.VMEM)

    def kernel(b_ref, q_ref):
        repeated(b_ref[...], q_ref)

    return pl.pallas_call(
        kernel, out_shape=jax.ShapeDtypeStruct(basis_t.shape, F32), in_specs=[v], out_specs=v,
        cost_estimate=pl.CostEstimate(flops=1 << 30, bytes_accessed=1 << 20, transcendentals=0),
    )(basis_t)


def weigh(iters, packed_ref, g_ref, split_ref, b_ref, q_ref):
    snaps = g_ref.shape[0]
    rows_in, cols_in = corner(snaps)
    g = unpack(packed_ref)
    trace = jnp.sum(jnp.where(rows_in == cols_in, g, 0.0), axis=(0, 1), keepdims=True)
    g_ref[...] = g * (1.0 / trace)
    q_ref[...] = b_ref[...]

    split_ref[...] = right_pieces(g_ref[...], 0)

    def product(q):
        return jnp.dot(left_pieces(q, 1), split_ref[...], preferred_element_type=F32)

    q, checks = b_ref[...], []
    for k in range(iters - 1):
        q = product(q) if k < iters - 2 else product(product(q))
        q, worst = orthonormal(q)
        checks.append(worst * (1.0 / (REPEAT_BELOW if k < iters - 2 else JOIN_ABOVE)))
    good = jnp.min(functools.reduce(jnp.minimum, checks)) >= 1.0
    q_ref[...] = q

    @pl.when(jnp.logical_not(good))
    def _():
        q_ref[...] = b_ref[...]

        def iterate(i, _):
            repeated(product(q_ref[...]), q_ref)
            return 0

        lax.fori_loop(0, iters, iterate, 0)

    q = q_ref[...]
    last = (lax.broadcasted_iota(jnp.int32, (1, snaps), 1) == snaps - 1).astype(F32)
    w = jnp.zeros((1, snaps), F32)
    for _ in range(3):
        y = jnp.sum(q * (last - w), axis=1, keepdims=True)
        w = w + jnp.sum(q * y, axis=0, keepdims=True)
    return w


def filtered_field(gram, basis_t, hist, first, second):
    comps, snaps_old, count, part = hist.shape
    v = pl.BlockSpec(memory_space=pltpu.VMEM)

    def kernel(gram_ref, b_ref, hist_ref, first_ref, second_ref, out_ref, g_ref, split_ref, q_ref, table):
        w = weigh(POD_ITERS, gram_ref, g_ref, split_ref, b_ref, q_ref)
        table[...] = jnp.broadcast_to(w, table.shape).T
        w1, w2 = (table[snaps_old + k:snaps_old + k + 1] for k in range(2))
        parts = [slice(count * c, count * (c + 1)) for c in range(comps)]
        start = [w1 * first_ref[p] + w2 * second_ref[p] for p in parts]

        def one(s, total):
            wk = table[pl.ds(s, 1), :]
            return [total[c] + wk * hist_ref[c, s].astype(F32) for c in range(comps)]
        total = lax.fori_loop(0, snaps_old, one, start, unroll=max(u for u in range(1, 43) if snaps_old % u == 0))
        for c in range(comps):
            out_ref[pl.ds(c, count, stride=comps), :] = total[c]

    return pl.pallas_call(
        kernel, out_shape=jax.ShapeDtypeStruct((count * comps, part), F32),
        in_specs=[v, v, v, v, v], out_specs=v,
        scratch_shapes=[pltpu.VMEM((snaps_old + 2, snaps_old + 2), F32), pltpu.VMEM((6 * (snaps_old + 2), snaps_old + 2), BF16),
                        pltpu.VMEM(basis_t.shape, F32),
                        pltpu.VMEM((snaps_old + 2, snaps_old + 2), F32)],
        compiler_params=pltpu.CompilerParams(vmem_limit_bytes=VMEM_LIMIT),
    )(gram, basis_t, hist, first, second)


def shift(x, axis, by):
    count = lax.axis_size(axis)
    return lax.ppermute(x, axis, [(i, (i + by) % count) for i in range(count)])


def reduce_all(x):
    axes = ("stream", "vert")
    sizes = [lax.axis_size(a) for a in axes]
    if any(n & (n - 1) for n in sizes):
        return lax.psum(x, axes)
    bits = [(0, 1 << k) for k in range(sizes[1].bit_length() - 1)] + [(1 << k, 0) for k in range(sizes[0].bit_length() - 1)]
    start = len(bits) % 2
    for group in [bits[0:start]] * start + [bits[k:k + 2] for k in range(start, len(bits), 2)]:
        masks = [(0, 0)]
        for s, v in group:
            masks = masks + [(a ^ s, b ^ v) for a, b in masks]
        total = x
        for s, v in masks[1:]:
            total = total + lax.ppermute(x, axes, [
                (i * sizes[1] + j, (i ^ s) * sizes[1] + (j ^ v)) for i in range(sizes[0]) for j in range(sizes[1])])
        x = total
    return x


def body(particles, phase_flags, neighbours, history, basis_start):
    count = particles.shape[0]
    codes = neighbours[:, 0].T
    width = codes.shape[0]
    hist = history[:, 0].transpose(1, 2, 0, 3)
    s, v = lax.axis_index("stream"), lax.axis_index("vert")
    ns, nv = lax.axis_size("stream"), lax.axis_size("vert")
    one = jnp.ones((), jnp.int32)
    common = [v > 0, one, v < nv - 1, s > 0, s < ns - 1]
    edges1 = jnp.stack(common + [2 * one, 0 * one, one]).astype(jnp.int32)
    edges2 = jnp.stack(common + [one, one, one]).astype(jnp.int32)
    state, lo, hi = prepare(particles[:, 0], phase_flags[:, 0], codes)
    from_low = shift(hi, "stream", 1)
    from_high = shift(lo, "stream", -1)
    mid = jnp.concatenate([from_low[0:2], state, from_high[0:2]], axis=0)
    wide_codes = jnp.concatenate(
        [from_low[2, 0:width, 0:1].astype(jnp.int32), codes, from_high[2, 0:width, 0:1].astype(jnp.int32)], axis=1)
    low_mid, high_mid = shift(mid, "vert", 1), shift(mid, "vert", -1)
    basis = start_basis(basis_start.T)
    inner, hist = lax.optimization_barrier((inner_sums(mid), hist))
    hist_gram = history_gram(hist)
    wide_codes, basis, hist_gram = lax.optimization_barrier((wide_codes, basis, hist_gram))
    first = first_step(wide_codes, edges1, low_mid, mid, high_mid, inner)
    low, high = shift(first, "vert", 1), shift(first, "vert", -1)
    inner = inner_sums(first)
    gram, first_new = early_row(hist, first, hist_gram)
    new_state, second_new, gram = second_step(wide_codes, edges2, low, first, high, inner, hist, first_new, gram)
    gram = reduce_all(gram)
    out = filtered_field(gram, basis, hist, first_new, second_new)
    return (new_state.reshape(count, 1, 7, -1), out.reshape(count, 1, 3, -1))


def solution(mesh):
    in_specs = (
        P("stream", "vert", None, None),
        P("stream", "vert", None),
        P("stream", "vert", None),
        P("stream", "vert", None, None, None),
        P(),
    )
    out_specs = (P("stream", "vert", None, None), P("stream", "vert", None, None))
    return jax.shard_map(body, mesh=mesh, in_specs=in_specs, out_specs=out_specs, check_vma=False)
```
